32 devices in a mesh: grp: 2 (over x), ch: 16 (over z, y, core).
Axes of the slice: x: 2, y: 2, z: 4, core: 2. Of those that a mesh axis runs over, the one named last changes fastest.
Arguments:
- features: bfloat16 [2048, 2048], P('ch', 'grp'), parts along dimension 1, may hold values from -50 to 50
- dw_weight: float32 [2048, 49], P('ch'), may hold values from -0.875 to 0.875
- norm_gain: float32 [2048], replicated, may hold values from 0.25 to 1.75
- layer_scale: float32 [2048], replicated, may hold values from 0.2 to 1
- w_in: bfloat16 [8192, 2048], P('ch'), may hold values from -0.125 to 0.125
- w_out: bfloat16 [8192, 2048], P('ch'), may hold values from -0.0625 to 0.0625
- w_head: bfloat16 [2048, 150], replicated, may hold values from -3 to 3
- labels: int32 [2048], P('grp'), parts along dimension 0, may hold values from 0 to 149
Outputs:
- d_features: float32 [2048, 2048], P('ch', 'grp'), parts along dimension 1
- d_dw: float32 [2048, 98], P('ch', 'grp'), parts along dimension 1
- d_scale: float32 [4096], P(('grp', 'ch')), parts along dimension 0
- d_w_in: float32 [16384, 2048], P(('grp', 'ch')), parts along dimension 0
- d_w_out: float32 [16384, 2048], P(('grp', 'ch')), parts along dimension 0
- d_head: float32 [2048, 300], P('ch', 'grp'), parts along dimension 1
- mean_loss: float32 [2], P('grp'), parts along dimension 0
The draws below stay inside these ranges and needn't reach their ends.
There are 2 independent parts, one for each index of `grp`. The reference program is written for one: setup_inputs(seed, part) draws one part's arguments, and reference() takes and returns one part's arrays. A program takes and returns all parts, laid end to end along the dimension named above; an argument that names none is the same for every part. Nothing has to cross between parts.
All inputs are finite; a program needn't handle non-finite values.
Results may differ from the reference program's by a relative error of at most 0.012.
Values may be sent and summed in bfloat16 or wider, within the bound.
A program may use at most 128 MiB of HBM per device.

```python
import math
import jax
import jax.numpy as jnp
from jax import lax

C = 2048
FF = 8192
K = 150
KS = 7
WIN_H = 32
WIN_W = 32
TOKENS = 1024


def draw_features(key, part):
    key_base, key_tok = jax.random.split(jax.random.fold_in(key, 11), 2)
    base = jnp.clip(jax.random.normal(key_base, (C, TOKENS), jnp.float32), -4.0, 4.0)
    ramp = 0.3 * jnp.power(10.0, jnp.arange(C, dtype=jnp.float32) / C)
    tok_scale = jnp.exp(jax.random.uniform(key_tok, (TOKENS,), jnp.float32, math.log(0.3), math.log(3.0)))
    values = base * ramp[:, None] * tok_scale[None, :]
    return jnp.clip(values, -50.0, 50.0).astype(jnp.bfloat16)


def draw_w_head(key, part):
    key_base = jax.random.fold_in(jax.random.fold_in(key, 23), 0)
    spread = 2.0 / math.sqrt(C)
    values = jnp.clip(jax.random.normal(key_base, (C, K), jnp.float32), -4.0, 4.0) * spread
    return jnp.clip(values, -3.0, 3.0).astype(jnp.bfloat16)


def plant(values, rng, least, largest):
    longest = values.shape.index(max(values.shape))
    spots = []
    for shift in (0, 1):
        where = [jax.random.randint(jax.random.fold_in(rng, axis), (), 0, length) for axis, length in enumerate(values.shape)]
        where[longest] = (where[longest] + shift) % values.shape[longest]
        spots.append(tuple(where))
    return values.at[spots[0]].set(least).at[spots[1]].set(largest)


def block_levels(stream_key, shape, cuts, least, top_value):
    loudness, own = 1.0, jax.random.fold_in(stream_key, 6)
    for position, parts in cuts:
        heights = jnp.exp(jax.random.uniform(jax.random.fold_in(own, position), (parts,), jnp.float32, least / len(cuts), top_value / len(cuts)))
        loudness = loudness * jnp.repeat(heights, shape[position] // parts).reshape([-1 if axis == position else 1 for axis in range(len(shape))])
    return loudness


def gaussian(key, extent, scale, most, cuts=(), kind=jnp.bfloat16):
    result = jax.random.normal(key, extent, jnp.float32) * scale
    if len(cuts) > 0:
        result = block_levels(key, extent, cuts, -0.22, 0.18) * result
    return jnp.clip(result, min=-most, max=most).astype(kind)


def setup_inputs(seed: int = 0, part: int = 0) -> dict:
    key_of = jax.random.split(jax.random.key(seed), 9)
    part_splits = jax.random.split(jax.random.fold_in(key_of[8], part), 9)
    features = draw_features(jax.random.fold_in(jax.random.fold_in(key_of[8], part), 71), part)
    dw_weight = gaussian(key_of[1], (C, KS * KS), (KS * KS) ** -0.5, 0.875, ((0, 16),), jnp.float32)
    norm_gain = jnp.clip(1.0 + 0.15 * jax.random.normal(key_of[2], (C,), jnp.float32), 0.25, 1.75)
    layer_scale = jnp.clip(jnp.exp(jax.random.uniform(key_of[3], (C,), jnp.float32, math.log(0.2), math.log(1.0))), 0.2, 1.0)
    w_in = gaussian(key_of[4], (FF, C), C ** -0.5, 0.125, ((0, 16),))
    w_out = gaussian(key_of[5], (FF, C), FF ** -0.5, 0.0625, ((0, 16),))
    w_head = draw_w_head(jax.random.fold_in(key_of[8], 71), part)
    labels = plant(jax.random.randint(part_splits[7], (TOKENS,), 0, K), jax.random.fold_in(part_splits[7], 1), 0, K - 1).astype(jnp.int32)
    return {"features": features, "dw_weight": dw_weight, "norm_gain": norm_gain, "layer_scale": layer_scale, "w_in": w_in, "w_out": w_out, "w_head": w_head, "labels": labels}


norm_eps = 1e-06

def conv_apply(in_grid, kernel):
    half = KS // 2
    padded = jnp.pad(in_grid, ((0, 0), (half, half), (half, half)))
    running = jnp.zeros(in_grid.shape, in_grid.dtype)
    for row_shift in range(KS):
        for col_shift in range(KS):
            tap = kernel[:, row_shift * KS + col_shift]
            running = running + tap[:, None, None] * padded[:, row_shift:row_shift + WIN_H, col_shift:col_shift + WIN_W]
    return running

def gelu_parts(values):
    cum_prob = 0.5 * (1.0 + lax.erf(values * 0.7071067811865476))
    density = jnp.exp(-0.5 * values * values) * 0.3989422804014327
    return (values * cum_prob, cum_prob + values * density)

def reference(features, dw_weight, norm_gain, layer_scale, w_in, w_out, w_head, labels):
    highest = lax.Precision.HIGHEST
    inputs_wide = features.astype(jnp.float32)
    in_grid = inputs_wide.reshape(C, WIN_H, WIN_W)
    conv_out = conv_apply(in_grid, dw_weight).reshape(C, TOKENS).astype(jnp.bfloat16)
    conv_wide = conv_out.astype(jnp.float32)
    tok_mean = lax.optimization_barrier(jnp.mean(conv_wide, axis=0))
    centered = conv_wide - tok_mean[None, :]
    tok_var = lax.optimization_barrier(jnp.mean(centered * centered, axis=0))
    inv_std = 1.0 / jnp.sqrt(tok_var + norm_eps)
    normed = centered * inv_std[None, :]
    norm_out = (norm_gain[:, None] * normed).astype(jnp.bfloat16)
    pre_act = jnp.dot(w_in, norm_out, preferred_element_type=jnp.float32)
    gelu_out, gelu_slope = gelu_parts(pre_act)
    hidden = gelu_out.astype(jnp.bfloat16)
    branch_sum = lax.dot_general(w_out, hidden, (((0,), (0,)), ((), ())), preferred_element_type=jnp.float32)
    block_out = inputs_wide + layer_scale[:, None] * branch_sum
    head_wide = w_head.astype(jnp.float32)
    logits = lax.dot_general(block_out, head_wide, (((0,), (0,)), ((), ())), precision=highest)
    row_max = lax.optimization_barrier(jnp.max(logits, axis=1, keepdims=True))
    exp_terms = jnp.exp(logits - row_max)
    exp_total = lax.optimization_barrier(jnp.sum(exp_terms, axis=1, keepdims=True))
    log_total = jnp.log(exp_total) + row_max
    onehot = (labels[:, None] == jnp.arange(K, dtype=jnp.int32)[None, :]).astype(jnp.float32)
    picked = lax.optimization_barrier(jnp.sum(logits * onehot, axis=1))
    mean_loss = jnp.mean(log_total[:, 0] - picked).reshape(1)
    logit_grad = exp_terms / exp_total - onehot
    out_grad = lax.dot_general(head_wide, logit_grad, (((1,), (1,)), ((), ())), precision=highest)
    d_head = jnp.dot(block_out, logit_grad, precision=highest)
    d_scale = lax.optimization_barrier(jnp.sum(out_grad * branch_sum, axis=1))
    branch_grad = (layer_scale[:, None] * out_grad).astype(jnp.bfloat16)
    hidden_grad = jnp.dot(w_out, branch_grad, preferred_element_type=jnp.float32)
    d_w_out = lax.dot_general(hidden, branch_grad, (((1,), (1,)), ((), ())), preferred_element_type=jnp.float32)
    pre_grad = (hidden_grad * gelu_slope).astype(jnp.bfloat16)
    d_w_in = lax.dot_general(pre_grad, norm_out, (((1,), (1,)), ((), ())), preferred_element_type=jnp.float32)
    norm_grad = lax.dot_general(w_in, pre_grad, (((0,), (0,)), ((), ())), preferred_element_type=jnp.float32)
    gained = norm_gain[:, None] * norm_grad
    conv_grad = (gained - lax.optimization_barrier(jnp.mean(gained, axis=0))[None, :] - normed * lax.optimization_barrier(jnp.mean(gained * normed, axis=0))[None, :]) * inv_std[None, :]
    unused, pullback = jax.vjp(conv_apply, in_grid, dw_weight)
    grid_grad, d_dw = pullback(conv_grad.reshape(C, WIN_H, WIN_W))
    d_features = out_grad + grid_grad.reshape(C, TOKENS)
    return (d_features, d_dw, d_scale, d_w_in, d_w_out, d_head, mean_loss)
```

```python
import functools
import jax
import jax.numpy as jnp
from jax import lax
from jax.experimental import pallas as pl
from jax.experimental.pallas import tpu as pltpu
from jax.sharding import PartitionSpec as P

KS = 7
WIN_H = 32
WIN_W = 32

norm_eps = 1e-06
VMEM_LIMIT = 56 * 1024 * 1024


def slide(values, rows, cols):
    area = values.shape[1]
    token = lax.broadcasted_iota(jnp.int32, values.shape, 1)
    step = rows * WIN_W + cols
    if step == 0:
        return values
    spot = (token & (WIN_W - 1)) if cols else token
    inside = (spot < (WIN_W if cols else area) - step) if step > 0 else (spot >= -step)
    return jnp.where(inside, pltpu.roll(values, (-step) % area, 1), 0.0)


def conv_rows(values, taps):
    half = KS // 2
    shifted = [slide(values, 0, j - half) for j in range(KS)]
    running = None
    for i in range(KS):
        line = sum(taps[:, i * KS + j : i * KS + j + 1] * shifted[j] for j in range(KS))
        line = slide(line, i - half, 0)
        running = line if running is None else running + line
    return running


def gelu_parts(values):
    cum_prob = 0.5 * (1.0 + lax.erf(values * 0.7071067811865476))
    density = jnp.exp(-0.5 * values * values) * 0.3989422804014327
    return (values * cum_prob, cum_prob + values * density)


def place(n):
    me = lax.axis_index("ch")
    return lax.div(me, 4), lax.rem(lax.div(me, 2), 2), lax.rem(me, 2)


def index_of(z, y, c):
    return (z * 2 + y) * 2 + c


def greet(devices, z, a, between=None):
    barrier = pltpu.get_barrier_semaphore()
    for device in devices:
        pl.semaphore_signal(barrier, inc=1, device_id={"ch": device})
    me = lax.axis_index("ch")

    @pl.when(z > 0)
    def _():
        pl.semaphore_signal(barrier, inc=1, device_id={"ch": me - 4})

    @pl.when(z < a - 1)
    def _():
        pl.semaphore_signal(barrier, inc=1, device_id={"ch": me + 4})

    if between is not None:
        between()
    count = len(devices) + jnp.where(z > 0, 1, 0) + jnp.where(z < a - 1, 1, 0)
    pl.semaphore_wait(barrier, count)


def gather_kernel(
    n, x_ref, taps_ref, w_ref, head_ref, out_ref, mixed_ref, wide, conv, send_sem, recv_sem
):
    a = n // 4
    rows = x_ref.shape[0]
    parts = 2 if rows % 32 == 0 else 1
    chunk = rows // parts
    z, y, c = place(n)
    me = index_of(z, y, c)
    twin, across = index_of(z, y, 1 - c), index_of(z, 1 - y, c)

    def convolve():
        wide[...] = x_ref[...].astype(jnp.float32)

        convolve_part(0)

    def convolve_part(h):
        first = h * chunk

        @pl.loop(0, chunk // 8)
        def _(g):
            own = pl.ds(pl.multiple_of(first + g * 8, 8), 8)
            conv[own, :] = conv_rows(wide[own, :], taps_ref[own, :])

        out_ref[pl.ds(pl.multiple_of(me * rows + first, chunk), chunk)] = conv[
            first : first + chunk
        ].astype(jnp.bfloat16)

    greet([twin, across], z, a, convolve)

    def copy(kind, b, device, h):
        piece = out_ref.at[pl.ds(pl.multiple_of(b * rows + h * chunk, chunk), chunk)]
        return pltpu.make_async_remote_copy(
            src_ref=piece,
            dst_ref=piece,
            send_sem=send_sem.at[kind, b * parts + h],
            recv_sem=recv_sem.at[b * parts + h],
            device_id={"ch": device},
        )

    def send_own(h):
        @pl.when(z < a - 1)
        def _():
            copy(0, me, me + 4, h).start()

        @pl.when(z > 0)
        def _():
            copy(1, me, me - 4, h).start()

        copy(2, me, across, h).start()
        copy(3, me, twin, h).start()

    for h in range(parts):
        if h > 0:
            convolve_part(h)
        send_own(h)

    head = head_ref[...]
    high = head.astype(jnp.bfloat16)
    low = (head - high.astype(jnp.float32)).astype(jnp.bfloat16)
    units = w_ref.shape[0]
    part = min(units, 128)

    @pl.loop(0, units // part)
    def _(g):
        own = pl.ds(pl.multiple_of(g * part, part), part)
        weights = w_ref[own, :]
        mixed_ref[own, :] = jnp.dot(
            weights, high, preferred_element_type=jnp.float32
        ) + jnp.dot(weights, low, preferred_element_type=jnp.float32)

    def from_line(s, h):
        below, above = me - 4 * s, me + 4 * s

        @pl.when(z >= s)
        def _():
            copy(0, below, me, h).wait_recv()

            @pl.when(z < a - 1)
            def _():
                copy(0, below, me + 4, h).start()

            copy(2, below, across, h).start()
            copy(3, below, twin, h).start()

        @pl.when(z + s < a)
        def _():
            copy(1, above, me, h).wait_recv()

            @pl.when(z > 0)
            def _():
                copy(1, above, me - 4, h).start()

            copy(2, above, across, h).start()
            copy(3, above, twin, h).start()

    def from_across(s, h):
        def take(b):
            copy(2, b, across, h).wait_recv()
            copy(3, b, twin, h).start()

        if s == 0:
            take(across)
            return

        @pl.when(z >= s)
        def _():
            take(across - 4 * s)

        @pl.when(z + s < a)
        def _():
            take(across + 4 * s)

    for s in range(1, a):
        for h in range(parts):
            from_line(s, h)
            from_across(s - 1, h)
    for h in range(parts):
        from_across(a - 1, h)

    for h in range(parts):
        for q in range(n // 2):
            copy(3, q * 2 + 1 - c, twin, h).wait_recv()
            copy(3, q * 2 + c, twin, h).wait_send()
        for zz in range(a):
            copy(2, index_of(zz, y, c), across, h).wait_send()

            @pl.when((z < a - 1) & (zz <= z))
            def _():
                copy(0, index_of(zz, y, c), me + 4, h).wait_send()

            @pl.when((z > 0) & (zz >= z))
            def _():
                copy(1, index_of(zz, y, c), me - 4, h).wait_send()


def gather(n, x, taps, weights, head):
    rows, cols = x.shape
    return pl.pallas_call(
        functools.partial(gather_kernel, n),
        out_shape=(
            jax.ShapeDtypeStruct((n * rows, cols), x.dtype),
            jax.ShapeDtypeStruct((weights.shape[0], head.shape[1]), jnp.float32),
        ),
        in_specs=[pl.BlockSpec(memory_space=pltpu.VMEM)] * 4,
        out_specs=(pl.BlockSpec(memory_space=pltpu.VMEM),) * 2,
        scratch_shapes=[
            pltpu.VMEM((rows, cols), jnp.float32),
            pltpu.VMEM((rows, cols), jnp.float32),
            pltpu.SemaphoreType.DMA((4, 2 * n)),
            pltpu.SemaphoreType.DMA((2 * n,)),
        ],
        compiler_params=pltpu.CompilerParams(
            collective_id=0, has_side_effects=True, vmem_limit_bytes=VMEM_LIMIT
        ),
    )(x, taps, weights, head)


def total_kernel(n, x_ref, out_ref, buf, from_twin, acc, slots, sums, t_sem, r_sem, g_sem, f_sem):
    m = n // 2
    height, cols = x_ref.shape
    strips = cols // 128
    half = height * strips // 2
    rows = half // m
    me = lax.axis_index("ch")
    q, c = lax.div(me, 2), lax.rem(me, 2)
    twin = q * 2 + 1 - c
    barrier = pltpu.get_barrier_semaphore()
    pl.semaphore_signal(barrier, inc=1, device_id={"ch": twin})
    for d in range(1, m):
        pl.semaphore_signal(barrier, inc=1, device_id={"ch": lax.rem(q + d, m) * 2 + c})
    for j in range(strips):
        buf[j * height : (j + 1) * height, :] = x_ref[:, j * 128 : (j + 1) * 128]
    pl.semaphore_wait(barrier, m)

    def piece(ref, start, length):
        return ref.at[pl.ds(pl.multiple_of(start, 8), length)]

    swap = pltpu.make_async_remote_copy(
        src_ref=piece(buf, (1 - c) * half, half),
        dst_ref=from_twin,
        send_sem=t_sem.at[0],
        recv_sem=t_sem.at[1],
        device_id={"ch": twin},
    )
    swap.start()
    swap.wait_recv()
    acc[...] = buf[pl.ds(pl.multiple_of(c * half, 8), half), :] + from_twin[...]

    def scatter(d):
        other = lax.rem(q + d, m)
        return pltpu.make_async_remote_copy(
            src_ref=piece(acc, other * rows, rows),
            dst_ref=slots.at[d],
            send_sem=r_sem.at[0, d],
            recv_sem=r_sem.at[1, d],
            device_id={"ch": other * 2 + c},
        )

    for d in range(1, m):
        scatter(d).start()
    mine = acc[pl.ds(pl.multiple_of(q * rows, 8), rows), :]
    for d in range(1, m):
        scatter(d).wait_recv()
        mine = mine + slots[d]
    my_start = c * half + q * rows
    sums[pl.ds(pl.multiple_of(my_start, 8), rows), :] = mine

    def spread(d, start, device):
        return pltpu.make_async_remote_copy(
            src_ref=piece(sums, start, rows),
            dst_ref=piece(sums, start, rows),
            send_sem=g_sem.at[0, d],
            recv_sem=g_sem.at[1, d],
            device_id={"ch": device},
        )

    def forward(d, start):
        return pltpu.make_async_remote_copy(
            src_ref=piece(sums, start, rows),
            dst_ref=piece(sums, start, rows),
            send_sem=f_sem.at[0, d],
            recv_sem=f_sem.at[1, d],
            device_id={"ch": twin},
        )

    for d in range(1, m):
        spread(d, my_start, lax.rem(q + d, m) * 2 + c).start()
    forward(0, my_start).start()
    for d in range(1, m):
        start = c * half + lax.rem(q - d + m, m) * rows
        spread(d, start, twin).wait_recv()
        forward(d, start).start()
    for d in range(m):
        forward(d, (1 - c) * half + lax.rem(q - d + m, m) * rows).wait_recv()
    for j in range(strips):
        out_ref[:, j * 128 : (j + 1) * 128] = sums[j * height : (j + 1) * height, :]
    swap.wait_send()
    for d in range(1, m):
        scatter(d).wait_send()
        spread(d, my_start, twin).wait_send()
    for d in range(m):
        forward(d, my_start).wait_send()


def total(n, x):
    height, cols = x.shape
    area = height * (cols // 128)
    m = n // 2
    return pl.pallas_call(
        functools.partial(total_kernel, n),
        out_shape=jax.ShapeDtypeStruct(x.shape, x.dtype),
        in_specs=[pl.BlockSpec(memory_space=pltpu.VMEM)],
        out_specs=pl.BlockSpec(memory_space=pltpu.VMEM),
        scratch_shapes=[
            pltpu.VMEM((area, 128), jnp.float32),
            pltpu.VMEM((area // 2, 128), jnp.float32),
            pltpu.VMEM((area // 2, 128), jnp.float32),
            pltpu.VMEM((m, area // n, 128), jnp.float32),
            pltpu.VMEM((area, 128), jnp.float32),
            pltpu.SemaphoreType.DMA((2,)),
            pltpu.SemaphoreType.DMA((2, m)),
            pltpu.SemaphoreType.DMA((2, m)),
            pltpu.SemaphoreType.DMA((2, m)),
        ],
        compiler_params=pltpu.CompilerParams(
            collective_id=1, has_side_effects=True, vmem_limit_bytes=VMEM_LIMIT
        ),
    )(x)


def scatter_kernel(
    n, conv_ref, w_ref, p_ref, rows_ref, seen_ref, out_ref,
    g_ref, t_in, y_in, u_in, d_in, y_out, z_out, t_sem, y_sem, u_sem, d_sem, zs_sem
):
    a = n // 4
    rows = out_ref.shape[0]
    z, y, c = place(n)
    me = index_of(z, y, c)
    twin, across = index_of(z, y, 1 - c), index_of(z, 1 - y, c)
    greet([twin, across], z, a)

    def own(b):
        return pl.ds(pl.multiple_of(b * rows, rows), rows)

    def order(k):
        if k == a - 1:
            return z
        low = jnp.where(k < a - 1 - z, a - 1 - k, k - (a - 1 - z))
        high = jnp.where(k < z, k, a - 1 - (k - z))
        return jnp.where(2 * z < a, low, high)

    def to_twin(zz, side, core):
        return pltpu.make_async_remote_copy(
            src_ref=g_ref.at[own(index_of(zz, side, core))],
            dst_ref=t_in.at[zz * 2 + side],
            send_sem=t_sem.at[0, zz * 2 + side],
            recv_sem=t_sem.at[1, zz * 2 + side],
            device_id={"ch": twin},
        )

    def to_across(k, zz):
        return pltpu.make_async_remote_copy(
            src_ref=y_out.at[k],
            dst_ref=y_in.at[zz],
            send_sem=y_sem.at[0, zz],
            recv_sem=y_sem.at[1, zz],
            device_id={"ch": across},
        )

    def along(k, zz, landing, sem, device):
        return pltpu.make_async_remote_copy(
            src_ref=z_out.at[k],
            dst_ref=landing.at[zz],
            send_sem=zs_sem.at[k],
            recv_sem=sem.at[zz],
            device_id={"ch": device},
        )

    tokens = conv_ref.shape[1]
    tok_mean, inv_std = rows_ref[0:1, :], rows_ref[1:2, :]
    mean_gained, mean_both = rows_ref[2:3, :], rows_ref[3:4, :]

    def fill(zz, side, core):
        mine = own(index_of(zz, side, core))
        grad = jnp.dot(w_ref[mine, :], p_ref[...], preferred_element_type=jnp.float32)
        normed = (conv_ref[mine, :].astype(jnp.float32) - tok_mean) * inv_std
        term = (grad - mean_gained - normed * mean_both) * inv_std
        g_ref[mine, :tokens] = term.astype(jnp.bfloat16)
        g_ref[mine, tokens:] = seen_ref[mine, :]

    def cross(k):
        zz = order(k)
        to_twin(zz, 1 - y, c).wait_recv()
        y_out[k] = (
            g_ref[own(index_of(zz, 1 - y, c))].astype(jnp.float32)
            + t_in[zz * 2 + 1 - y].astype(jnp.float32)
        ).astype(jnp.bfloat16)
        to_across(k, zz).start()

    for k in range(a):
        fill(order(k), 1 - y, 1 - c)
        to_twin(order(k), 1 - y, 1 - c).start()
        fill(order(k), 1 - y, c)
        if k > 0:
            cross(k - 1)
    fill(order(0), y, 1 - c)
    to_twin(order(0), y, 1 - c).start()
    cross(a - 1)
    fill(order(0), y, c)
    for k in range(a):
        zz = order(k)
        if k < a - 1:
            fill(order(k + 1), y, 1 - c)
            to_twin(order(k + 1), y, 1 - c).start()
            fill(order(k + 1), y, c)
        to_twin(zz, y, c).wait_recv()
        to_across(k, zz).wait_recv()
        term = (
            g_ref[own(index_of(zz, y, c))].astype(jnp.float32)
            + t_in[zz * 2 + y].astype(jnp.float32)
            + y_in[zz].astype(jnp.float32)
        )
        if k < a - 1:
            out_ref[...] = term

            @pl.when((zz > z) & (z > 0))
            def _():
                along(k, zz, u_in, u_sem, me).wait_recv()
                out_ref[...] += u_in[zz].astype(jnp.float32)

            @pl.when((zz < z) & (z < a - 1))
            def _():
                along(k, zz, d_in, d_sem, me).wait_recv()
                out_ref[...] += d_in[zz].astype(jnp.float32)

            z_out[k] = out_ref[...].astype(jnp.bfloat16)

            @pl.when(zz > z)
            def _():
                along(k, zz, u_in, u_sem, me + 4).start()

            @pl.when(zz < z)
            def _():
                along(k, zz, d_in, d_sem, me - 4).start()

        else:
            out_ref[...] = term

            @pl.when(z > 0)
            def _():
                along(0, z, u_in, u_sem, me).wait_recv()
                out_ref[...] += u_in[z].astype(jnp.float32)

            @pl.when(z < a - 1)
            def _():
                along(0, z, d_in, d_sem, me).wait_recv()
                out_ref[...] += d_in[z].astype(jnp.float32)

    for k in range(a):
        zz = order(k)
        to_twin(zz, 1 - y, 1 - c).wait_send()
        to_twin(zz, y, 1 - c).wait_send()
        to_across(k, zz).wait_send()
        if k < a - 1:
            along(k, zz, u_in, u_sem, me).wait_send()


def scatter(n, conv_all, weights, pre_grad, token_rows, seen):
    rows, cols = conv_all.shape[0] // n, conv_all.shape[1] + seen.shape[1]
    a = n // 4
    return pl.pallas_call(
        functools.partial(scatter_kernel, n),
        out_shape=jax.ShapeDtypeStruct((rows, cols), jnp.float32),
        in_specs=[pl.BlockSpec(memory_space=pltpu.VMEM)] * 5,
        out_specs=pl.BlockSpec(memory_space=pltpu.VMEM),
        scratch_shapes=[
            pltpu.VMEM((n * rows, cols), jnp.bfloat16),
            pltpu.VMEM((n // 2, rows, cols), jnp.bfloat16),
            pltpu.VMEM((a, rows, cols), jnp.bfloat16),
            pltpu.VMEM((a, rows, cols), jnp.bfloat16),
            pltpu.VMEM((a, rows, cols), jnp.bfloat16),
            pltpu.VMEM((a, rows, cols), jnp.bfloat16),
            pltpu.VMEM((a, rows, cols), jnp.bfloat16),
            pltpu.SemaphoreType.DMA((2, n // 2)),
            pltpu.SemaphoreType.DMA((2, a)),
            pltpu.SemaphoreType.DMA((a,)),
            pltpu.SemaphoreType.DMA((a,)),
            pltpu.SemaphoreType.DMA((a,)),
        ],
        compiler_params=pltpu.CompilerParams(
            collective_id=2, has_side_effects=True, vmem_limit_bytes=VMEM_LIMIT
        ),
    )(conv_all, weights, pre_grad, token_rows, seen)


LANES = 128
SUB = 8
PAD_W = WIN_W + 16


def fit(value, axis, length):
    short = length - value.shape[axis]
    if short == 0:
        return value
    pads = [(0, 0)] * value.ndim
    pads[axis] = (0, short)
    return jnp.pad(value, pads)


def clear_pads(grid_ref):
    half = KS // 2
    blank = jnp.zeros((half, PAD_W, LANES), jnp.float32)
    grid_ref[0:half] = blank
    grid_ref[half + WIN_H : 2 * half + WIN_H] = blank

    @pl.loop(0, WIN_H)
    def _(h):
        edge = jnp.zeros((SUB, LANES), jnp.float32)
        grid_ref[half + h, 0:SUB, :] = edge
        grid_ref[half + h, SUB + WIN_W : PAD_W, :] = edge


def put_strip(grid_ref, strip, block):
    half = KS // 2
    turned = block.T
    for r in range(LANES // WIN_W):
        grid_ref[half + strip * (LANES // WIN_W) + r, SUB : SUB + WIN_W, :] = turned[
            r * WIN_W : (r + 1) * WIN_W
        ]


def spread_taps(taps_ref, wide_ref):
    for k in range(KS * KS):
        wide_ref[k] = jnp.broadcast_to(taps_ref[k : k + 1, :], (SUB, LANES))


ROWS_AT_ONCE = 8


def conv_piece(grid_ref, taps_ref, first, col, flip=False):
    outs = [None] * ROWS_AT_ONCE
    for j in range(KS):
        start = SUB + col + j - KS // 2
        seen = [
            grid_ref[first + r, start : start + SUB, :] for r in range(ROWS_AT_ONCE + KS - 1)
        ]
        for i in range(KS):
            k = i * KS + j
            tap = taps_ref[KS * KS - 1 - k if flip else k]
            for r in range(ROWS_AT_ONCE):
                term = tap * seen[r + i]
                outs[r] = term if outs[r] is None else outs[r] + term
    return outs


def tail_kernel(
    x_ref, grad_ref, taps_ref, lg_ref, head_ref, seen_ref, scale_ref,
    dx_ref, dtaps_ref, dscale_ref, dhead_ref,
    x_grid, g_grid, turned, wide, taps, sums
):
    rows, tokens = x_ref.shape
    strips = tokens // LANES
    wide[...] = jnp.zeros_like(wide)
    wide[0:rows, :] = x_ref[...].astype(jnp.float32)
    spread_taps(taps_ref, taps)
    clear_pads(x_grid)
    clear_pads(g_grid)
    for s in range(strips):
        put_strip(x_grid, s, wide[:, s * LANES : (s + 1) * LANES])
        put_strip(g_grid, s, grad_ref[:, s * LANES : (s + 1) * LANES])
    sums[...] = jnp.zeros_like(sums)
    half = KS // 2

    @pl.loop(0, WIN_H // ROWS_AT_ONCE)
    def _(block):
        first = block * ROWS_AT_ONCE
        for col in range(0, WIN_W, SUB):
            outs = conv_piece(g_grid, taps, first, col, flip=True)
            for r in range(ROWS_AT_ONCE):
                turned[first + r, col : col + SUB, :] = outs[r]
            grads = [
                g_grid[first + half + r, SUB + col : SUB + col + SUB, :]
                for r in range(ROWS_AT_ONCE)
            ]
            for j in range(KS):
                start = SUB + col + j - half
                seen = [
                    x_grid[first + r, start : start + SUB, :]
                    for r in range(ROWS_AT_ONCE + KS - 1)
                ]
                for i in range(KS):
                    total = sums[i * KS + j]
                    for r in range(ROWS_AT_ONCE):
                        total = total + grads[r] * seen[r + i]
                    sums[i * KS + j] = total

    for k in range(KS * KS):
        dtaps_ref[k : k + 1, :] = jnp.sum(sums[k], axis=0, keepdims=True)

    head = head_ref[...].astype(jnp.float32).T.astype(jnp.bfloat16)
    per = LANES // WIN_W
    for s in range(strips):
        own = slice(s * LANES, (s + 1) * LANES)
        back = jnp.concatenate([turned[s * per + r] for r in range(per)], axis=0).T
        out_grad = jnp.dot(head, lg_ref[:, own], preferred_element_type=jnp.float32)
        dx_ref[:, own] = (back + out_grad)[0:rows]
    direct = lax.dot_general(
        lg_ref[...], wide[...].astype(jnp.bfloat16), (((1,), (1,)), ((), ())),
        preferred_element_type=jnp.float32,
    )
    seen = seen_ref[...]
    classes = dhead_ref.shape[0]
    dhead_ref[...] = (direct + scale_ref[...] * seen)[0:classes]
    dscale_ref[...] = jnp.sum(head_ref[...].astype(jnp.float32) * seen, axis=0, keepdims=True)


def tail(classes, x, grad, taps, lg, head, seen, scale):
    rows, tokens = x.shape
    vmem = pl.BlockSpec(memory_space=pltpu.VMEM)
    return pl.pallas_call(
        tail_kernel,
        out_shape=(
            jax.ShapeDtypeStruct((rows, tokens), jnp.float32),
            jax.ShapeDtypeStruct((KS * KS, LANES), jnp.float32),
            jax.ShapeDtypeStruct((1, LANES), jnp.float32),
            jax.ShapeDtypeStruct((classes, LANES), jnp.float32),
        ),
        in_specs=[vmem] * 7,
        out_specs=(vmem,) * 4,
        scratch_shapes=[
            pltpu.VMEM((WIN_H + KS - 1, PAD_W, LANES), jnp.float32),
            pltpu.VMEM((WIN_H + KS - 1, PAD_W, LANES), jnp.float32),
            pltpu.VMEM((WIN_H, WIN_W, LANES), jnp.float32),
            pltpu.VMEM((LANES, tokens), jnp.float32),
            pltpu.VMEM((KS * KS, SUB, LANES), jnp.float32),
            pltpu.VMEM((KS * KS, SUB, LANES), jnp.float32),
        ],
        compiler_params=pltpu.CompilerParams(vmem_limit_bytes=VMEM_LIMIT),
    )(x, grad, taps, lg, head, seen, scale)


def dot(lhs, rhs, over, precision=None):
    return lax.dot_general(
        lhs, rhs, ((over[:1], over[1:]), ((), ())),
        precision=precision, preferred_element_type=jnp.float32,
    )


def per_device(n, features, dw_weight, norm_gain, layer_scale, w_in, w_out, w_head, labels):
    fine = lax.Precision.HIGH
    my_rows, tok_count = features.shape
    channels, class_count = w_head.shape
    row_offset = lax.axis_index("ch") * my_rows
    classes = -(-class_count // max(n, 16)) * max(n, 16)
    head_pad = jnp.pad(w_head, ((0, 0), (0, classes - class_count)))
    scaled_head = layer_scale[:, None] * head_pad.astype(jnp.float32)
    conv_all, mixed = gather(n, features, dw_weight, w_out, scaled_head)
    conv_wide = conv_all.astype(jnp.float32)
    tok_mean = jnp.mean(conv_wide, axis=0)
    centered = conv_wide - tok_mean[None, :]
    tok_var = jnp.mean(centered * centered, axis=0)
    inv_std = 1.0 / jnp.sqrt(tok_var + norm_eps)
    norm_out = (norm_gain[:, None] * (centered * inv_std[None, :])).astype(jnp.bfloat16)
    pre_act = jnp.dot(w_in, norm_out, preferred_element_type=jnp.float32)
    gelu_out, gelu_slope = gelu_parts(pre_act)
    hidden = gelu_out.astype(jnp.bfloat16)

    my_scale = lax.dynamic_slice_in_dim(layer_scale, row_offset, my_rows, 0)
    my_head = lax.dynamic_slice_in_dim(head_pad, row_offset, my_rows, 0)
    part = dot(mixed, hidden.astype(jnp.float32), (0, 0), fine) + dot(my_head, features, (0, 0))
    logits = total(n, part)

    kinds = lax.broadcasted_iota(jnp.int32, (classes, tok_count), 0)
    logits = jnp.where(kinds < class_count, logits, -jnp.inf)
    row_max = jnp.max(logits, axis=0, keepdims=True)
    exp_terms = jnp.exp(logits - row_max)
    exp_total = jnp.sum(exp_terms, axis=0, keepdims=True)
    log_total = jnp.log(exp_total) + row_max
    hit = kinds == labels[None, :]
    picked = jnp.sum(jnp.where(hit, logits, 0.0), axis=0)
    mean_loss = jnp.mean(log_total[0] - picked).reshape(1)
    logit_grad = exp_terms / exp_total - hit.astype(jnp.float32)
    grad_narrow = logit_grad.astype(jnp.bfloat16)

    seen = dot(hidden, grad_narrow, (1, 1))
    hidden_grad = dot(mixed, logit_grad, (1, 0), fine)
    seen_narrow = seen.astype(jnp.bfloat16)
    d_w_out = dot(seen_narrow, scaled_head.astype(jnp.bfloat16), (1, 1))
    branch_seen = dot(w_out, seen_narrow, (0, 0)).astype(jnp.bfloat16)
    pre_grad_wide = hidden_grad * gelu_slope
    pre_grad = pre_grad_wide.astype(jnp.bfloat16)
    d_w_in = dot(pre_grad, norm_out, (1, 1))
    gain_rows = jnp.sum(w_in.astype(jnp.float32) * norm_gain[None, :], axis=1)
    mean_gained = jnp.sum(gain_rows[:, None] * pre_grad_wide, axis=0) / channels
    mean_both = jnp.sum(pre_act * pre_grad_wide, axis=0) / channels
    weights = (w_in.astype(jnp.float32) * norm_gain[None, :]).astype(jnp.bfloat16).T
    width = -(-classes // 128) * 128
    token_rows = jnp.stack([tok_mean, inv_std, mean_gained, mean_both])
    token_rows = jnp.pad(token_rows, ((0, 4), (0, 0)))
    branch_seen = jnp.pad(branch_seen, ((0, 0), (0, width - classes)))
    landed = scatter(n, conv_all, weights, pre_grad, token_rows, branch_seen)
    conv_grad = fit(landed[:, :tok_count], 0, LANES)
    my_seen = fit(landed[:, tok_count : tok_count + classes].T, 1, LANES)
    own_head = fit(my_head.T, 1, LANES)
    d_features, d_dw, d_scale, d_head = tail(
        class_count, features, conv_grad, fit(dw_weight.T, 1, LANES), grad_narrow, own_head, my_seen,
        fit(my_scale[None, :], 1, LANES),
    )
    d_dw = d_dw.T[:my_rows]
    d_scale = d_scale[0, :my_rows]
    d_head = d_head.T[:my_rows]
    return (d_features, d_dw, d_scale, d_w_in, d_w_out, d_head, mean_loss)


def solution(mesh):
    placed = (P("ch", "grp"), P("ch", None), P(), P(), P("ch", None), P("ch", None), P(), P("grp"))
    return jax.shard_map(
        functools.partial(per_device, mesh.shape["ch"]),
        mesh=mesh,
        in_specs=placed,
        out_specs=(
            P("ch", "grp"),
            P("ch", "grp"),
            P(("grp", "ch")),
            P(("grp", "ch"), None),
            P(("grp", "ch"), None),
            P("ch", "grp"),
            P("grp"),
        ),
        check_vma=False,
    )
```

```python
import functools
import jax
import jax.numpy as jnp
from jax import lax
from jax.experimental import pallas as pl
from jax.experimental.pallas import tpu as pltpu
from jax.sharding import PartitionSpec as P

KS = 7
WIN_H = 32
WIN_W = 32

norm_eps = 1e-06
VMEM_LIMIT = 56 * 1024 * 1024


def place(n):
    me = lax.axis_index("ch")
    return lax.div(me, 4), lax.rem(lax.div(me, 2), 2), lax.rem(me, 2)


def index_of(z, y, c):
    return (z * 2 + y) * 2 + c


LANES = 128
MOVES = WIN_H // 8
SUB = 8
PAD_W = WIN_W + 16


def fit(value, axis, length):
    short = length - value.shape[axis]
    if short == 0:
        return value
    pads = [(0, 0)] * value.ndim
    pads[axis] = (0, short)
    return jnp.pad(value, pads)


def clear_pads(grid_ref):
    half = KS // 2
    blank = jnp.zeros((half, PAD_W, LANES), jnp.float32)
    grid_ref[0:half] = blank
    grid_ref[half + WIN_H : 2 * half + WIN_H] = blank

    @pl.loop(0, WIN_H)
    def _(h):
        edge = jnp.zeros((SUB, LANES), jnp.float32)
        grid_ref[half + h, 0:SUB, :] = edge
        grid_ref[half + h, SUB + WIN_W : PAD_W, :] = edge


def put_strip(grid_ref, strip, block):
    half = KS // 2
    turned = block.T
    for r in range(LANES // WIN_W):
        grid_ref[half + strip * (LANES // WIN_W) + r, SUB : SUB + WIN_W, :] = turned[
            r * WIN_W : (r + 1) * WIN_W
        ]


def spread_taps(taps_ref, wide_ref):
    for k in range(KS * KS):
        wide_ref[k] = jnp.broadcast_to(taps_ref[k : k + 1, :], (SUB, LANES))


ROWS_AT_ONCE = 8


def conv_piece(grid_ref, taps_ref, first, col, flip=False):
    outs = [None] * ROWS_AT_ONCE
    for j in range(KS):
        start = SUB + col + j - KS // 2
        seen = [
            grid_ref[first + r, start : start + SUB, :] for r in range(ROWS_AT_ONCE + KS - 1)
        ]
        for i in range(KS):
            k = i * KS + j
            tap = taps_ref[KS * KS - 1 - k if flip else k]
            for r in range(ROWS_AT_ONCE):
                term = tap * seen[r + i]
                outs[r] = term if outs[r] is None else outs[r] + term
    return outs


def tail_kernel(
    x_ref, grad_ref, taps_ref, lg_ref, head_ref, seen_ref, scale_ref, loss_ref, dwi_ref, dwo_ref,
    dx_ref, dtaps_ref, dscale_ref, dhead_ref, mean_ref, dwi_out, dwo_out,
    x_grid, g_grid, turned, wide, taps, sums, dwi_buf, dwo_buf, move_sem
):
    rows, tokens = x_ref.shape
    tall = dwi_ref.shape[0] // MOVES
    through = ((dwi_ref, dwi_buf, dwi_out), (dwo_ref, dwo_buf, dwo_out))

    def fetch(i, k):
        own = rows_of(k, tall)
        return pltpu.make_async_copy(through[i][0].at[own], through[i][1].at[own], move_sem.at[0, i, k])

    def put(i, k):
        own = rows_of(k, tall)
        return pltpu.make_async_copy(through[i][1].at[own], through[i][2].at[own], move_sem.at[1, i, k])

    for k in range(MOVES):
        for i in range(2):
            fetch(i, k).start()
    mean_ref[...] = jnp.sum(loss_ref[...], axis=1, keepdims=True) * (1.0 / tokens)
    strips = tokens // LANES
    wide[...] = jnp.zeros_like(wide)
    wide[0:rows, :] = x_ref[...].astype(jnp.float32)
    spread_taps(taps_ref, taps)
    clear_pads(x_grid)
    clear_pads(g_grid)
    for s in range(strips):
        put_strip(x_grid, s, wide[:, s * LANES : (s + 1) * LANES])
        put_strip(g_grid, s, grad_ref[:, s * LANES : (s + 1) * LANES])
    sums[...] = jnp.zeros_like(sums)
    half = KS // 2

    @pl.loop(0, WIN_H // ROWS_AT_ONCE)
    def _(block):
        for i in range(2):
            fetch(i, block).wait()
            put(i, block).start()
        first = block * ROWS_AT_ONCE
        for col in range(0, WIN_W, SUB):
            outs = conv_piece(g_grid, taps, first, col, flip=True)
            for r in range(ROWS_AT_ONCE):
                turned[first + r, col : col + SUB, :] = outs[r]
            grads = [
                g_grid[first + half + r, SUB + col : SUB + col + SUB, :]
                for r in range(ROWS_AT_ONCE)
            ]
            for j in range(KS):
                start = SUB + col + j - half
                seen = [
                    x_grid[first + r, start : start + SUB, :]
                    for r in range(ROWS_AT_ONCE + KS - 1)
                ]
                for i in range(KS):
                    total = sums[i * KS + j]
                    for r in range(ROWS_AT_ONCE):
                        total = total + grads[r] * seen[r + i]
                    sums[i * KS + j] = total

    for k in range(KS * KS):
        dtaps_ref[k : k + 1, :] = jnp.sum(sums[k], axis=0, keepdims=True)

    head = head_ref[...].astype(jnp.float32).T.astype(jnp.bfloat16)
    per = LANES // WIN_W
    for s in range(strips):
        own = slice(s * LANES, (s + 1) * LANES)
        back = jnp.concatenate([turned[s * per + r] for r in range(per)], axis=0).T
        out_grad = jnp.dot(head, lg_ref[:, own], preferred_element_type=jnp.float32)
        dx_ref[:, own] = (back + out_grad)[0:rows]
    direct = lax.dot_general(
        lg_ref[...], wide[...].astype(jnp.bfloat16), (((1,), (1,)), ((), ())),
        preferred_element_type=jnp.float32,
    )
    seen = seen_ref[...]
    classes = dhead_ref.shape[0]
    dhead_ref[...] = (direct + scale_ref[...] * seen)[0:classes]
    dscale_ref[...] = jnp.sum(head_ref[...].astype(jnp.float32) * seen, axis=0, keepdims=True)
    for k in range(MOVES):
        for i in range(2):
            put(i, k).wait()


def tail(classes, x, grad, taps, lg, head, seen, scale, loss, d_w_in, d_w_out):
    rows, tokens = x.shape
    vmem = pl.BlockSpec(memory_space=pltpu.VMEM)
    hbm = pl.BlockSpec(memory_space=pl.ANY)
    return pl.pallas_call(
        tail_kernel,
        out_shape=(
            jax.ShapeDtypeStruct((rows, tokens), jnp.float32),
            jax.ShapeDtypeStruct((KS * KS, LANES), jnp.float32),
            jax.ShapeDtypeStruct((1, LANES), jnp.float32),
            jax.ShapeDtypeStruct((classes, LANES), jnp.float32),
            jax.ShapeDtypeStruct((1, 1), jnp.float32),
            jax.ShapeDtypeStruct(d_w_in.shape, jnp.float32),
            jax.ShapeDtypeStruct(d_w_out.shape, jnp.float32),
        ),
        in_specs=[vmem] * 8 + [hbm] * 2,
        out_specs=(vmem,) * 5 + (hbm,) * 2,
        scratch_shapes=[
            pltpu.VMEM((WIN_H + KS - 1, PAD_W, LANES), jnp.float32),
            pltpu.VMEM((WIN_H + KS - 1, PAD_W, LANES), jnp.float32),
            pltpu.VMEM((WIN_H, WIN_W, LANES), jnp.float32),
            pltpu.VMEM((LANES, tokens), jnp.float32),
            pltpu.VMEM((KS * KS, SUB, LANES), jnp.float32),
            pltpu.VMEM((KS * KS, SUB, LANES), jnp.float32),
            pltpu.VMEM(d_w_in.shape, jnp.float32),
            pltpu.VMEM(d_w_out.shape, jnp.float32),
            pltpu.SemaphoreType.DMA((2, 2, MOVES)),
        ],
        compiler_params=pltpu.CompilerParams(vmem_limit_bytes=VMEM_LIMIT),
    )(x, grad, taps, lg, head, seen, scale, loss, d_w_in, d_w_out)


PARTS = 2
SQRT_HALF = 0.7071067811865476
NORMAL = 0.3989422804014327


def lanes_of(j, size=LANES):
    return pl.ds(pl.multiple_of(j * size, size), size)


def rows_of(j, size):
    return pl.ds(pl.multiple_of(j * size, size), size)


def nt_dot(lhs, rhs):
    return lax.dot_general(lhs, rhs, (((1,), (1,)), ((), ())), preferred_element_type=jnp.float32)


def nn_dot(lhs, rhs):
    return jnp.dot(lhs, rhs, preferred_element_type=jnp.float32)


def three_parts(value):
    high = value.astype(jnp.bfloat16)
    rest = value - high.astype(jnp.float32)
    middle = rest.astype(jnp.bfloat16)
    low = (rest - middle.astype(jnp.float32)).astype(jnp.bfloat16)
    return high, middle, low


def stack_rows(parts, height, width):
    row = lax.broadcasted_iota(jnp.int32, (height, width), 0)
    out = jnp.zeros((height, width), jnp.float32)
    for i, part in enumerate(parts):
        out = jnp.where(row == i, part.astype(jnp.float32), out)
    return out.astype(jnp.bfloat16)


def block_kernel(
    n, class_count,
    x_ref, taps_ref, gain_ref, scale_ref, labels_ref, own_head_ref, head_hbm, w_in_hbm, w_out_hbm,
    land_ref, seen_ref, lg_ref, loss_ref, dwi_hbm, dwo_hbm,
    head_ref, w_in_ref, w_out_ref, load_sem,
    x_grid, wide, taps, turned,
    conv_all, wg, wg_turned, acc, gains, stats, token_rows,
    sh_high, sh_low, mix_high, mix_low, mix,
    hidden, slope, narrow, back_rows, seen_narrow,
    tw_keep, tw_out, tw_in, rs_out, slots, packs,
    msg, t_in, y_out, y_in, u_in, d_in, z_out, sums,
    dwi_buf, dwo_buf, store_sem,
    send_sem, recv_sem, tw_sem, rs_sem, lg_sem, f_sem,
    t_sem, y_sem, u_sem, d_sem, zs_sem,
):
    a, m = n // 4, n // 2
    rows, tokens = x_ref.shape
    units, channels = w_in_ref.shape
    strips = tokens // LANES
    classes = lg_ref.shape[0]
    pack = classes // 2
    z, y, c = place(n)
    me = index_of(z, y, c)
    chip = z * 2 + y
    twin, across = index_of(z, y, 1 - c), index_of(z, 1 - y, c)
    f32 = jnp.float32

    loads = [
        pltpu.make_async_copy(src, dst, load_sem.at[i])
        for i, (src, dst) in enumerate(
            ((w_in_hbm, w_in_ref), (head_hbm, head_ref), (w_out_hbm, w_out_ref))
        )
    ]
    barrier = pltpu.get_barrier_semaphore()
    pl.semaphore_signal(barrier, inc=1, device_id={"ch": twin})
    for d in range(1, m):
        pl.semaphore_signal(barrier, inc=1, device_id={"ch": lax.rem(chip + d, m) * 2 + c})
    for load in loads:
        load.start()

    span = tokens // PARTS
    half = KS // 2
    per = LANES // WIN_W
    if rows < LANES:
        wide[...] = jnp.zeros_like(wide)
    wide[0:rows, :] = x_ref[...].astype(f32)
    spread_taps(taps_ref, taps)
    clear_pads(x_grid)
    for s in range(strips):
        put_strip(x_grid, s, wide[:, s * LANES : (s + 1) * LANES])

    def convolve(h):
        blocks = WIN_H // ROWS_AT_ONCE // PARTS

        @pl.loop(h * blocks, (h + 1) * blocks)
        def _(block):
            first = block * ROWS_AT_ONCE
            for col in range(0, WIN_W, SUB):
                outs = conv_piece(x_grid, taps, first, col)
                for r in range(ROWS_AT_ONCE):
                    turned[first + r, col : col + SUB, :] = outs[r]

        for s in range(h * strips // PARTS, (h + 1) * strips // PARTS):
            back = jnp.concatenate([turned[s * per + r] for r in range(per)], axis=0).T
            conv_all[rows_of(me, rows), s * LANES : (s + 1) * LANES] = back[0:rows].astype(
                jnp.bfloat16
            )

    def copy(kind, b, device, h):
        piece = conv_all.at[rows_of(b, rows), pl.ds(h * span, span)]
        return pltpu.make_async_remote_copy(
            src_ref=piece,
            dst_ref=piece,
            send_sem=send_sem.at[kind, b * PARTS + h],
            recv_sem=recv_sem.at[b * PARTS + h],
            device_id={"ch": device},
        )

    for h in range(PARTS):
        convolve(h)
        if h == 0:
            pl.semaphore_wait(barrier, m)

        @pl.when(z < a - 1)
        def _():
            copy(0, me, me + 4, h).start()

        @pl.when(z > 0)
        def _():
            copy(1, me, me - 4, h).start()

        copy(2, me, across, h).start()
        copy(3, me, twin, h).start()

    loads[0].wait()
    pair = 2 * rows
    gains[...] = jnp.zeros_like(gains)
    ones = jnp.ones((pair, LANES), jnp.bfloat16)
    for p in range(m):
        own = slice(p * pair, (p + 1) * pair)
        gained = w_in_ref[:, own].astype(f32) * gain_ref[:, own]
        gained_narrow = gained.astype(jnp.bfloat16)
        wg[p] = gained_narrow
        wg_turned[p] = gained.T.astype(jnp.bfloat16)
        gains[...] += nn_dot(gained_narrow, ones)

    def mix_weights():
        loads[1].wait()
        loads[2].wait()
        scaled = head_ref[...].astype(f32) * scale_ref[...]
        high = scaled.astype(jnp.bfloat16)
        sh_high[...] = jnp.zeros_like(sh_high)
        sh_low[...] = jnp.zeros_like(sh_low)
        sh_high[0:class_count, :] = high
        sh_low[0:class_count, :] = (scaled - high.astype(f32)).astype(jnp.bfloat16)
        mixed = nt_dot(sh_high[...], w_out_ref[...]) + nt_dot(sh_low[...], w_out_ref[...])
        high = mixed.astype(jnp.bfloat16)
        mix_high[...] = high
        mix_low[...] = (mixed - high.astype(f32)).astype(jnp.bfloat16)
        mix[...] = nt_dot(w_out_ref[...], sh_high[...]).astype(jnp.bfloat16)

    def absorb(p, first=False):
        for h in range(PARTS):
            copy(3, p * 2 + 1 - c, twin, h).wait_recv()

        @pl.loop(0, tokens // (2 * LANES))
        def _(g):
            own = lanes_of(g, 2 * LANES)
            block = conv_all[rows_of(p, pair), own]
            product = nn_dot(wg[p], block)
            if first:
                acc[:, own] = product
            else:
                acc[:, own] += product
            block_wide = block.astype(f32)
            whole = jnp.sum(block_wide, axis=0, keepdims=True)
            off = block_wide - whole * (1.0 / pair)
            stats[p, 0:1, own] = whole
            stats[p, 1:2, own] = jnp.sum(off * off, axis=0, keepdims=True)

    def from_line(s, h):
        below, above = me - 4 * s, me + 4 * s

        @pl.when(z >= s)
        def _():
            copy(0, below, me, h).wait_recv()

            @pl.when(z < a - 1)
            def _():
                copy(0, below, me + 4, h).start()

            copy(2, below, across, h).start()
            copy(3, below, twin, h).start()

        @pl.when(z + s < a)
        def _():
            copy(1, above, me, h).wait_recv()

            @pl.when(z > 0)
            def _():
                copy(1, above, me - 4, h).start()

            copy(2, above, across, h).start()
            copy(3, above, twin, h).start()

    def from_across(s, h):
        def take(b):
            copy(2, b, across, h).wait_recv()
            copy(3, b, twin, h).start()

        if s == 0:
            take(across)
            return

        @pl.when(z >= s)
        def _():
            take(across - 4 * s)

        @pl.when(z + s < a)
        def _():
            take(across + 4 * s)

    def absorb_at(s, side):
        if s == 0:
            absorb(z * 2 + side, first=side is y)
            return

        @pl.when(z >= s)
        def _():
            absorb((z - s) * 2 + side)

        @pl.when(z + s < a)
        def _():
            absorb((z + s) * 2 + side)

    mingle = a <= 4
    for s in range(1, a):
        for h in range(PARTS):
            from_line(s, h)
            from_across(s - 1, h)
        if mingle:
            if s == 1:
                mix_weights()
            absorb_at(s - 1, y)
            if s > 1:
                absorb_at(s - 2, 1 - y)
    if not mingle:
        mix_weights()
    for h in range(PARTS):
        from_across(a - 1, h)
    if mingle:
        absorb_at(a - 1, y)
        if a > 1:
            absorb_at(a - 2, 1 - y)
        absorb_at(a - 1, 1 - y)
    else:
        acc[...] = jnp.zeros_like(acc)

        @pl.loop(0, m)
        def _(p):
            absorb(p)

    total = stats[0, 0:1, :]
    for p in range(1, m):
        total = total + stats[p, 0:1, :]
    tok_mean = total * (1.0 / channels)
    square = jnp.zeros_like(total)
    for p in range(m):
        off = stats[p, 0:1, :] * (1.0 / pair) - tok_mean
        square = square + stats[p, 1:2, :] + (pair * off) * off
    inv_std = 1.0 / jnp.sqrt(square * (1.0 / channels) + norm_eps)
    token_rows[0:1, :] = tok_mean
    token_rows[1:2, :] = inv_std

    step = m // strips
    base = lax.div(chip, step) if step > 1 else chip
    lane = lax.broadcasted_iota(jnp.int32, (pack, LANES), 1)
    left = lane < LANES // 2
    chunk = min(units, 64)

    def to_twin_strip(d):
        return pltpu.make_async_remote_copy(
            src_ref=tw_out.at[d], dst_ref=tw_in.at[d],
            send_sem=tw_sem.at[0, d], recv_sem=tw_sem.at[1, d], device_id={"ch": twin},
        )

    def to_owner(d, owner, source):
        return pltpu.make_async_remote_copy(
            src_ref=rs_out.at[d], dst_ref=slots.at[source],
            send_sem=rs_sem.at[0, d], recv_sem=rs_sem.at[1, source],
            device_id={"ch": owner * 2 + c},
        )

    def strip_at(d):
        return lax.rem(base + d + 1, strips)

    def activate(d):
        j = strip_at(d)
        own = lanes_of(j)
        mean_here, inv_here = token_rows[0:1, own], token_rows[1:2, own]

        @pl.loop(0, units // chunk)
        def _(g):
            piece = rows_of(g, chunk)
            pre = (acc[piece, own] - gains[piece, :] * mean_here) * inv_here
            cum_prob = 0.5 * (1.0 + lax.erf(pre * SQRT_HALF))
            density = jnp.exp(-0.5 * pre * pre) * NORMAL
            acc[piece, own] = pre
            hidden[piece, own] = (pre * cum_prob).astype(jnp.bfloat16)
            slope[piece, own] = (cum_prob + pre * density) * inv_here

        active = hidden[:, own]
        scores = (
            nn_dot(mix_high[...], active)
            + nn_dot(mix_low[...], active)
            + nn_dot(own_scores[...], x_strip(own))
        )
        upper, lower = scores[0:pack], scores[pack : 2 * pack]
        first = jnp.where(left, upper, pltpu.roll(lower, LANES // 2, 1))
        second = jnp.where(left, pltpu.roll(upper, LANES // 2, 1), lower)
        tw_keep[d] = jnp.where(c == 0, first, second)
        tw_out[d] = jnp.where(c == 0, second, first)
        to_twin_strip(d).start()

    def pass_on(d):
        owner = strip_at(d) * step
        to_twin_strip(d).wait_recv()
        rs_out[d] = tw_keep[d] + tw_in[d]
        if d < strips - 1:
            to_owner(d, owner, chip).start()
        elif step > 1:

            @pl.when(owner != chip)
            def _():
                to_owner(d, owner, chip).start()

    own_scores = own_head_ref

    def x_strip(own):
        return x_ref[:, own] if rows == LANES else wide[:, own].astype(jnp.bfloat16)

    for d in range(strips):
        activate(d)
        if d > 0:
            pass_on(d - 1)
    pass_on(strips - 1)

    def to_all(r):
        return pltpu.make_async_remote_copy(
            src_ref=packs.at[base, c], dst_ref=packs.at[base, c],
            send_sem=lg_sem.at[0, r], recv_sem=lg_sem.at[1, base],
            device_id={"ch": lax.rem(chip + r, m) * 2 + c},
        )

    def from_owner(j):
        return pltpu.make_async_remote_copy(
            src_ref=packs.at[j, c], dst_ref=packs.at[j, c],
            send_sem=lg_sem.at[0, 0], recv_sem=lg_sem.at[1, j],
            device_id={"ch": twin},
        )

    def forward(j, core):
        return pltpu.make_async_remote_copy(
            src_ref=packs.at[j, core], dst_ref=packs.at[j, core],
            send_sem=f_sem.at[0, j], recv_sem=f_sem.at[1, j],
            device_id={"ch": twin},
        )

    def own_strip():
        whole = rs_out[strips - 1]
        for r in range(1, m):
            source = lax.rem(chip + r, m)
            to_owner(0, 0, source).wait_recv()
            whole = whole + slots[source]
        row = lax.broadcasted_iota(jnp.int32, (pack, LANES), 0)
        kind = row + jnp.where(left, 0, pack)
        scores = jnp.where(kind < class_count, whole, -jnp.inf)
        label = jnp.broadcast_to(labels_ref[pl.ds(base, 1), :], (SUB, LANES))
        moved = pltpu.roll(label, LANES // 2, 1)
        label = jnp.where(left[0:SUB] == (c == 0), label, moved)[0:1]

        def both(value, join):
            value = jnp.broadcast_to(value, (SUB, LANES))
            return join(value, pltpu.roll(value, LANES // 2, 1))[0:1]

        row_max = both(jnp.max(scores, axis=0, keepdims=True), jnp.maximum)
        terms = jnp.exp(scores - row_max)
        exp_total = both(jnp.sum(terms, axis=0, keepdims=True), jnp.add)
        hit = kind == label
        picked = both(
            jnp.sum(jnp.where(hit, whole, 0.0), axis=0, keepdims=True), jnp.add
        )
        loss = jnp.log(exp_total) + row_max - picked
        grads = terms / exp_total - hit.astype(f32)
        packs[base, c, 0:pack] = grads.astype(jnp.bfloat16)
        packs[base, c, pack : pack + 16] = stack_rows(three_parts(loss), 16, LANES)
        for r in range(1, m):
            to_all(r).start()
        forward(base, c).start()

    if step > 1:
        pl.when(base * step == chip)(own_strip)
    else:
        own_strip()

    loss_ref[...] = jnp.zeros_like(loss_ref)

    def receive(d):
        j = strip_at(d)
        if d < strips - 1:
            from_owner(j).wait_recv()
            forward(j, c).start()
        elif step > 1:

            @pl.when(base * step != chip)
            def _():
                from_owner(j).wait_recv()
                forward(j, c).start()

    def go_back(d):
        j = strip_at(d)
        own = lanes_of(j)
        forward(j, 1 - c).wait_recv()
        first, second = packs[j, 0].astype(f32), packs[j, 1].astype(f32)
        loss = jnp.where(left[0:SUB], first[pack : pack + SUB], second[pack : pack + SUB])
        loss_ref[...] += jnp.sum(loss[0:3], axis=0, keepdims=True)
        first, second = first[0:pack], second[0:pack]
        upper = jnp.where(left, first, pltpu.roll(second, LANES // 2, 1))
        lower = jnp.where(left, pltpu.roll(first, LANES // 2, 1), second)
        grads = jnp.concatenate([upper, lower], axis=0).astype(jnp.bfloat16)
        lg_ref[:, own] = grads
        sum_gain, sum_both = jnp.zeros((1, LANES), f32), jnp.zeros((1, LANES), f32)
        for g in range(units // chunk):
            piece = slice(g * chunk, (g + 1) * chunk)
            value = nn_dot(mix[piece, :], grads) * slope[piece, own]
            narrow[piece, own] = value.astype(jnp.bfloat16)
            sum_gain = sum_gain + jnp.sum(gains[piece, :] * value, axis=0, keepdims=True)
            sum_both = sum_both + jnp.sum(acc[piece, own] * value, axis=0, keepdims=True)
        share = sum_both * (1.0 / channels) * token_rows[1:2, own]
        back_rows[0:1, own] = sum_gain * (1.0 / channels) - token_rows[0:1, own] * share
        back_rows[1:2, own] = share

    order_here = [strips - 1] + list(range(strips - 1))
    for i, d in enumerate(order_here):
        receive(d)
        if i > 0:
            go_back(order_here[i - 1])
    go_back(order_here[-1])

    body = strips * rows
    cuts = ((0, body // 2), (body // 2, body + classes))

    def dest(k):
        if k == a - 1:
            return z
        low = jnp.where(k < a - 1 - z, a - 1 - k, k - (a - 1 - z))
        high = jnp.where(k < z, k, a - 1 - (k - z))
        return jnp.where(2 * z < a, low, high)

    def cut(ref, h):
        return ref.at[pl.ds(cuts[h][0], cuts[h][1] - cuts[h][0])]

    def to_twin(zz, side, core, h):
        return pltpu.make_async_remote_copy(
            src_ref=cut(msg.at[index_of(zz, side, core)], h),
            dst_ref=cut(t_in.at[zz * 2 + side], h),
            send_sem=t_sem.at[0, zz * 2 + side, h],
            recv_sem=t_sem.at[1, zz * 2 + side, h],
            device_id={"ch": twin},
        )

    def to_across(k, zz, h):
        return pltpu.make_async_remote_copy(
            src_ref=cut(y_out.at[k], h),
            dst_ref=cut(y_in.at[zz], h),
            send_sem=y_sem.at[0, zz, h],
            recv_sem=y_sem.at[1, zz, h],
            device_id={"ch": across},
        )

    def along(k, zz, landing, sem, device, h):
        return pltpu.make_async_remote_copy(
            src_ref=cut(z_out.at[k], h),
            dst_ref=cut(landing.at[zz], h),
            send_sem=zs_sem.at[k, h],
            recv_sem=sem.at[zz, h],
            device_id={"ch": device},
        )

    def fill(zz, side, core, h):
        p = zz * 2 + side
        b = p * 2 + core
        count = strips // 2
        own = slice(h * count * LANES, (h + 1) * count * LANES)
        grad = nn_dot(wg_turned[p, rows_of(core, rows), :], narrow[:, own])
        term = grad - back_rows[0:1, own] - conv_all[rows_of(b, rows), own].astype(f32) * back_rows[1:2, own]
        term = term.astype(jnp.bfloat16)
        for s in range(count):
            first = (h * count + s) * rows
            msg[b, first : first + rows, :] = term[:, s * LANES : (s + 1) * LANES]

    def see():
        back = nt_dot(lg_ref[...], hidden[...]).astype(jnp.bfloat16)
        for p in range(m):
            block = nn_dot(back, w_out_ref[:, p * pair : (p + 1) * pair]).astype(jnp.bfloat16)
            for core in range(2):
                msg[p * 2 + core, body : body + classes, :] = fit(
                    block[:, core * rows : (core + 1) * rows], 1, LANES
                )

    slab = 32

    def cross(k, h):
        zz = dest(k)
        to_twin(zz, 1 - y, c, h).wait_recv()
        low, high = cuts[h]

        @pl.loop(low // slab, high // slab)
        def _(g):
            own = rows_of(g, slab)
            y_out[k, own] = (
                msg[index_of(zz, 1 - y, c), own].astype(f32)
                + t_in[zz * 2 + 1 - y, own].astype(f32)
            ).astype(jnp.bfloat16)

        to_across(k, zz, h).start()

    turns = [(k, h) for k in range(a) for h in range(2)]
    for i, (k, h) in enumerate(turns):
        fill(dest(k), 1 - y, 1 - c, h)
        if i == 1:
            see()
        to_twin(dest(k), 1 - y, 1 - c, h).start()
        fill(dest(k), 1 - y, c, h)
        if i > 0:
            cross(*turns[i - 1])
    for i, (k, h) in enumerate(turns):
        fill(dest(k), y, 1 - c, h)
        to_twin(dest(k), y, 1 - c, h).start()
        fill(dest(k), y, c, h)
        if i == 0:
            cross(*turns[-1])

    seen_narrow[...] = nt_dot(hidden[...], lg_ref[...]).astype(jnp.bfloat16)
    mean_rows = stack_rows(three_parts(token_rows[0:1, :]), 16, tokens)
    means = jnp.sum(nt_dot(narrow[...], mean_rows), axis=1, keepdims=True)

    swath = dwi_buf.shape[2]

    def store(buf, out, i, p):
        return pltpu.make_async_copy(
            buf.at[p % 2], out.at[:, pl.ds(p * swath, swath)], store_sem.at[i, p % 2]
        )

    def weights_piece(p):
        own = slice(p * swath, (p + 1) * swath)
        if p >= 2:
            store(dwi_buf, dwi_hbm, 0, p - 2).wait()
            store(dwo_buf, dwo_hbm, 1, p - 2).wait()
        dwi_buf[p % 2] = (nt_dot(narrow[...], conv_all[own, :]) - means) * gain_ref[:, own]
        store(dwi_buf, dwi_hbm, 0, p).start()
        dwo_buf[p % 2] = nn_dot(seen_narrow[...], sh_high[:, own])
        store(dwo_buf, dwo_hbm, 1, p).start()

    pieces = list(range(channels // swath))
    share = -(-len(pieces) // (2 * a - 1))

    def sum_up(zz, h):
        low, high = cuts[h]

        @pl.loop(low // slab, high // slab)
        def _(g):
            own = rows_of(g, slab)
            sums[own] = (
                msg[index_of(zz, y, c), own].astype(f32)
                + t_in[zz * 2 + y, own].astype(f32)
                + y_in[zz, own].astype(f32)
            )

    def add(landing, zz, h):
        low, high = cuts[h]

        @pl.loop(low // slab, high // slab)
        def _(g):
            own = rows_of(g, slab)
            sums[own] += landing[zz, own].astype(f32)

    for i, (k, h) in enumerate(turns):
        zz = dest(k)
        for p in pieces[i * share : (i + 1) * share]:
            weights_piece(p)
        to_twin(zz, y, c, h).wait_recv()
        to_across(k, zz, h).wait_recv()
        sum_up(zz, h)
        if k < a - 1:

            @pl.when((zz > z) & (z > 0))
            def _():
                along(k, zz, u_in, u_sem, me, h).wait_recv()
                add(u_in, zz, h)

            @pl.when((zz < z) & (z < a - 1))
            def _():
                along(k, zz, d_in, d_sem, me, h).wait_recv()
                add(d_in, zz, h)

            low, high = cuts[h]
            z_out[k, low:high] = sums[low:high].astype(jnp.bfloat16)

            @pl.when(zz > z)
            def _():
                along(k, zz, u_in, u_sem, me + 4, h).start()

            @pl.when(zz < z)
            def _():
                along(k, zz, d_in, d_sem, me - 4, h).start()

        else:

            @pl.when(z > 0)
            def _():
                along(0, z, u_in, u_sem, me, h).wait_recv()
                add(u_in, z, h)

            @pl.when(z < a - 1)
            def _():
                along(0, z, d_in, d_sem, me, h).wait_recv()
                add(d_in, z, h)

            for s in range(h * strips // 2, (h + 1) * strips // 2):
                land_ref[:, s * LANES : (s + 1) * LANES] = sums[s * rows : (s + 1) * rows, :]
    seen_ref[...] = sums[body : body + classes, :]

    for h in range(PARTS):
        for q in range(m):
            copy(3, q * 2 + c, twin, h).wait_send()
        for zz in range(a):
            copy(2, index_of(zz, y, c), across, h).wait_send()

            @pl.when((z < a - 1) & (zz <= z))
            def _():
                copy(0, index_of(zz, y, c), me + 4, h).wait_send()

            @pl.when((z > 0) & (zz >= z))
            def _():
                copy(1, index_of(zz, y, c), me - 4, h).wait_send()

    for d in range(strips):
        to_twin_strip(d).wait_send()
        if d < strips - 1:
            to_owner(d, 0, 0).wait_send()
        elif step > 1:

            @pl.when(base * step != chip)
            def _():
                to_owner(d, 0, 0).wait_send()

        forward(d, c).wait_send()

    def all_left():
        for r in range(1, m):
            to_all(r).wait_send()

    if step > 1:
        pl.when(base * step == chip)(all_left)
    else:
        all_left()
    for k, h in turns:
        zz = dest(k)
        to_twin(zz, 1 - y, 1 - c, h).wait_send()
        to_twin(zz, y, 1 - c, h).wait_send()
        to_across(k, zz, h).wait_send()
        if k < a - 1:
            along(k, zz, u_in, u_sem, me, h).wait_send()
    for p in pieces[-2:]:
        store(dwi_buf, dwi_hbm, 0, p).wait()
        store(dwo_buf, dwo_hbm, 1, p).wait()


def block(n, class_count, x, taps, gain, scale, labels, own_head, head, w_in, w_out):
    a, m = n // 4, n // 2
    rows, tokens = x.shape
    units, channels = w_in.shape
    strips = tokens // LANES
    classes = own_head.shape[0]
    pack = classes // 2
    length = strips * rows + classes
    pair = 2 * rows
    bf16, f32 = jnp.bfloat16, jnp.float32
    vmem = pl.BlockSpec(memory_space=pltpu.VMEM)
    hbm = pl.BlockSpec(memory_space=pl.ANY)
    dma = pltpu.SemaphoreType.DMA
    return pl.pallas_call(
        functools.partial(block_kernel, n, class_count),
        out_shape=(
            jax.ShapeDtypeStruct((rows, tokens), f32),
            jax.ShapeDtypeStruct((classes, LANES), f32),
            jax.ShapeDtypeStruct((classes, tokens), bf16),
            jax.ShapeDtypeStruct((1, LANES), f32),
            jax.ShapeDtypeStruct((units, channels), f32),
            jax.ShapeDtypeStruct((units, channels), f32),
        ),
        in_specs=[vmem] * 6 + [hbm] * 3,
        out_specs=(vmem,) * 4 + (hbm,) * 2,
        scratch_shapes=[
            pltpu.VMEM(head.shape, bf16),
            pltpu.VMEM(w_in.shape, bf16),
            pltpu.VMEM(w_out.shape, bf16),
            dma((3,)),
            pltpu.VMEM((WIN_H + KS - 1, PAD_W, LANES), f32),
            pltpu.VMEM((LANES, tokens), f32),
            pltpu.VMEM((KS * KS, SUB, LANES), f32),
            pltpu.VMEM((WIN_H, WIN_W, LANES), f32),
            pltpu.VMEM((n * rows, tokens), bf16),
            pltpu.VMEM((m, units, pair), bf16),
            pltpu.VMEM((m, pair, units), bf16),
            pltpu.VMEM((units, tokens), f32),
            pltpu.VMEM((units, LANES), f32),
            pltpu.VMEM((m, SUB, tokens), f32),
            pltpu.VMEM((SUB, tokens), f32),
            pltpu.VMEM((classes, channels), bf16),
            pltpu.VMEM((classes, channels), bf16),
            pltpu.VMEM((classes, units), bf16),
            pltpu.VMEM((classes, units), bf16),
            pltpu.VMEM((units, classes), bf16),
            pltpu.VMEM((units, tokens), bf16),
            pltpu.VMEM((units, tokens), f32),
            pltpu.VMEM((units, tokens), bf16),
            pltpu.VMEM((SUB, tokens), f32),
            pltpu.VMEM((units, classes), bf16),
            pltpu.VMEM((strips, pack, LANES), f32),
            pltpu.VMEM((strips, pack, LANES), f32),
            pltpu.VMEM((strips, pack, LANES), f32),
            pltpu.VMEM((strips, pack, LANES), f32),
            pltpu.VMEM((m, pack, LANES), f32),
            pltpu.VMEM((strips, 2, pack + 16, LANES), bf16),
            pltpu.VMEM((n, length, LANES), bf16),
            pltpu.VMEM((m, length, LANES), bf16),
            pltpu.VMEM((a, length, LANES), bf16),
            pltpu.VMEM((a, length, LANES), bf16),
            pltpu.VMEM((a, length, LANES), bf16),
            pltpu.VMEM((a, length, LANES), bf16),
            pltpu.VMEM((a, length, LANES), bf16),
            pltpu.VMEM((length, LANES), f32),
            pltpu.VMEM((2, units, 2 * LANES), f32),
            pltpu.VMEM((2, units, 2 * LANES), f32),
            dma((2, 2)),
            dma((4, n * PARTS)),
            dma((n * PARTS,)),
            dma((2, strips)),
            dma((2, m)),
            dma((2, m)),
            dma((2, strips)),
            dma((2, m, 2)),
            dma((2, a, 2)),
            dma((a, 2)),
            dma((a, 2)),
            dma((a, 2)),
        ],
        compiler_params=pltpu.CompilerParams(
            collective_id=0, has_side_effects=True, vmem_limit_bytes=VMEM_LIMIT
        ),
    )(x, taps, gain, scale, labels, own_head, head, w_in, w_out)


def per_device(n, features, dw_weight, norm_gain, layer_scale, w_in, w_out, w_head, labels):
    my_rows, tok_count = features.shape
    class_count = w_head.shape[1]
    classes = -(-class_count // 32) * 32
    head = w_head.T
    taps = fit(dw_weight.T, 1, LANES)
    row_offset = lax.axis_index("ch") * my_rows
    own_head = lax.dynamic_slice_in_dim(head, row_offset, my_rows, 1)
    own_head = fit(fit(own_head, 0, classes), 1, LANES)
    my_scale = fit(lax.dynamic_slice_in_dim(layer_scale, row_offset, my_rows, 0)[None, :], 1, LANES)
    conv_grad, seen, lg, loss, d_w_in, d_w_out = block(
        n, class_count, features, taps, norm_gain[None, :], layer_scale[None, :],
        labels.reshape(-1, LANES), own_head, head, w_in, w_out,
    )
    d_features, d_dw, d_scale, d_head, mean_loss, d_w_in, d_w_out = tail(
        class_count, features, fit(conv_grad, 0, LANES), taps, lg, own_head, seen, my_scale, loss, d_w_in, d_w_out
    )
    return (
        d_features, d_dw.T[:my_rows], d_scale[0, :my_rows], d_w_in, d_w_out, d_head.T[:my_rows],
        mean_loss[0],
    )


def solution(mesh):
    placed = (P("ch", "grp"), P("ch", None), P(), P(), P("ch", None), P("ch", None), P(), P("grp"))
    return jax.shard_map(
        functools.partial(per_device, mesh.shape["ch"]),
        mesh=mesh,
        in_specs=placed,
        out_specs=(
            P("ch", "grp"),
            P("ch", "grp"),
            P(("grp", "ch")),
            P(("grp", "ch"), None),
            P(("grp", "ch"), None),
            P("ch", "grp"),
            P("grp"),
        ),
        check_vma=False,
    )
```

```python
import functools
import jax
import jax.numpy as jnp
from jax import lax
from jax.experimental import pallas as pl
from jax.experimental.pallas import tpu as pltpu
from jax.sharding import PartitionSpec as P

KS = 7
WIN_H = 32
WIN_W = 32

norm_eps = 1e-06
BLOCK_LIMIT = 53 * 1024 * 1024


def place(n):
    me = lax.axis_index("ch")
    return lax.div(me, 4), lax.rem(lax.div(me, 2), 2), lax.rem(me, 2)


def index_of(z, y, c):
    return (z * 2 + y) * 2 + c


LANES = 128
MOVES = WIN_H // 8
SUB = 8
PAD_W = WIN_W + 16


def fit(value, axis, length):
    short = length - value.shape[axis]
    if short == 0:
        return value
    pads = [(0, 0)] * value.ndim
    pads[axis] = (0, short)
    return jnp.pad(value, pads)


def clear_pads(grid_ref):
    half = KS // 2
    blank = jnp.zeros((half, PAD_W, LANES), jnp.float32)
    grid_ref[0:half] = blank
    grid_ref[half + WIN_H : 2 * half + WIN_H] = blank

    @pl.loop(0, WIN_H)
    def _(h):
        edge = jnp.zeros((SUB, LANES), jnp.float32)
        grid_ref[half + h, 0:SUB, :] = edge
        grid_ref[half + h, SUB + WIN_W : PAD_W, :] = edge


def put_strip(grid_ref, strip, block):
    half = KS // 2
    turned = block.T
    for r in range(LANES // WIN_W):
        grid_ref[half + strip * (LANES // WIN_W) + r, SUB : SUB + WIN_W, :] = turned[
            r * WIN_W : (r + 1) * WIN_W
        ]


def spread_taps(taps_ref, wide_ref):
    for k in range(KS * KS):
        wide_ref[k] = jnp.broadcast_to(taps_ref[k : k + 1, :], (SUB, LANES))


ROWS_AT_ONCE = 8


def conv_piece(grid_ref, taps_ref, first, col, flip=False):
    outs = [None] * ROWS_AT_ONCE
    for j in range(KS):
        start = SUB + col + j - KS // 2
        seen = [
            grid_ref[first + r, start : start + SUB, :] for r in range(ROWS_AT_ONCE + KS - 1)
        ]
        for i in range(KS):
            k = i * KS + j
            tap = taps_ref[KS * KS - 1 - k if flip else k]
            for r in range(ROWS_AT_ONCE):
                term = tap * seen[r + i]
                outs[r] = term if outs[r] is None else outs[r] + term
    return outs


def tail_kernel(
    x_ref, grad_ref, taps_ref, lg_ref, head_ref, seen_ref, scale_ref, loss_ref, dwi_ref, dwo_ref,
    dx_ref, dtaps_ref, dscale_ref, dhead_ref, mean_ref, dwi_out, dwo_out,
    x_grid, g_grid, turned, wide, taps, sums, move_sem
):
    rows, tokens = x_ref.shape
    tall = dwi_ref.shape[0] // MOVES
    puts = [
        pltpu.make_async_copy(
            src.at[pl.ds(k * tall, tall)], dst.at[pl.ds(k * tall, tall)], move_sem.at[i, k]
        )
        for k in range(MOVES)
        for i, (src, dst) in enumerate(((dwi_ref, dwi_out), (dwo_ref, dwo_out)))
    ]
    for put in puts:
        put.start()
    mean_ref[...] = jnp.sum(loss_ref[...], axis=1, keepdims=True) * (1.0 / tokens)
    strips = tokens // LANES
    wide[...] = jnp.zeros_like(wide)
    wide[0:rows, :] = x_ref[...].astype(jnp.float32)
    spread_taps(taps_ref, taps)
    clear_pads(x_grid)
    clear_pads(g_grid)
    for s in range(strips):
        put_strip(x_grid, s, wide[:, s * LANES : (s + 1) * LANES])
        put_strip(g_grid, s, grad_ref[:, s * LANES : (s + 1) * LANES])
    sums[...] = jnp.zeros_like(sums)
    half = KS // 2

    @pl.loop(0, WIN_H // ROWS_AT_ONCE)
    def _(block):
        first = block * ROWS_AT_ONCE
        for col in range(0, WIN_W, SUB):
            outs = conv_piece(g_grid, taps, first, col, flip=True)
            for r in range(ROWS_AT_ONCE):
                turned[first + r, col : col + SUB, :] = outs[r]
            grads = [
                g_grid[first + half + r, SUB + col : SUB + col + SUB, :]
                for r in range(ROWS_AT_ONCE)
            ]
            for j in range(KS):
                start = SUB + col + j - half
                seen = [
                    x_grid[first + r, start : start + SUB, :]
                    for r in range(ROWS_AT_ONCE + KS - 1)
                ]
                for i in range(KS):
                    total = sums[i * KS + j]
                    for r in range(ROWS_AT_ONCE):
                        total = total + grads[r] * seen[r + i]
                    sums[i * KS + j] = total

    for k in range(KS * KS):
        dtaps_ref[k : k + 1, :] = jnp.sum(sums[k], axis=0, keepdims=True)

    head = head_ref[...].astype(jnp.float32).T.astype(jnp.bfloat16)
    per = LANES // WIN_W
    for s in range(strips):
        own = slice(s * LANES, (s + 1) * LANES)
        back = jnp.concatenate([turned[s * per + r] for r in range(per)], axis=0).T
        out_grad = jnp.dot(head, lg_ref[:, own], preferred_element_type=jnp.float32)
        dx_ref[:, own] = (back + out_grad)[0:rows]
    direct = lax.dot_general(
        lg_ref[...], wide[...].astype(jnp.bfloat16), (((1,), (1,)), ((), ())),
        preferred_element_type=jnp.float32,
    )
    seen = seen_ref[...]
    classes = dhead_ref.shape[0]
    dhead_ref[...] = (direct + scale_ref[...] * seen)[0:classes]
    dscale_ref[...] = jnp.sum(head_ref[...].astype(jnp.float32) * seen, axis=0, keepdims=True)
    for put in puts:
        put.wait()


def tail(classes, x, grad, taps, lg, head, seen, scale, loss, d_w_in, d_w_out):
    rows, tokens = x.shape
    vmem = pl.BlockSpec(memory_space=pltpu.VMEM)
    hbm = pl.BlockSpec(memory_space=pltpu.HBM)
    return pl.pallas_call(
        tail_kernel,
        out_shape=(
            jax.ShapeDtypeStruct((rows, tokens), jnp.float32),
            jax.ShapeDtypeStruct((KS * KS, LANES), jnp.float32),
            jax.ShapeDtypeStruct((1, LANES), jnp.float32),
            jax.ShapeDtypeStruct((classes, LANES), jnp.float32),
            jax.ShapeDtypeStruct((1, 1), jnp.float32),
            jax.ShapeDtypeStruct(d_w_in.shape, jnp.float32),
            jax.ShapeDtypeStruct(d_w_out.shape, jnp.float32),
        ),
        in_specs=[vmem] * 10,
        out_specs=(vmem,) * 5 + (hbm,) * 2,
        scratch_shapes=[
            pltpu.VMEM((WIN_H + KS - 1, PAD_W, LANES), jnp.float32),
            pltpu.VMEM((WIN_H + KS - 1, PAD_W, LANES), jnp.float32),
            pltpu.VMEM((WIN_H, WIN_W, LANES), jnp.float32),
            pltpu.VMEM((LANES, tokens), jnp.float32),
            pltpu.VMEM((KS * KS, SUB, LANES), jnp.float32),
            pltpu.VMEM((KS * KS, SUB, LANES), jnp.float32),
            pltpu.SemaphoreType.DMA((2, MOVES)),
        ],
        compiler_params=pltpu.CompilerParams(vmem_limit_bytes=32 * 1024 * 1024),
    )(x, grad, taps, lg, head, seen, scale, loss, d_w_in, d_w_out)


PARTS = 2
SQRT_HALF = 0.7071067811865476
NORMAL = 0.3989422804014327


def lanes_of(j, size=LANES):
    return pl.ds(pl.multiple_of(j * size, size), size)


def rows_of(j, size):
    return pl.ds(pl.multiple_of(j * size, size), size)


def nt_dot(lhs, rhs):
    return lax.dot_general(lhs, rhs, (((1,), (1,)), ((), ())), preferred_element_type=jnp.float32)


def nn_dot(lhs, rhs):
    return jnp.dot(lhs, rhs, preferred_element_type=jnp.float32)


def three_parts(value):
    high = value.astype(jnp.bfloat16)
    rest = value - high.astype(jnp.float32)
    middle = rest.astype(jnp.bfloat16)
    low = (rest - middle.astype(jnp.float32)).astype(jnp.bfloat16)
    return high, middle, low


def stack_rows(parts, height, width):
    row = lax.broadcasted_iota(jnp.int32, (height, width), 0)
    out = jnp.zeros((height, width), jnp.float32)
    for i, part in enumerate(parts):
        out = jnp.where(row == i, part.astype(jnp.float32), out)
    return out.astype(jnp.bfloat16)


def block_kernel(
    n, class_count,
    x_hbm, taps_hbm, gain_hbm, scale_hbm, labels_hbm, head_hbm, w_in_hbm, w_out_hbm,
    land_ref, seen_ref, lg_ref, loss_ref, own_head_ref, own_scale_ref, dwi_ref, dwo_ref,
    x_ref, taps_ref, gain_ref, scale_ref, labels_ref, head_ref, w_in_ref, w_out_ref, load_sem,
    x_grid, wide, taps, turned,
    conv_all, wg, wg_turned, acc, gains, stats, token_rows,
    sh_high, sh_low, mix_high, mix_low, mix,
    hidden, slope, narrow, back_rows, seen_narrow,
    tw_keep, tw_out, tw_in, rs_out, slots, packs,
    msg, t_in, y_out, y_in, u_in, d_in, z_out, sums,
    send_sem, recv_sem, tw_sem, rs_sem, lg_sem, f_sem,
    t_sem, y_sem, u_sem, d_sem, zs_sem,
):
    a, m = n // 4, n // 2
    rows, tokens = x_ref.shape
    units, channels = w_in_ref.shape
    strips = tokens // LANES
    classes = lg_ref.shape[0]
    pack = classes // 2
    z, y, c = place(n)
    me = index_of(z, y, c)
    chip = z * 2 + y
    twin, across = index_of(z, y, 1 - c), index_of(z, 1 - y, c)
    f32 = jnp.float32

    loads = [
        pltpu.make_async_copy(src, dst, load_sem.at[i])
        for i, (src, dst) in enumerate(
            (
                (x_hbm, x_ref), (taps_hbm, taps_ref), (w_in_hbm, w_in_ref), (gain_hbm, gain_ref),
                (head_hbm, head_ref), (w_out_hbm, w_out_ref), (scale_hbm, scale_ref),
                (labels_hbm, labels_ref),
            )
        )
    ]
    for load in loads:
        load.start()
    barrier = pltpu.get_barrier_semaphore()
    pl.semaphore_signal(barrier, inc=1, device_id={"ch": twin})
    for d in range(1, m):
        pl.semaphore_signal(barrier, inc=1, device_id={"ch": lax.rem(chip + d, m) * 2 + c})

    span = tokens // PARTS
    half = KS // 2
    per = LANES // WIN_W
    if rows < LANES:
        wide[...] = jnp.zeros_like(wide)
    clear_pads(x_grid)
    loads[0].wait()
    loads[1].wait()
    wide[0:rows, :] = x_ref[...].astype(f32)
    spread_taps(taps_ref, taps)
    for s in range(strips):
        put_strip(x_grid, s, wide[:, s * LANES : (s + 1) * LANES])

    def convolve(h):
        blocks = WIN_H // ROWS_AT_ONCE // PARTS

        @pl.loop(h * blocks, (h + 1) * blocks)
        def _(block):
            first = block * ROWS_AT_ONCE
            for col in range(0, WIN_W, SUB):
                outs = conv_piece(x_grid, taps, first, col)
                for r in range(ROWS_AT_ONCE):
                    turned[first + r, col : col + SUB, :] = outs[r]

        for s in range(h * strips // PARTS, (h + 1) * strips // PARTS):
            back = jnp.concatenate([turned[s * per + r] for r in range(per)], axis=0).T
            conv_all[rows_of(me, rows), s * LANES : (s + 1) * LANES] = back[0:rows].astype(
                jnp.bfloat16
            )

    def copy(kind, b, device, h):
        piece = conv_all.at[rows_of(b, rows), pl.ds(h * span, span)]
        return pltpu.make_async_remote_copy(
            src_ref=piece,
            dst_ref=piece,
            send_sem=send_sem.at[kind, b * PARTS + h],
            recv_sem=recv_sem.at[b * PARTS + h],
            device_id={"ch": device},
        )

    for h in range(PARTS):
        convolve(h)
        if h == 0:
            pl.semaphore_wait(barrier, m)

        @pl.when(z < a - 1)
        def _():
            copy(0, me, me + 4, h).start()

        @pl.when(z > 0)
        def _():
            copy(1, me, me - 4, h).start()

        copy(2, me, across, h).start()
        copy(3, me, twin, h).start()

    loads[2].wait()
    loads[3].wait()
    pair = 2 * rows
    gains[...] = jnp.zeros_like(gains)
    ones = jnp.ones((pair, LANES), jnp.bfloat16)
    for p in range(m):
        own = slice(p * pair, (p + 1) * pair)
        gained = w_in_ref[:, own].astype(f32) * gain_ref[:, own]
        gained_narrow = gained.astype(jnp.bfloat16)
        wg[p] = gained_narrow
        wg_turned[p] = gained.T.astype(jnp.bfloat16)
        gains[...] += nn_dot(gained_narrow, ones)

    def mix_weights():
        for load in loads[4:]:
            load.wait()
        scaled = head_ref[...].astype(f32) * scale_ref[...]
        high = scaled.astype(jnp.bfloat16)
        sh_high[...] = jnp.zeros_like(sh_high)
        sh_low[...] = jnp.zeros_like(sh_low)
        sh_high[0:class_count, :] = high
        sh_low[0:class_count, :] = (scaled - high.astype(f32)).astype(jnp.bfloat16)
        mixed = nt_dot(sh_high[...], w_out_ref[...]) + nt_dot(sh_low[...], w_out_ref[...])
        high = mixed.astype(jnp.bfloat16)
        mix_high[...] = high
        mix_low[...] = (mixed - high.astype(f32)).astype(jnp.bfloat16)
        mix[...] = nt_dot(w_out_ref[...], sh_high[...]).astype(jnp.bfloat16)
        channel = lax.broadcasted_iota(jnp.int32, (channels, LANES), 0) - me * rows
        at = lax.broadcasted_iota(jnp.int32, (channels, LANES), 1)
        chosen = ((channel == at) & (at < rows)).astype(f32).astype(jnp.bfloat16)
        own_head_ref[...] = jnp.zeros_like(own_head_ref)
        own_head_ref[0:class_count, :] = nn_dot(head_ref[...], chosen).astype(jnp.bfloat16)
        scale_rows = stack_rows(three_parts(scale_ref[...]), 16, channels)
        own_scale_ref[...] = jnp.sum(nn_dot(scale_rows, chosen), axis=0, keepdims=True)

    def absorb(p, first=False):
        for h in range(PARTS):
            copy(3, p * 2 + 1 - c, twin, h).wait_recv()

        @pl.loop(0, tokens // (2 * LANES))
        def _(g):
            own = lanes_of(g, 2 * LANES)
            block = conv_all[rows_of(p, pair), own]
            product = nn_dot(wg[p], block)
            if first:
                acc[:, own] = product
            else:
                acc[:, own] += product
            block_wide = block.astype(f32)
            whole = jnp.sum(block_wide, axis=0, keepdims=True)
            off = block_wide - whole * (1.0 / pair)
            stats[p, 0:1, own] = whole
            stats[p, 1:2, own] = jnp.sum(off * off, axis=0, keepdims=True)

    def from_line(s, h):
        below, above = me - 4 * s, me + 4 * s

        @pl.when(z >= s)
        def _():
            copy(0, below, me, h).wait_recv()

            @pl.when(z < a - 1)
            def _():
                copy(0, below, me + 4, h).start()

            copy(2, below, across, h).start()
            copy(3, below, twin, h).start()

        @pl.when(z + s < a)
        def _():
            copy(1, above, me, h).wait_recv()

            @pl.when(z > 0)
            def _():
                copy(1, above, me - 4, h).start()

            copy(2, above, across, h).start()
            copy(3, above, twin, h).start()

    def from_across(s, h):
        def take(b):
            copy(2, b, across, h).wait_recv()
            copy(3, b, twin, h).start()

        if s == 0:
            take(across)
            return

        @pl.when(z >= s)
        def _():
            take(across - 4 * s)

        @pl.when(z + s < a)
        def _():
            take(across + 4 * s)

    def absorb_at(s, side):
        if s == 0:
            absorb(z * 2 + side, first=side is y)
            return

        @pl.when(z >= s)
        def _():
            absorb((z - s) * 2 + side)

        @pl.when(z + s < a)
        def _():
            absorb((z + s) * 2 + side)

    mingle = a <= 4
    for s in range(1, a):
        for h in range(PARTS):
            from_line(s, h)
            from_across(s - 1, h)
        if mingle:
            if s == 1:
                mix_weights()
            absorb_at(s - 1, y)
            if s > 1:
                absorb_at(s - 2, 1 - y)
    if not mingle:
        mix_weights()
    for h in range(PARTS):
        from_across(a - 1, h)
    if mingle:
        absorb_at(a - 1, y)
        if a > 1:
            absorb_at(a - 2, 1 - y)
        absorb_at(a - 1, 1 - y)
    else:
        acc[...] = jnp.zeros_like(acc)

        @pl.loop(0, m)
        def _(p):
            absorb(p)

    total = stats[0, 0:1, :]
    for p in range(1, m):
        total = total + stats[p, 0:1, :]
    tok_mean = total * (1.0 / channels)
    square = jnp.zeros_like(total)
    for p in range(m):
        off = stats[p, 0:1, :] * (1.0 / pair) - tok_mean
        square = square + stats[p, 1:2, :] + (pair * off) * off
    inv_std = 1.0 / jnp.sqrt(square * (1.0 / channels) + norm_eps)
    token_rows[0:1, :] = tok_mean
    token_rows[1:2, :] = inv_std

    step = m // strips
    base = lax.div(chip, step) if step > 1 else chip
    lane = lax.broadcasted_iota(jnp.int32, (pack, LANES), 1)
    left = lane < LANES // 2
    chunk = min(units, 64)

    def to_twin_strip(d):
        return pltpu.make_async_remote_copy(
            src_ref=tw_out.at[d], dst_ref=tw_in.at[d],
            send_sem=tw_sem.at[0, d], recv_sem=tw_sem.at[1, d], device_id={"ch": twin},
        )

    def to_owner(d, owner, source):
        return pltpu.make_async_remote_copy(
            src_ref=rs_out.at[d], dst_ref=slots.at[source],
            send_sem=rs_sem.at[0, d], recv_sem=rs_sem.at[1, source],
            device_id={"ch": owner * 2 + c},
        )

    def strip_at(d):
        return lax.rem(base + d + 1, strips)

    def activate(d):
        j = strip_at(d)
        own = lanes_of(j)
        mean_here, inv_here = token_rows[0:1, own], token_rows[1:2, own]

        @pl.loop(0, units // chunk)
        def _(g):
            piece = rows_of(g, chunk)
            pre = (acc[piece, own] - gains[piece, :] * mean_here) * inv_here
            cum_prob = 0.5 * (1.0 + lax.erf(pre * SQRT_HALF))
            density = jnp.exp(-0.5 * pre * pre) * NORMAL
            acc[piece, own] = pre
            hidden[piece, own] = (pre * cum_prob).astype(jnp.bfloat16)
            slope[piece, own] = (cum_prob + pre * density) * inv_here

        active = hidden[:, own]
        scores = (
            nn_dot(mix_high[...], active)
            + nn_dot(mix_low[...], active)
            + nn_dot(own_scores[...], x_strip(own))
        )
        upper, lower = scores[0:pack], scores[pack : 2 * pack]
        first = jnp.where(left, upper, pltpu.roll(lower, LANES // 2, 1))
        second = jnp.where(left, pltpu.roll(upper, LANES // 2, 1), lower)
        tw_keep[d] = jnp.where(c == 0, first, second)
        tw_out[d] = jnp.where(c == 0, second, first)
        to_twin_strip(d).start()

    def pass_on(d):
        owner = strip_at(d) * step
        to_twin_strip(d).wait_recv()
        rs_out[d] = tw_keep[d] + tw_in[d]
        if d < strips - 1:
            to_owner(d, owner, chip).start()
        elif step > 1:

            @pl.when(owner != chip)
            def _():
                to_owner(d, owner, chip).start()

    own_scores = own_head_ref

    def x_strip(own):
        return x_ref[:, own] if rows == LANES else wide[:, own].astype(jnp.bfloat16)

    for d in range(strips):
        activate(d)
        if d > 0:
            pass_on(d - 1)
    pass_on(strips - 1)

    def to_all(r):
        return pltpu.make_async_remote_copy(
            src_ref=packs.at[base, c], dst_ref=packs.at[base, c],
            send_sem=lg_sem.at[0, r], recv_sem=lg_sem.at[1, base],
            device_id={"ch": lax.rem(chip + r, m) * 2 + c},
        )

    def from_owner(j):
        return pltpu.make_async_remote_copy(
            src_ref=packs.at[j, c], dst_ref=packs.at[j, c],
            send_sem=lg_sem.at[0, 0], recv_sem=lg_sem.at[1, j],
            device_id={"ch": twin},
        )

    def forward(j, core):
        return pltpu.make_async_remote_copy(
            src_ref=packs.at[j, core], dst_ref=packs.at[j, core],
            send_sem=f_sem.at[0, j], recv_sem=f_sem.at[1, j],
            device_id={"ch": twin},
        )

    def own_strip():
        whole = rs_out[strips - 1]
        for r in range(1, m):
            source = lax.rem(chip + r, m)
            to_owner(0, 0, source).wait_recv()
            whole = whole + slots[source]
        row = lax.broadcasted_iota(jnp.int32, (pack, LANES), 0)
        kind = row + jnp.where(left, 0, pack)
        scores = jnp.where(kind < class_count, whole, -jnp.inf)
        label = jnp.broadcast_to(labels_ref[pl.ds(base, 1), :], (SUB, LANES))
        moved = pltpu.roll(label, LANES // 2, 1)
        label = jnp.where(left[0:SUB] == (c == 0), label, moved)[0:1]

        def both(value, join):
            value = jnp.broadcast_to(value, (SUB, LANES))
            return join(value, pltpu.roll(value, LANES // 2, 1))[0:1]

        row_max = both(jnp.max(scores, axis=0, keepdims=True), jnp.maximum)
        terms = jnp.exp(scores - row_max)
        exp_total = both(jnp.sum(terms, axis=0, keepdims=True), jnp.add)
        hit = kind == label
        picked = both(
            jnp.sum(jnp.where(hit, whole, 0.0), axis=0, keepdims=True), jnp.add
        )
        loss = jnp.log(exp_total) + row_max - picked
        grads = terms / exp_total - hit.astype(f32)
        packs[base, c, 0:pack] = grads.astype(jnp.bfloat16)
        packs[base, c, pack : pack + 16] = stack_rows(three_parts(loss), 16, LANES)
        for r in range(1, m):
            to_all(r).start()
        forward(base, c).start()

    if step > 1:
        pl.when(base * step == chip)(own_strip)
    else:
        own_strip()

    loss_ref[...] = jnp.zeros_like(loss_ref)

    def receive(d):
        j = strip_at(d)
        if d < strips - 1:
            from_owner(j).wait_recv()
            forward(j, c).start()
        elif step > 1:

            @pl.when(base * step != chip)
            def _():
                from_owner(j).wait_recv()
                forward(j, c).start()

    def go_back(d):
        j = strip_at(d)
        own = lanes_of(j)
        forward(j, 1 - c).wait_recv()
        first, second = packs[j, 0].astype(f32), packs[j, 1].astype(f32)
        loss = jnp.where(left[0:SUB], first[pack : pack + SUB], second[pack : pack + SUB])
        loss_ref[...] += jnp.sum(loss[0:3], axis=0, keepdims=True)
        first, second = first[0:pack], second[0:pack]
        upper = jnp.where(left, first, pltpu.roll(second, LANES // 2, 1))
        lower = jnp.where(left, pltpu.roll(first, LANES // 2, 1), second)
        grads = jnp.concatenate([upper, lower], axis=0).astype(jnp.bfloat16)
        lg_ref[:, own] = grads
        sum_gain, sum_both = jnp.zeros((1, LANES), f32), jnp.zeros((1, LANES), f32)
        for g in range(units // chunk):
            piece = slice(g * chunk, (g + 1) * chunk)
            value = nn_dot(mix[piece, :], grads) * slope[piece, own]
            narrow[piece, own] = value.astype(jnp.bfloat16)
            sum_gain = sum_gain + jnp.sum(gains[piece, :] * value, axis=0, keepdims=True)
            sum_both = sum_both + jnp.sum(acc[piece, own] * value, axis=0, keepdims=True)
        share = sum_both * (1.0 / channels) * token_rows[1:2, own]
        back_rows[0:1, own] = sum_gain * (1.0 / channels) - token_rows[0:1, own] * share
        back_rows[1:2, own] = share

    order_here = [strips - 1] + list(range(strips - 1))
    for i, d in enumerate(order_here):
        receive(d)
        if i > 0:
            go_back(order_here[i - 1])
    go_back(order_here[-1])

    body = strips * rows
    cuts = ((0, body // 2), (body // 2, body + classes))

    def dest(k):
        if k == a - 1:
            return z
        low = jnp.where(k < a - 1 - z, a - 1 - k, k - (a - 1 - z))
        high = jnp.where(k < z, k, a - 1 - (k - z))
        return jnp.where(2 * z < a, low, high)

    def cut(ref, h):
        return ref.at[pl.ds(cuts[h][0], cuts[h][1] - cuts[h][0])]

    def to_twin(zz, side, core, h):
        return pltpu.make_async_remote_copy(
            src_ref=cut(msg.at[index_of(zz, side, core)], h),
            dst_ref=cut(t_in.at[zz * 2 + side], h),
            send_sem=t_sem.at[0, zz * 2 + side, h],
            recv_sem=t_sem.at[1, zz * 2 + side, h],
            device_id={"ch": twin},
        )

    def to_across(k, zz, h):
        return pltpu.make_async_remote_copy(
            src_ref=cut(y_out.at[k], h),
            dst_ref=cut(y_in.at[zz], h),
            send_sem=y_sem.at[0, zz, h],
            recv_sem=y_sem.at[1, zz, h],
            device_id={"ch": across},
        )

    def along(k, zz, landing, sem, device, h):
        return pltpu.make_async_remote_copy(
            src_ref=cut(z_out.at[k], h),
            dst_ref=cut(landing.at[zz], h),
            send_sem=zs_sem.at[k, h],
            recv_sem=sem.at[zz, h],
            device_id={"ch": device},
        )

    def fill(zz, side, core, h):
        p = zz * 2 + side
        b = p * 2 + core
        count = strips // 2
        own = slice(h * count * LANES, (h + 1) * count * LANES)
        grad = nn_dot(wg_turned[p, rows_of(core, rows), :], narrow[:, own])
        term = grad - back_rows[0:1, own] - conv_all[rows_of(b, rows), own].astype(f32) * back_rows[1:2, own]
        term = term.astype(jnp.bfloat16)
        for s in range(count):
            first = (h * count + s) * rows
            msg[b, first : first + rows, :] = term[:, s * LANES : (s + 1) * LANES]

    def see():
        back = nt_dot(lg_ref[...], hidden[...]).astype(jnp.bfloat16)
        for p in range(m):
            block = nn_dot(back, w_out_ref[:, p * pair : (p + 1) * pair]).astype(jnp.bfloat16)
            for core in range(2):
                msg[p * 2 + core, body : body + classes, :] = fit(
                    block[:, core * rows : (core + 1) * rows], 1, LANES
                )

    slab = 32

    def cross(k, h):
        zz = dest(k)
        to_twin(zz, 1 - y, c, h).wait_recv()
        low, high = cuts[h]

        @pl.loop(low // slab, high // slab)
        def _(g):
            own = rows_of(g, slab)
            y_out[k, own] = (
                msg[index_of(zz, 1 - y, c), own].astype(f32)
                + t_in[zz * 2 + 1 - y, own].astype(f32)
            ).astype(jnp.bfloat16)

        to_across(k, zz, h).start()

    turns = [(k, h) for k in range(a) for h in range(2)]
    for i, (k, h) in enumerate(turns):
        fill(dest(k), 1 - y, 1 - c, h)
        if i == 1:
            see()
        to_twin(dest(k), 1 - y, 1 - c, h).start()
        fill(dest(k), 1 - y, c, h)
        if i > 0:
            cross(*turns[i - 1])
    for i, (k, h) in enumerate(turns):
        fill(dest(k), y, 1 - c, h)
        to_twin(dest(k), y, 1 - c, h).start()
        fill(dest(k), y, c, h)
        if i == 0:
            cross(*turns[-1])

    seen_narrow[...] = nt_dot(hidden[...], lg_ref[...]).astype(jnp.bfloat16)
    mean_rows = stack_rows(three_parts(token_rows[0:1, :]), 16, tokens)
    means = jnp.sum(nt_dot(narrow[...], mean_rows), axis=1, keepdims=True)

    swath = 2 * LANES

    def weights_piece(p):
        own = slice(p * swath, (p + 1) * swath)
        dwi_ref[:, own] = (nt_dot(narrow[...], conv_all[own, :]) - means) * gain_ref[:, own]
        dwo_ref[:, own] = nn_dot(seen_narrow[...], sh_high[:, own])

    pieces = list(range(channels // swath))
    share = -(-len(pieces) // (2 * a - 1))

    def sum_up(zz, h):
        low, high = cuts[h]

        @pl.loop(low // slab, high // slab)
        def _(g):
            own = rows_of(g, slab)
            sums[own] = (
                msg[index_of(zz, y, c), own].astype(f32)
                + t_in[zz * 2 + y, own].astype(f32)
                + y_in[zz, own].astype(f32)
            )

    def add(landing, zz, h):
        low, high = cuts[h]

        @pl.loop(low // slab, high // slab)
        def _(g):
            own = rows_of(g, slab)
            sums[own] += landing[zz, own].astype(f32)

    for i, (k, h) in enumerate(turns):
        zz = dest(k)
        for p in pieces[i * share : (i + 1) * share]:
            weights_piece(p)
        to_twin(zz, y, c, h).wait_recv()
        to_across(k, zz, h).wait_recv()
        sum_up(zz, h)
        if k < a - 1:

            @pl.when((zz > z) & (z > 0))
            def _():
                along(k, zz, u_in, u_sem, me, h).wait_recv()
                add(u_in, zz, h)

            @pl.when((zz < z) & (z < a - 1))
            def _():
                along(k, zz, d_in, d_sem, me, h).wait_recv()
                add(d_in, zz, h)

            low, high = cuts[h]
            z_out[k, low:high] = sums[low:high].astype(jnp.bfloat16)

            @pl.when(zz > z)
            def _():
                along(k, zz, u_in, u_sem, me + 4, h).start()

            @pl.when(zz < z)
            def _():
                along(k, zz, d_in, d_sem, me - 4, h).start()

        else:

            @pl.when(z > 0)
            def _():
                along(0, z, u_in, u_sem, me, h).wait_recv()
                add(u_in, z, h)

            @pl.when(z < a - 1)
            def _():
                along(0, z, d_in, d_sem, me, h).wait_recv()
                add(d_in, z, h)

            for s in range(h * strips // 2, (h + 1) * strips // 2):
                land_ref[:, s * LANES : (s + 1) * LANES] = sums[s * rows : (s + 1) * rows, :]
    seen_ref[...] = sums[body : body + classes, :]

    for h in range(PARTS):
        for q in range(m):
            copy(3, q * 2 + c, twin, h).wait_send()
        for zz in range(a):
            copy(2, index_of(zz, y, c), across, h).wait_send()

            @pl.when((z < a - 1) & (zz <= z))
            def _():
                copy(0, index_of(zz, y, c), me + 4, h).wait_send()

            @pl.when((z > 0) & (zz >= z))
            def _():
                copy(1, index_of(zz, y, c), me - 4, h).wait_send()

    for d in range(strips):
        to_twin_strip(d).wait_send()
        if d < strips - 1:
            to_owner(d, 0, 0).wait_send()
        elif step > 1:

            @pl.when(base * step != chip)
            def _():
                to_owner(d, 0, 0).wait_send()

        forward(d, c).wait_send()

    def all_left():
        for r in range(1, m):
            to_all(r).wait_send()

    if step > 1:
        pl.when(base * step == chip)(all_left)
    else:
        all_left()
    for k, h in turns:
        zz = dest(k)
        to_twin(zz, 1 - y, 1 - c, h).wait_send()
        to_twin(zz, y, 1 - c, h).wait_send()
        to_across(k, zz, h).wait_send()
        if k < a - 1:
            along(k, zz, u_in, u_sem, me, h).wait_send()


def block(n, class_count, x, taps, gain, scale, labels, head, w_in, w_out):
    a, m = n // 4, n // 2
    rows, tokens = x.shape
    units, channels = w_in.shape
    strips = tokens // LANES
    classes = -(-class_count // 32) * 32
    pack = classes // 2
    length = strips * rows + classes
    pair = 2 * rows
    bf16, f32 = jnp.bfloat16, jnp.float32
    vmem = pl.BlockSpec(memory_space=pltpu.VMEM)
    hbm = pl.BlockSpec(memory_space=pltpu.HBM)
    dma = pltpu.SemaphoreType.DMA
    scratch = [
        pltpu.VMEM(x.shape, x.dtype),
        pltpu.VMEM(taps.shape, taps.dtype),
        pltpu.VMEM(gain.shape, gain.dtype),
        pltpu.VMEM(scale.shape, scale.dtype),
        pltpu.VMEM(labels.shape, labels.dtype),
        pltpu.VMEM(head.shape, head.dtype),
        pltpu.VMEM(w_in.shape, w_in.dtype),
        pltpu.VMEM(w_out.shape, w_out.dtype),
        dma((8,)),
        pltpu.VMEM((WIN_H + KS - 1, PAD_W, LANES), f32),
        pltpu.VMEM((LANES, tokens), f32),
        pltpu.VMEM((KS * KS, SUB, LANES), f32),
        pltpu.VMEM((WIN_H, WIN_W, LANES), f32),
        pltpu.VMEM((n * rows, tokens), bf16),
        pltpu.VMEM((m, units, pair), bf16),
        pltpu.VMEM((m, pair, units), bf16),
        pltpu.VMEM((units, tokens), f32),
        pltpu.VMEM((units, LANES), f32),
        pltpu.VMEM((m, SUB, tokens), f32),
        pltpu.VMEM((SUB, tokens), f32),
        pltpu.VMEM((classes, channels), bf16),
        pltpu.VMEM((classes, channels), bf16),
        pltpu.VMEM((classes, units), bf16),
        pltpu.VMEM((classes, units), bf16),
        pltpu.VMEM((units, classes), bf16),
        pltpu.VMEM((units, tokens), bf16),
        pltpu.VMEM((units, tokens), f32),
        pltpu.VMEM((units, tokens), bf16),
        pltpu.VMEM((SUB, tokens), f32),
        pltpu.VMEM((units, classes), bf16),
        pltpu.VMEM((strips, pack, LANES), f32),
        pltpu.VMEM((strips, pack, LANES), f32),
        pltpu.VMEM((strips, pack, LANES), f32),
        pltpu.VMEM((strips, pack, LANES), f32),
        pltpu.VMEM((m, pack, LANES), f32),
        pltpu.VMEM((strips, 2, pack + 16, LANES), bf16),
        pltpu.VMEM((n, length, LANES), bf16),
        pltpu.VMEM((m, length, LANES), bf16),
        pltpu.VMEM((a, length, LANES), bf16),
        pltpu.VMEM((a, length, LANES), bf16),
        pltpu.VMEM((a, length, LANES), bf16),
        pltpu.VMEM((a, length, LANES), bf16),
        pltpu.VMEM((a, length, LANES), bf16),
        pltpu.VMEM((length, LANES), f32),
        dma((4, n * PARTS)),
        dma((n * PARTS,)),
        dma((2, strips)),
        dma((2, m)),
        dma((2, m)),
        dma((2, strips)),
        dma((2, m, 2)),
        dma((2, a, 2)),
        dma((a, 2)),
        dma((a, 2)),
        dma((a, 2)),
    ]
    return pl.pallas_call(
        functools.partial(block_kernel, n, class_count),
        out_shape=(
            pltpu.VMEM((rows, tokens), f32),
            pltpu.VMEM((classes, LANES), f32),
            pltpu.VMEM((classes, tokens), bf16),
            pltpu.VMEM((1, LANES), f32),
            pltpu.VMEM((classes, LANES), bf16),
            pltpu.VMEM((1, LANES), f32),
            pltpu.VMEM((units, channels), f32),
            pltpu.VMEM((units, channels), f32),
        ),
        in_specs=[hbm] * 8,
        out_specs=(vmem,) * 8,
        scratch_shapes=scratch,
        compiler_params=pltpu.CompilerParams(
            collective_id=0, has_side_effects=True,
            vmem_limit_bytes=BLOCK_LIMIT,
        ),
    )(x, taps, gain, scale, labels, head, w_in, w_out)


def per_device(n, features, dw_weight, norm_gain, layer_scale, w_in, w_out, w_head, labels):
    my_rows, tok_count = features.shape
    class_count = w_head.shape[1]
    head = w_head.T
    taps = fit(dw_weight.T, 1, LANES)
    conv_grad, seen, lg, loss, own_head, my_scale, d_w_in, d_w_out = block(
        n, class_count, features, taps, norm_gain[None, :], layer_scale[None, :],
        labels.reshape(-1, LANES), head, w_in, w_out,
    )
    d_features, d_dw, d_scale, d_head, mean_loss, d_w_in, d_w_out = tail(
        class_count, features, fit(conv_grad, 0, LANES), taps, lg, own_head, seen, my_scale, loss, d_w_in, d_w_out
    )
    return (
        d_features, d_dw.T[:my_rows], d_scale[0, :my_rows], d_w_in, d_w_out, d_head.T[:my_rows],
        mean_loss[0],
    )


def solution(mesh):
    placed = (P("ch", "grp"), P("ch", None), P(), P(), P("ch", None), P("ch", None), P(), P("grp"))
    return jax.shard_map(
        functools.partial(per_device, mesh.shape["ch"]),
        mesh=mesh,
        in_specs=placed,
        out_specs=(
            P("ch", "grp"),
            P("ch", "grp"),
            P(("grp", "ch")),
            P(("grp", "ch"), None),
            P(("grp", "ch"), None),
            P("ch", "grp"),
            P("grp"),
        ),
        check_vma=False,
    )
```

```python
import functools
import jax
import jax.numpy as jnp
from jax import lax
from jax.experimental import pallas as pl
from jax.experimental.pallas import tpu as pltpu
from jax.sharding import PartitionSpec as P

KS = 7
WIN_H = 32
WIN_W = 32

norm_eps = 1e-06
BLOCK_LIMIT = 53 * 1024 * 1024


def place(n):
    me = lax.axis_index("ch")
    return lax.div(me, 4), lax.rem(lax.div(me, 2), 2), lax.rem(me, 2)


def index_of(z, y, c):
    return (z * 2 + y) * 2 + c


LANES = 128
MOVES = WIN_H // 8
SUB = 8
PAD_W = WIN_W + 16


def fit(value, axis, length):
    short = length - value.shape[axis]
    if short == 0:
        return value
    pads = [(0, 0)] * value.ndim
    pads[axis] = (0, short)
    return jnp.pad(value, pads)


def clear_pads(grid_ref):
    half = KS // 2
    blank = jnp.zeros((half, PAD_W, LANES), jnp.float32)
    grid_ref[0:half] = blank
    grid_ref[half + WIN_H : 2 * half + WIN_H] = blank

    @pl.loop(0, WIN_H)
    def _(h):
        edge = jnp.zeros((SUB, LANES), jnp.float32)
        grid_ref[half + h, 0:SUB, :] = edge
        grid_ref[half + h, SUB + WIN_W : PAD_W, :] = edge


def put_strip(grid_ref, strip, block):
    half = KS // 2
    turned = block.T
    for r in range(LANES // WIN_W):
        grid_ref[half + strip * (LANES // WIN_W) + r, SUB : SUB + WIN_W, :] = turned[
            r * WIN_W : (r + 1) * WIN_W
        ]


def spread_taps(taps_ref, wide_ref):
    for k in range(KS * KS):
        wide_ref[k] = jnp.broadcast_to(taps_ref[k : k + 1, :], (SUB, LANES))


ROWS_AT_ONCE = 8


def conv_piece(grid_ref, taps_ref, first, col, flip=False):
    outs = [None] * ROWS_AT_ONCE
    for j in range(KS):
        start = SUB + col + j - KS // 2
        seen = [
            grid_ref[first + r, start : start + SUB, :] for r in range(ROWS_AT_ONCE + KS - 1)
        ]
        for i in range(KS):
            k = i * KS + j
            tap = taps_ref[KS * KS - 1 - k if flip else k]
            for r in range(ROWS_AT_ONCE):
                term = tap * seen[r + i]
                outs[r] = term if outs[r] is None else outs[r] + term
    return outs


def tail_kernel(
    x_ref, grad_ref, taps_ref, lg_ref, head_ref, seen_ref, scale_ref, loss_ref, dwi_ref, dwo_ref,
    dx_ref, dtaps_ref, dscale_ref, dhead_ref, mean_ref, dwi_out, dwo_out,
    x_grid, g_grid, turned, wide, taps, sums, move_sem
):
    rows, tokens = x_ref.shape
    tall = dwi_ref.shape[0] // MOVES
    puts = [
        pltpu.make_async_copy(
            src.at[pl.ds(k * tall, tall)], dst.at[pl.ds(k * tall, tall)], move_sem.at[i, k]
        )
        for k in range(MOVES)
        for i, (src, dst) in enumerate(((dwi_ref, dwi_out), (dwo_ref, dwo_out)))
    ]
    for put in puts:
        put.start()
    mean_ref[...] = jnp.sum(loss_ref[...], axis=1, keepdims=True) * (1.0 / tokens)
    strips = tokens // LANES
    wide[...] = jnp.zeros_like(wide)
    wide[0:rows, :] = x_ref[...].astype(jnp.float32)
    spread_taps(taps_ref, taps)
    clear_pads(x_grid)
    clear_pads(g_grid)
    for s in range(strips):
        put_strip(x_grid, s, wide[:, s * LANES : (s + 1) * LANES])
        put_strip(g_grid, s, grad_ref[:, s * LANES : (s + 1) * LANES])
    sums[...] = jnp.zeros_like(sums)
    half = KS // 2

    @pl.loop(0, WIN_H // ROWS_AT_ONCE)
    def _(block):
        first = block * ROWS_AT_ONCE
        for col in range(0, WIN_W, SUB):
            outs = conv_piece(g_grid, taps, first, col, flip=True)
            for r in range(ROWS_AT_ONCE):
                turned[first + r, col : col + SUB, :] = outs[r]
            grads = [
                g_grid[first + half + r, SUB + col : SUB + col + SUB, :]
                for r in range(ROWS_AT_ONCE)
            ]
            for j in range(KS):
                start = SUB + col + j - half
                seen = [
                    x_grid[first + r, start : start + SUB, :]
                    for r in range(ROWS_AT_ONCE + KS - 1)
                ]
                for i in range(KS):
                    total = sums[i * KS + j]
                    for r in range(ROWS_AT_ONCE):
                        total = total + grads[r] * seen[r + i]
                    sums[i * KS + j] = total

    for k in range(KS * KS):
        dtaps_ref[k : k + 1, :] = jnp.sum(sums[k], axis=0, keepdims=True)

    head = head_ref[...].astype(jnp.float32).T.astype(jnp.bfloat16)
    per = LANES // WIN_W
    for s in range(strips):
        own = slice(s * LANES, (s + 1) * LANES)
        back = jnp.concatenate([turned[s * per + r] for r in range(per)], axis=0).T
        out_grad = jnp.dot(head, lg_ref[:, own], preferred_element_type=jnp.float32)
        dx_ref[:, own] = (back + out_grad)[0:rows]
    direct = lax.dot_general(
        lg_ref[...], wide[...].astype(jnp.bfloat16), (((1,), (1,)), ((), ())),
        preferred_element_type=jnp.float32,
    )
    seen = seen_ref[...]
    classes = dhead_ref.shape[0]
    dhead_ref[...] = (direct + scale_ref[...] * seen)[0:classes]
    dscale_ref[...] = jnp.sum(head_ref[...].astype(jnp.float32) * seen, axis=0, keepdims=True)
    for put in puts:
        put.wait()


def tail(classes, x, grad, taps, lg, head, seen, scale, loss, d_w_in, d_w_out):
    rows, tokens = x.shape
    vmem = pl.BlockSpec(memory_space=pltpu.VMEM)
    hbm = pl.BlockSpec(memory_space=pltpu.HBM)
    return pl.pallas_call(
        tail_kernel,
        out_shape=(
            jax.ShapeDtypeStruct((rows, tokens), jnp.float32),
            jax.ShapeDtypeStruct((KS * KS, LANES), jnp.float32),
            jax.ShapeDtypeStruct((1, LANES), jnp.float32),
            jax.ShapeDtypeStruct((classes, LANES), jnp.float32),
            jax.ShapeDtypeStruct((1, 1), jnp.float32),
            jax.ShapeDtypeStruct(d_w_in.shape, jnp.float32),
            jax.ShapeDtypeStruct(d_w_out.shape, jnp.float32),
        ),
        in_specs=[vmem] * 10,
        out_specs=(vmem,) * 5 + (hbm,) * 2,
        scratch_shapes=[
            pltpu.VMEM((WIN_H + KS - 1, PAD_W, LANES), jnp.float32),
            pltpu.VMEM((WIN_H + KS - 1, PAD_W, LANES), jnp.float32),
            pltpu.VMEM((WIN_H, WIN_W, LANES), jnp.float32),
            pltpu.VMEM((LANES, tokens), jnp.float32),
            pltpu.VMEM((KS * KS, SUB, LANES), jnp.float32),
            pltpu.VMEM((KS * KS, SUB, LANES), jnp.float32),
            pltpu.SemaphoreType.DMA((2, MOVES)),
        ],
        compiler_params=pltpu.CompilerParams(vmem_limit_bytes=32 * 1024 * 1024),
    )(x, grad, taps, lg, head, seen, scale, loss, d_w_in, d_w_out)


PARTS = 2
SQRT_HALF = 0.7071067811865476
NORMAL = 0.3989422804014327


def lanes_of(j, size=LANES):
    return pl.ds(pl.multiple_of(j * size, size), size)


def rows_of(j, size):
    return pl.ds(pl.multiple_of(j * size, size), size)


def nt_dot(lhs, rhs):
    return lax.dot_general(lhs, rhs, (((1,), (1,)), ((), ())), preferred_element_type=jnp.float32)


def nn_dot(lhs, rhs):
    return jnp.dot(lhs, rhs, preferred_element_type=jnp.float32)


def three_parts(value):
    high = value.astype(jnp.bfloat16)
    rest = value - high.astype(jnp.float32)
    middle = rest.astype(jnp.bfloat16)
    low = (rest - middle.astype(jnp.float32)).astype(jnp.bfloat16)
    return high, middle, low


def stack_rows(parts, height, width):
    row = lax.broadcasted_iota(jnp.int32, (height, width), 0)
    out = jnp.zeros((height, width), jnp.float32)
    for i, part in enumerate(parts):
        out = jnp.where(row == i, part.astype(jnp.float32), out)
    return out.astype(jnp.bfloat16)


def block_kernel(
    n, class_count,
    x_hbm, taps_hbm, gain_hbm, scale_hbm, labels_hbm, head_hbm, w_in_hbm, w_out_hbm,
    land_ref, seen_ref, lg_ref, loss_ref, own_head_ref, own_scale_ref, dwi_ref, dwo_ref,
    x_ref, taps_ref, gain_ref, scale_ref, labels_ref, head_ref, w_in_ref, w_out_ref, load_sem,
    x_grid, wide, taps, turned,
    conv_all, wg, wg_turned, acc, gains, stats, token_rows,
    sh_high, sh_low, mix_high, mix_low, mix,
    hidden, slope, narrow, back_rows, seen_narrow,
    tw_keep, tw_out, tw_in, rs_out, slots, packs,
    msg, t_in, y_out, y_in, u_in, d_in, z_out, sums,
    send_sem, recv_sem, tw_sem, rs_sem, lg_sem, f_sem,
    t_sem, y_sem, u_sem, d_sem, zs_sem, m_in, m_sem,
):
    a, m = n // 4, n // 2
    rows, tokens = x_ref.shape
    units, channels = w_in_ref.shape
    strips = tokens // LANES
    classes = lg_ref.shape[0]
    pack = classes // 2
    z, y, c = place(n)
    me = index_of(z, y, c)
    chip = z * 2 + y
    twin, across = index_of(z, y, 1 - c), index_of(z, 1 - y, c)
    f32 = jnp.float32

    loads = [
        pltpu.make_async_copy(src, dst, load_sem.at[i])
        for i, (src, dst) in enumerate(
            (
                (x_hbm, x_ref), (taps_hbm, taps_ref), (w_in_hbm, w_in_ref), (gain_hbm, gain_ref),
                (head_hbm, head_ref), (w_out_hbm, w_out_ref), (scale_hbm, scale_ref),
                (labels_hbm, labels_ref),
            )
        )
    ]
    for load in loads:
        load.start()
    barrier = pltpu.get_barrier_semaphore()
    pl.semaphore_signal(barrier, inc=1, device_id={"ch": twin})
    for d in range(1, m):
        pl.semaphore_signal(barrier, inc=1, device_id={"ch": lax.rem(chip + d, m) * 2 + c})

    span = tokens // PARTS
    half = KS // 2
    per = LANES // WIN_W
    if rows < LANES:
        wide[...] = jnp.zeros_like(wide)
    clear_pads(x_grid)
    loads[0].wait()
    loads[1].wait()
    wide[0:rows, :] = x_ref[...].astype(f32)
    spread_taps(taps_ref, taps)
    for s in range(strips):
        put_strip(x_grid, s, wide[:, s * LANES : (s + 1) * LANES])

    def convolve(h):
        blocks = WIN_H // ROWS_AT_ONCE // PARTS

        @pl.loop(h * blocks, (h + 1) * blocks)
        def _(block):
            first = block * ROWS_AT_ONCE
            for col in range(0, WIN_W, SUB):
                outs = conv_piece(x_grid, taps, first, col)
                for r in range(ROWS_AT_ONCE):
                    turned[first + r, col : col + SUB, :] = outs[r]

        for s in range(h * strips // PARTS, (h + 1) * strips // PARTS):
            back = jnp.concatenate([turned[s * per + r] for r in range(per)], axis=0).T
            conv_all[rows_of(me, rows), s * LANES : (s + 1) * LANES] = back[0:rows].astype(
                jnp.bfloat16
            )

    def copy(kind, b, device, h):
        piece = conv_all.at[rows_of(b, rows), pl.ds(h * span, span)]
        return pltpu.make_async_remote_copy(
            src_ref=piece,
            dst_ref=piece,
            send_sem=send_sem.at[kind, b * PARTS + h],
            recv_sem=recv_sem.at[b * PARTS + h],
            device_id={"ch": device},
        )

    balance = a == 4
    odd = lax.rem(z, 2) == 1
    mate = jnp.where(odd, z - 1, z + 1)
    end = (z == 0) | (z == a - 1)

    def to_mate(h):
        return copy(4, across, index_of(mate, y, c), h)

    def when_by_line(own_end, h, then):
        if 2 * h >= PARTS:
            then()
        else:
            pl.when(jnp.logical_not(own_end))(then)

    def send_across(b, below, s, h):
        def go():
            copy(2, b, across, h).start()

        if not balance or s > 1:
            go()
            return
        is_mate = odd if below else jnp.logical_not(odd)
        if 2 * h >= PARTS:
            pl.when(jnp.logical_not(is_mate))(go)
        else:
            pl.when(jnp.logical_not(is_mate) | end)(go)

    for h in range(PARTS):
        convolve(h)
        if h == 0:
            pl.semaphore_wait(barrier, m)

        @pl.when(z < a - 1)
        def _():
            copy(0, me, me + 4, h).start()

        @pl.when(z > 0)
        def _():
            copy(1, me, me - 4, h).start()

        copy(2, me, across, h).start()
        copy(3, me, twin, h).start()

    loads[2].wait()
    loads[3].wait()
    pair = 2 * rows
    gains[...] = jnp.zeros_like(gains)
    ones = jnp.ones((pair, LANES), jnp.bfloat16)
    for p in range(m):
        own = slice(p * pair, (p + 1) * pair)
        gained = w_in_ref[:, own].astype(f32) * gain_ref[:, own]
        gained_narrow = gained.astype(jnp.bfloat16)
        wg[p] = gained_narrow
        wg_turned[p] = gained.T.astype(jnp.bfloat16)
        gains[...] += nn_dot(gained_narrow, ones)

    def scale_head():
        for load in loads[4:]:
            load.wait()
        scaled = head_ref[...].astype(f32) * scale_ref[...]
        high = scaled.astype(jnp.bfloat16)
        sh_high[...] = jnp.zeros_like(sh_high)
        sh_low[...] = jnp.zeros_like(sh_low)
        sh_high[0:class_count, :] = high
        sh_low[0:class_count, :] = (scaled - high.astype(f32)).astype(jnp.bfloat16)

    def mix_head():
        mixed = nt_dot(sh_high[...], w_out_ref[...]) + nt_dot(sh_low[...], w_out_ref[...])
        high = mixed.astype(jnp.bfloat16)
        mix_high[...] = high
        mix_low[...] = (mixed - high.astype(f32)).astype(jnp.bfloat16)

    def mix_back():
        mix[...] = nt_dot(w_out_ref[...], sh_high[...]).astype(jnp.bfloat16)
        channel = lax.broadcasted_iota(jnp.int32, (channels, LANES), 0) - me * rows
        at = lax.broadcasted_iota(jnp.int32, (channels, LANES), 1)
        chosen = ((channel == at) & (at < rows)).astype(f32).astype(jnp.bfloat16)
        own_head_ref[...] = jnp.zeros_like(own_head_ref)
        own_head_ref[0:class_count, :] = nn_dot(head_ref[...], chosen).astype(jnp.bfloat16)
        scale_rows = stack_rows(three_parts(scale_ref[...]), 16, channels)
        own_scale_ref[...] = jnp.sum(nn_dot(scale_rows, chosen), axis=0, keepdims=True)

    def absorb(p, first=False):
        for h in range(PARTS):
            copy(3, p * 2 + 1 - c, twin, h).wait_recv()

        @pl.loop(0, tokens // (2 * LANES))
        def _(g):
            own = lanes_of(g, 2 * LANES)
            block = conv_all[rows_of(p, pair), own]
            product = nn_dot(wg[p], block)
            if first:
                acc[:, own] = product
            else:
                acc[:, own] += product
            block_wide = block.astype(f32)
            whole = jnp.sum(block_wide, axis=0, keepdims=True)
            off = block_wide - whole * (1.0 / pair)
            stats[p, 0:1, own] = whole
            stats[p, 1:2, own] = jnp.sum(off * off, axis=0, keepdims=True)

    def from_line(s, h):
        below, above = me - 4 * s, me + 4 * s

        @pl.when(z >= s)
        def _():
            copy(0, below, me, h).wait_recv()

            @pl.when(z < a - 1)
            def _():
                copy(0, below, me + 4, h).start()

            send_across(below, True, s, h)
            copy(3, below, twin, h).start()

        @pl.when(z + s < a)
        def _():
            copy(1, above, me, h).wait_recv()

            @pl.when(z > 0)
            def _():
                copy(1, above, me - 4, h).start()

            send_across(above, False, s, h)
            copy(3, above, twin, h).start()

    def from_across(s, h):
        def take(b):
            copy(2, b, across, h).wait_recv()
            copy(3, b, twin, h).start()

        if s == 0:
            take(across)
            if balance:
                pl.when(end)(lambda: to_mate(h).start())
            return

        if balance and s == 1 and 2 * h >= PARTS:
            @pl.when(jnp.logical_not(end))
            def _():
                take(across - 4)
                take(across + 4)

            return

        @pl.when(z >= s)
        def _():
            take(across - 4 * s)

        @pl.when(z + s < a)
        def _():
            take(across + 4 * s)

    def absorb_at(s, side):
        if s == 0:
            absorb(z * 2 + side, first=side is y)
            return

        @pl.when(z >= s)
        def _():
            absorb((z - s) * 2 + side)

        @pl.when(z + s < a)
        def _():
            absorb((z + s) * 2 + side)

    def absorb_beside(inner):
        @pl.when(jnp.logical_not(end) if inner else end)
        def _():
            absorb(mate * 2 + 1 - y)
            if inner:
                absorb((2 * z - mate) * 2 + 1 - y)

    work = {
        (1, 0): [scale_head],
        (1, 1): [mix_head],
        (2, 0): [mix_back],
        (2, 1): [lambda: absorb_at(0, y), lambda: absorb_at(0, 1 - y)],
        (3, 0): [lambda: absorb_at(1, y)],
        (3, 1): [lambda: absorb_at(2, y), lambda: absorb_beside(True)],
    }
    for s in range(1, a):
        for h in range(PARTS):
            from_line(s, h)
            from_across(s - 1, h)
            if balance and s == a - 2 and 2 * h >= PARTS:
                pl.when(jnp.logical_not(end))(lambda: to_mate(h).start())
            for item in work.get((s, h), []) if balance else []:
                item()
    for h in range(PARTS):
        from_across(a - 1, h)
    if balance:

        @pl.when(end)
        def _():
            for h in range(PARTS // 2, PARTS):
                block_there = index_of(mate, 1 - y, c)
                copy(2, block_there, across, h).wait_recv()
                copy(3, block_there, twin, h).start()

        absorb_at(2, 1 - y)
        absorb_at(3, y)
        absorb_at(3, 1 - y)
        absorb_beside(False)
    else:
        scale_head()
        mix_head()
        mix_back()
        acc[...] = jnp.zeros_like(acc)

        @pl.loop(0, m)
        def _(p):
            absorb(p)

    total = stats[0, 0:1, :]
    for p in range(1, m):
        total = total + stats[p, 0:1, :]
    tok_mean = total * (1.0 / channels)
    square = jnp.zeros_like(total)
    for p in range(m):
        off = stats[p, 0:1, :] * (1.0 / pair) - tok_mean
        square = square + stats[p, 1:2, :] + (pair * off) * off
    inv_std = 1.0 / jnp.sqrt(square * (1.0 / channels) + norm_eps)
    token_rows[0:1, :] = tok_mean
    token_rows[1:2, :] = inv_std

    step = m // strips
    base = lax.div(chip, step) if step > 1 else chip
    lane = lax.broadcasted_iota(jnp.int32, (pack, LANES), 1)
    left = lane < LANES // 2
    chunk = min(units, 64)

    def to_twin_strip(d):
        return pltpu.make_async_remote_copy(
            src_ref=tw_out.at[d], dst_ref=tw_in.at[d],
            send_sem=tw_sem.at[0, d], recv_sem=tw_sem.at[1, d], device_id={"ch": twin},
        )

    def to_owner(d, owner, source):
        return pltpu.make_async_remote_copy(
            src_ref=rs_out.at[d], dst_ref=slots.at[source],
            send_sem=rs_sem.at[0, d], recv_sem=rs_sem.at[1, source],
            device_id={"ch": owner * 2 + c},
        )

    def strip_at(d):
        return lax.rem(base + d + 1, strips)

    def activate(d):
        j = strip_at(d)
        own = lanes_of(j)
        mean_here, inv_here = token_rows[0:1, own], token_rows[1:2, own]

        @pl.loop(0, units // chunk)
        def _(g):
            piece = rows_of(g, chunk)
            pre = (acc[piece, own] - gains[piece, :] * mean_here) * inv_here
            cum_prob = 0.5 * (1.0 + lax.erf(pre * SQRT_HALF))
            density = jnp.exp(-0.5 * pre * pre) * NORMAL
            acc[piece, own] = pre
            hidden[piece, own] = (pre * cum_prob).astype(jnp.bfloat16)
            slope[piece, own] = (cum_prob + pre * density) * inv_here

        active = hidden[:, own]
        scores = (
            nn_dot(mix_high[...], active)
            + nn_dot(mix_low[...], active)
            + nn_dot(own_scores[...], x_strip(own))
        )
        upper, lower = scores[0:pack], scores[pack : 2 * pack]
        first = jnp.where(left, upper, pltpu.roll(lower, LANES // 2, 1))
        second = jnp.where(left, pltpu.roll(upper, LANES // 2, 1), lower)
        tw_keep[d] = jnp.where(c == 0, first, second)
        tw_out[d] = jnp.where(c == 0, second, first)
        to_twin_strip(d).start()

    def pass_on(d):
        owner = strip_at(d) * step
        to_twin_strip(d).wait_recv()
        rs_out[d] = tw_keep[d] + tw_in[d]
        if d < strips - 1:
            to_owner(d, owner, chip).start()
        elif step > 1:

            @pl.when(owner != chip)
            def _():
                to_owner(d, owner, chip).start()

    own_scores = own_head_ref

    def x_strip(own):
        return x_ref[:, own] if rows == LANES else wide[:, own].astype(jnp.bfloat16)

    for d in range(strips):
        activate(d)
        if d > 0:
            pass_on(d - 1)
    pass_on(strips - 1)

    def to_all(r):
        return pltpu.make_async_remote_copy(
            src_ref=packs.at[base, c], dst_ref=packs.at[base, c],
            send_sem=lg_sem.at[0, r], recv_sem=lg_sem.at[1, base],
            device_id={"ch": lax.rem(chip + r, m) * 2 + c},
        )

    def from_owner(j):
        return pltpu.make_async_remote_copy(
            src_ref=packs.at[j, c], dst_ref=packs.at[j, c],
            send_sem=lg_sem.at[0, 0], recv_sem=lg_sem.at[1, j],
            device_id={"ch": twin},
        )

    def forward(j, core):
        return pltpu.make_async_remote_copy(
            src_ref=packs.at[j, core], dst_ref=packs.at[j, core],
            send_sem=f_sem.at[0, j], recv_sem=f_sem.at[1, j],
            device_id={"ch": twin},
        )

    def own_strip():
        whole = rs_out[strips - 1]
        for r in range(1, m):
            source = lax.rem(chip + r, m)
            to_owner(0, 0, source).wait_recv()
            whole = whole + slots[source]
        row = lax.broadcasted_iota(jnp.int32, (pack, LANES), 0)
        kind = row + jnp.where(left, 0, pack)
        scores = jnp.where(kind < class_count, whole, -jnp.inf)
        label = jnp.broadcast_to(labels_ref[pl.ds(base, 1), :], (SUB, LANES))
        moved = pltpu.roll(label, LANES // 2, 1)
        label = jnp.where(left[0:SUB] == (c == 0), label, moved)[0:1]

        def both(value, join):
            value = jnp.broadcast_to(value, (SUB, LANES))
            return join(value, pltpu.roll(value, LANES // 2, 1))[0:1]

        row_max = both(jnp.max(scores, axis=0, keepdims=True), jnp.maximum)
        terms = jnp.exp(scores - row_max)
        exp_total = both(jnp.sum(terms, axis=0, keepdims=True), jnp.add)
        hit = kind == label
        picked = both(
            jnp.sum(jnp.where(hit, whole, 0.0), axis=0, keepdims=True), jnp.add
        )
        loss = jnp.log(exp_total) + row_max - picked
        grads = terms / exp_total - hit.astype(f32)
        packs[base, c, 0:pack] = grads.astype(jnp.bfloat16)
        packs[base, c, pack : pack + 16] = stack_rows(three_parts(loss), 16, LANES)
        for r in range(1, m):
            to_all(r).start()
        forward(base, c).start()

    if step > 1:
        pl.when(base * step == chip)(own_strip)
    else:
        own_strip()

    loss_ref[...] = jnp.zeros_like(loss_ref)

    def receive(d):
        j = strip_at(d)
        if d < strips - 1:
            from_owner(j).wait_recv()
            forward(j, c).start()
        elif step > 1:

            @pl.when(base * step != chip)
            def _():
                from_owner(j).wait_recv()
                forward(j, c).start()

    def go_back(d):
        j = strip_at(d)
        own = lanes_of(j)
        forward(j, 1 - c).wait_recv()
        first, second = packs[j, 0].astype(f32), packs[j, 1].astype(f32)
        loss = jnp.where(left[0:SUB], first[pack : pack + SUB], second[pack : pack + SUB])
        loss_ref[...] += jnp.sum(loss[0:3], axis=0, keepdims=True)
        first, second = first[0:pack], second[0:pack]
        upper = jnp.where(left, first, pltpu.roll(second, LANES // 2, 1))
        lower = jnp.where(left, pltpu.roll(first, LANES // 2, 1), second)
        grads = jnp.concatenate([upper, lower], axis=0).astype(jnp.bfloat16)
        lg_ref[:, own] = grads
        sum_gain, sum_both = jnp.zeros((1, LANES), f32), jnp.zeros((1, LANES), f32)
        for g in range(units // chunk):
            piece = slice(g * chunk, (g + 1) * chunk)
            value = nn_dot(mix[piece, :], grads) * slope[piece, own]
            narrow[piece, own] = value.astype(jnp.bfloat16)
            sum_gain = sum_gain + jnp.sum(gains[piece, :] * value, axis=0, keepdims=True)
            sum_both = sum_both + jnp.sum(acc[piece, own] * value, axis=0, keepdims=True)
        share = sum_both * (1.0 / channels) * token_rows[1:2, own]
        back_rows[0:1, own] = sum_gain * (1.0 / channels) - token_rows[0:1, own] * share
        back_rows[1:2, own] = share

    order_here = [strips - 1] + list(range(strips - 1))
    for i, d in enumerate(order_here):
        receive(d)
        if i > 0:
            go_back(order_here[i - 1])
    go_back(order_here[-1])

    body = strips * rows
    cuts = ((0, body // 2), (body // 2, body + classes))

    def dest(k):
        if k == a - 1:
            return z
        low = jnp.where(k < a - 1 - z, a - 1 - k, k - (a - 1 - z))
        high = jnp.where(k < z, k, a - 1 - (k - z))
        return jnp.where(2 * z < a, low, high)

    def cut(ref, h):
        return ref.at[pl.ds(cuts[h][0], cuts[h][1] - cuts[h][0])]

    def to_twin(zz, side, core, h):
        return pltpu.make_async_remote_copy(
            src_ref=cut(msg.at[index_of(zz, side, core)], h),
            dst_ref=cut(t_in.at[zz * 2 + side], h),
            send_sem=t_sem.at[0, zz * 2 + side, h],
            recv_sem=t_sem.at[1, zz * 2 + side, h],
            device_id={"ch": twin},
        )

    def to_across(k, zz, h):
        return pltpu.make_async_remote_copy(
            src_ref=cut(y_out.at[k], h),
            dst_ref=cut(y_in.at[zz], h),
            send_sem=y_sem.at[0, zz, h],
            recv_sem=y_sem.at[1, zz, h],
            device_id={"ch": across},
        )

    def along(k, zz, landing, sem, device, h):
        return pltpu.make_async_remote_copy(
            src_ref=cut(z_out.at[k], h),
            dst_ref=cut(landing.at[zz], h),
            send_sem=zs_sem.at[k, h],
            recv_sem=sem.at[zz, h],
            device_id={"ch": device},
        )

    def fill(zz, side, core, h):
        p = zz * 2 + side
        b = p * 2 + core
        count = strips // 2
        own = slice(h * count * LANES, (h + 1) * count * LANES)
        grad = nn_dot(wg_turned[p, rows_of(core, rows), :], narrow[:, own])
        term = grad - back_rows[0:1, own] - conv_all[rows_of(b, rows), own].astype(f32) * back_rows[1:2, own]
        term = term.astype(jnp.bfloat16)
        for s in range(count):
            first = (h * count + s) * rows
            msg[b, first : first + rows, :] = term[:, s * LANES : (s + 1) * LANES]

    def see():
        back = nt_dot(lg_ref[...], hidden[...]).astype(jnp.bfloat16)
        for p in range(m):
            block = nn_dot(back, w_out_ref[:, p * pair : (p + 1) * pair]).astype(jnp.bfloat16)
            for core in range(2):
                msg[p * 2 + core, body : body + classes, :] = fit(
                    block[:, core * rows : (core + 1) * rows], 1, LANES
                )

    slab = 32

    def sums_to_mate(h):
        return pltpu.make_async_remote_copy(
            src_ref=cut(y_out.at[a - 2], h),
            dst_ref=cut(m_in, h),
            send_sem=m_sem.at[0, h],
            recv_sem=m_sem.at[1, h],
            device_id={"ch": index_of(mate, y, c)},
        )

    def cross(k, h):
        zz = dest(k)
        to_twin(zz, 1 - y, c, h).wait_recv()
        low, high = cuts[h]

        @pl.loop(low // slab, high // slab)
        def _(g):
            own = rows_of(g, slab)
            y_out[k, own] = (
                msg[index_of(zz, 1 - y, c), own].astype(f32)
                + t_in[zz * 2 + 1 - y, own].astype(f32)
            ).astype(jnp.bfloat16)

        if not balance:
            to_across(k, zz, h).start()
            return
        if k == a - 2:
            when_by_line(end, h, lambda: sums_to_mate(h).start())
            if h == 0:
                pl.when(end)(lambda: to_across(k, zz, h).start())
            return
        if k == a - 1:

            def join():
                sums_to_mate(h).wait_recv()

                @pl.loop(low // slab, high // slab)
                def _(g):
                    own = rows_of(g, slab)
                    y_out[k, own] = (y_out[k, own].astype(f32) + m_in[own].astype(f32)).astype(
                        jnp.bfloat16
                    )

            when_by_line(jnp.logical_not(end), h, join)
        to_across(k, zz, h).start()

    turns = [(k, h) for k in range(a) for h in range(2)]
    if balance:
        crossings = [(0, 0), (2, 1), (0, 1), (2, 0), (1, 0), (1, 1), (3, 0), (3, 1)]
        late = crossings[-2:]
    else:
        crossings, late = turns, []
    ready = []
    for i, (k, h) in enumerate(crossings):
        fill(dest(k), 1 - y, 1 - c, h)
        if i == 1:
            see()
        to_twin(dest(k), 1 - y, 1 - c, h).start()
        fill(dest(k), 1 - y, c, h)
        if ready:
            cross(*ready.pop())
        if (k, h) not in late:
            ready.append((k, h))
    for i, (k, h) in enumerate(turns):
        fill(dest(k), y, 1 - c, h)
        to_twin(dest(k), y, 1 - c, h).start()
        fill(dest(k), y, c, h)
        if ready:
            cross(*ready.pop())

    seen_narrow[...] = nt_dot(hidden[...], lg_ref[...]).astype(jnp.bfloat16)
    mean_rows = stack_rows(three_parts(token_rows[0:1, :]), 16, tokens)
    means = jnp.sum(nt_dot(narrow[...], mean_rows), axis=1, keepdims=True)

    swath = 2 * LANES

    def weights_piece(p):
        own = slice(p * swath, (p + 1) * swath)
        dwi_ref[:, own] = (nt_dot(narrow[...], conv_all[own, :]) - means) * gain_ref[:, own]
        dwo_ref[:, own] = nn_dot(seen_narrow[...], sh_high[:, own])

    pieces = list(range(channels // swath))
    share = -(-len(pieces) // (2 * a - 1))

    def sum_up(zz, h, with_across):
        low, high = cuts[h]

        @pl.loop(low // slab, high // slab)
        def _(g):
            own = rows_of(g, slab)
            total = msg[index_of(zz, y, c), own].astype(f32) + t_in[zz * 2 + y, own].astype(f32)
            sums[own] = total + y_in[zz, own].astype(f32) if with_across else total

    def add(landing, zz, h):
        low, high = cuts[h]

        @pl.loop(low // slab, high // slab)
        def _(g):
            own = rows_of(g, slab)
            sums[own] += landing[zz, own].astype(f32)

    for i, (k, h) in enumerate(turns):
        zz = dest(k)
        for p in pieces[i * share : (i + 1) * share]:
            weights_piece(p)
        to_twin(zz, y, c, h).wait_recv()
        with_across = not (balance and k == a - 2)
        if with_across:
            to_across(k, zz, h).wait_recv()
        sum_up(zz, h, with_across)
        if not with_across and h == 0:

            @pl.when(end)
            def _():
                to_across(k, zz, h).wait_recv()
                add(y_in, zz, h)

        if k < a - 1:

            @pl.when((zz > z) & (z > 0))
            def _():
                along(k, zz, u_in, u_sem, me, h).wait_recv()
                add(u_in, zz, h)

            @pl.when((zz < z) & (z < a - 1))
            def _():
                along(k, zz, d_in, d_sem, me, h).wait_recv()
                add(d_in, zz, h)

            low, high = cuts[h]
            z_out[k, low:high] = sums[low:high].astype(jnp.bfloat16)

            @pl.when(zz > z)
            def _():
                along(k, zz, u_in, u_sem, me + 4, h).start()

            @pl.when(zz < z)
            def _():
                along(k, zz, d_in, d_sem, me - 4, h).start()

        else:

            @pl.when(z > 0)
            def _():
                along(0, z, u_in, u_sem, me, h).wait_recv()
                add(u_in, z, h)

            @pl.when(z < a - 1)
            def _():
                along(0, z, d_in, d_sem, me, h).wait_recv()
                add(d_in, z, h)

            for s in range(h * strips // 2, (h + 1) * strips // 2):
                land_ref[:, s * LANES : (s + 1) * LANES] = sums[s * rows : (s + 1) * rows, :]
        if i == 1:
            for crossing in late:
                cross(*crossing)
    seen_ref[...] = sums[body : body + classes, :]

    for h in range(PARTS):
        for q in range(m):
            copy(3, q * 2 + c, twin, h).wait_send()
        if balance:
            when_by_line(jnp.logical_not(end), h, lambda: to_mate(h).wait_send())
        for zz in range(a):
            if balance:
                crossed = (zz != mate) if 2 * h >= PARTS else ((zz != mate) | end)

                @pl.when(crossed)
                def _():
                    copy(2, index_of(zz, y, c), across, h).wait_send()

            else:
                copy(2, index_of(zz, y, c), across, h).wait_send()

            @pl.when((z < a - 1) & (zz <= z))
            def _():
                copy(0, index_of(zz, y, c), me + 4, h).wait_send()

            @pl.when((z > 0) & (zz >= z))
            def _():
                copy(1, index_of(zz, y, c), me - 4, h).wait_send()

    for d in range(strips):
        to_twin_strip(d).wait_send()
        if d < strips - 1:
            to_owner(d, 0, 0).wait_send()
        elif step > 1:

            @pl.when(base * step != chip)
            def _():
                to_owner(d, 0, 0).wait_send()

        forward(d, c).wait_send()

    def all_left():
        for r in range(1, m):
            to_all(r).wait_send()

    if step > 1:
        pl.when(base * step == chip)(all_left)
    else:
        all_left()
    for k, h in turns:
        zz = dest(k)
        to_twin(zz, 1 - y, 1 - c, h).wait_send()
        to_twin(zz, y, 1 - c, h).wait_send()
        if balance and k == a - 2:
            when_by_line(end, h, lambda: sums_to_mate(h).wait_send())
            if h == 0:
                pl.when(end)(lambda: to_across(k, zz, h).wait_send())
        else:
            to_across(k, zz, h).wait_send()
        if k < a - 1:
            along(k, zz, u_in, u_sem, me, h).wait_send()


def block(n, class_count, x, taps, gain, scale, labels, head, w_in, w_out):
    a, m = n // 4, n // 2
    rows, tokens = x.shape
    units, channels = w_in.shape
    strips = tokens // LANES
    classes = -(-class_count // 32) * 32
    pack = classes // 2
    length = strips * rows + classes
    pair = 2 * rows
    bf16, f32 = jnp.bfloat16, jnp.float32
    vmem = pl.BlockSpec(memory_space=pltpu.VMEM)
    hbm = pl.BlockSpec(memory_space=pltpu.HBM)
    dma = pltpu.SemaphoreType.DMA
    scratch = [
        pltpu.VMEM(x.shape, x.dtype),
        pltpu.VMEM(taps.shape, taps.dtype),
        pltpu.VMEM(gain.shape, gain.dtype),
        pltpu.VMEM(scale.shape, scale.dtype),
        pltpu.VMEM(labels.shape, labels.dtype),
        pltpu.VMEM(head.shape, head.dtype),
        pltpu.VMEM(w_in.shape, w_in.dtype),
        pltpu.VMEM(w_out.shape, w_out.dtype),
        dma((8,)),
        pltpu.VMEM((WIN_H + KS - 1, PAD_W, LANES), f32),
        pltpu.VMEM((LANES, tokens), f32),
        pltpu.VMEM((KS * KS, SUB, LANES), f32),
        pltpu.VMEM((WIN_H, WIN_W, LANES), f32),
        pltpu.VMEM((n * rows, tokens), bf16),
        pltpu.VMEM((m, units, pair), bf16),
        pltpu.VMEM((m, pair, units), bf16),
        pltpu.VMEM((units, tokens), f32),
        pltpu.VMEM((units, LANES), f32),
        pltpu.VMEM((m, SUB, tokens), f32),
        pltpu.VMEM((SUB, tokens), f32),
        pltpu.VMEM((classes, channels), bf16),
        pltpu.VMEM((classes, channels), bf16),
        pltpu.VMEM((classes, units), bf16),
        pltpu.VMEM((classes, units), bf16),
        pltpu.VMEM((units, classes), bf16),
        pltpu.VMEM((units, tokens), bf16),
        pltpu.VMEM((units, tokens), f32),
        pltpu.VMEM((units, tokens), bf16),
        pltpu.VMEM((SUB, tokens), f32),
        pltpu.VMEM((units, classes), bf16),
        pltpu.VMEM((strips, pack, LANES), f32),
        pltpu.VMEM((strips, pack, LANES), f32),
        pltpu.VMEM((strips, pack, LANES), f32),
        pltpu.VMEM((strips, pack, LANES), f32),
        pltpu.VMEM((m, pack, LANES), f32),
        pltpu.VMEM((strips, 2, pack + 16, LANES), bf16),
        pltpu.VMEM((n, length, LANES), bf16),
        pltpu.VMEM((m, length, LANES), bf16),
        pltpu.VMEM((a, length, LANES), bf16),
        pltpu.VMEM((a, length, LANES), bf16),
        pltpu.VMEM((a, length, LANES), bf16),
        pltpu.VMEM((a, length, LANES), bf16),
        pltpu.VMEM((a, length, LANES), bf16),
        pltpu.VMEM((length, LANES), f32),
        dma((5, n * PARTS)),
        dma((n * PARTS,)),
        dma((2, strips)),
        dma((2, m)),
        dma((2, m)),
        dma((2, strips)),
        dma((2, m, 2)),
        dma((2, a, 2)),
        dma((a, 2)),
        dma((a, 2)),
        dma((a, 2)),
        pltpu.VMEM((length, LANES), bf16),
        dma((2, 2)),
    ]
    return pl.pallas_call(
        functools.partial(block_kernel, n, class_count),
        out_shape=(
            pltpu.VMEM((rows, tokens), f32),
            pltpu.VMEM((classes, LANES), f32),
            pltpu.VMEM((classes, tokens), bf16),
            pltpu.VMEM((1, LANES), f32),
            pltpu.VMEM((classes, LANES), bf16),
            pltpu.VMEM((1, LANES), f32),
            pltpu.VMEM((units, channels), f32),
            pltpu.VMEM((units, channels), f32),
        ),
        in_specs=[hbm] * 8,
        out_specs=(vmem,) * 8,
        scratch_shapes=scratch,
        compiler_params=pltpu.CompilerParams(
            collective_id=0, has_side_effects=True,
            vmem_limit_bytes=BLOCK_LIMIT,
        ),
    )(x, taps, gain, scale, labels, head, w_in, w_out)


def per_device(n, features, dw_weight, norm_gain, layer_scale, w_in, w_out, w_head, labels):
    my_rows, tok_count = features.shape
    class_count = w_head.shape[1]
    head = w_head.T
    taps = fit(dw_weight.T, 1, LANES)
    conv_grad, seen, lg, loss, own_head, my_scale, d_w_in, d_w_out = block(
        n, class_count, features, taps, norm_gain[None, :], layer_scale[None, :],
        labels.reshape(-1, LANES), head, w_in, w_out,
    )
    d_features, d_dw, d_scale, d_head, mean_loss, d_w_in, d_w_out = tail(
        class_count, features, fit(conv_grad, 0, LANES), taps, lg, own_head, seen, my_scale, loss, d_w_in, d_w_out
    )
    return (
        d_features, d_dw.T[:my_rows], d_scale[0, :my_rows], d_w_in, d_w_out, d_head.T[:my_rows],
        mean_loss[0],
    )


def solution(mesh):
    placed = (P("ch", "grp"), P("ch", None), P(), P(), P("ch", None), P("ch", None), P(), P("grp"))
    return jax.shard_map(
        functools.partial(per_device, mesh.shape["ch"]),
        mesh=mesh,
        in_specs=placed,
        out_specs=(
            P("ch", "grp"),
            P("ch", "grp"),
            P(("grp", "ch")),
            P(("grp", "ch"), None),
            P(("grp", "ch"), None),
            P("ch", "grp"),
            P("grp"),
        ),
        check_vma=False,
    )
```

```python
import functools
import jax
import jax.numpy as jnp
from jax import lax
from jax.experimental import pallas as pl
from jax.experimental.pallas import tpu as pltpu
from jax.sharding import PartitionSpec as P

KS = 7
WIN_H = 32
WIN_W = 32

norm_eps = 1e-06
BLOCK_LIMIT = 53 * 1024 * 1024


def place(n):
    me = lax.axis_index("ch")
    return lax.div(me, 4), lax.rem(lax.div(me, 2), 2), lax.rem(me, 2)


def index_of(z, y, c):
    return (z * 2 + y) * 2 + c


LANES = 128
MOVES = WIN_H // 8
SUB = 8
PAD_W = WIN_W + 16


def fit(value, axis, length):
    short = length - value.shape[axis]
    if short == 0:
        return value
    pads = [(0, 0)] * value.ndim
    pads[axis] = (0, short)
    return jnp.pad(value, pads)


def clear_pads(grid_ref):
    half = KS // 2
    blank = jnp.zeros((half, PAD_W, LANES), jnp.float32)
    grid_ref[0:half] = blank
    grid_ref[half + WIN_H : 2 * half + WIN_H] = blank

    @pl.loop(0, WIN_H)
    def _(h):
        edge = jnp.zeros((SUB, LANES), jnp.float32)
        grid_ref[half + h, 0:SUB, :] = edge
        grid_ref[half + h, SUB + WIN_W : PAD_W, :] = edge


def put_strip(grid_ref, strip, block):
    half = KS // 2
    turned = block.T
    for r in range(LANES // WIN_W):
        grid_ref[half + strip * (LANES // WIN_W) + r, SUB : SUB + WIN_W, :] = turned[
            r * WIN_W : (r + 1) * WIN_W
        ]


def spread_taps(taps_ref, wide_ref):
    for k in range(KS * KS):
        wide_ref[k] = jnp.broadcast_to(taps_ref[k : k + 1, :], (SUB, LANES))


ROWS_AT_ONCE = 8


def conv_piece(grid_ref, taps_ref, first, col, flip=False):
    outs = [None] * ROWS_AT_ONCE
    for j in range(KS):
        start = SUB + col + j - KS // 2
        seen = [
            grid_ref[first + r, start : start + SUB, :] for r in range(ROWS_AT_ONCE + KS - 1)
        ]
        for i in range(KS):
            k = i * KS + j
            tap = taps_ref[KS * KS - 1 - k if flip else k]
            for r in range(ROWS_AT_ONCE):
                term = tap * seen[r + i]
                outs[r] = term if outs[r] is None else outs[r] + term
    return outs


def tail_kernel(
    x_ref, grad_ref, taps_ref, lg_ref, head_ref, seen_ref, scale_ref, loss_ref, dwi_ref, dwo_ref,
    dx_ref, dtaps_ref, dscale_ref, dhead_ref, mean_ref, dwi_out, dwo_out,
    x_grid, g_grid, turned, wide, taps, sums, move_sem
):
    rows, tokens = x_ref.shape
    tall = dwi_ref.shape[0] // MOVES
    puts = [
        pltpu.make_async_copy(
            src.at[pl.ds(k * tall, tall)], dst.at[pl.ds(k * tall, tall)], move_sem.at[i, k]
        )
        for k in range(MOVES)
        for i, (src, dst) in enumerate(((dwi_ref, dwi_out), (dwo_ref, dwo_out)))
    ]
    for put in puts:
        put.start()
    mean_ref[...] = jnp.sum(loss_ref[...], axis=1, keepdims=True) * (1.0 / tokens)
    strips = tokens // LANES
    wide[...] = jnp.zeros_like(wide)
    wide[0:rows, :] = x_ref[...].astype(jnp.float32)
    spread_taps(taps_ref, taps)
    clear_pads(x_grid)
    clear_pads(g_grid)
    for s in range(strips):
        put_strip(x_grid, s, wide[:, s * LANES : (s + 1) * LANES])
        put_strip(g_grid, s, grad_ref[:, s * LANES : (s + 1) * LANES])
    sums[...] = jnp.zeros_like(sums)
    half = KS // 2

    @pl.loop(0, WIN_H // ROWS_AT_ONCE)
    def _(block):
        first = block * ROWS_AT_ONCE
        for col in range(0, WIN_W, SUB):
            outs = conv_piece(g_grid, taps, first, col, flip=True)
            for r in range(ROWS_AT_ONCE):
                turned[first + r, col : col + SUB, :] = outs[r]
            grads = [
                g_grid[first + half + r, SUB + col : SUB + col + SUB, :]
                for r in range(ROWS_AT_ONCE)
            ]
            for j in range(KS):
                start = SUB + col + j - half
                seen = [
                    x_grid[first + r, start : start + SUB, :]
                    for r in range(ROWS_AT_ONCE + KS - 1)
                ]
                for i in range(KS):
                    total = sums[i * KS + j]
                    for r in range(ROWS_AT_ONCE):
                        total = total + grads[r] * seen[r + i]
                    sums[i * KS + j] = total

    for k in range(KS * KS):
        dtaps_ref[k : k + 1, :] = jnp.sum(sums[k], axis=0, keepdims=True)

    head = head_ref[...].astype(jnp.float32).T.astype(jnp.bfloat16)
    per = LANES // WIN_W
    for s in range(strips):
        own = slice(s * LANES, (s + 1) * LANES)
        back = jnp.concatenate([turned[s * per + r] for r in range(per)], axis=0).T
        out_grad = jnp.dot(head, lg_ref[:, own], preferred_element_type=jnp.float32)
        dx_ref[:, own] = (back + out_grad)[0:rows]
    direct = lax.dot_general(
        lg_ref[...], wide[...].astype(jnp.bfloat16), (((1,), (1,)), ((), ())),
        preferred_element_type=jnp.float32,
    )
    seen = seen_ref[...]
    classes = dhead_ref.shape[0]
    dhead_ref[...] = (direct + scale_ref[...] * seen)[0:classes]
    dscale_ref[...] = jnp.sum(head_ref[...].astype(jnp.float32) * seen, axis=0, keepdims=True)
    for put in puts:
        put.wait()


def tail(classes, x, grad, taps, lg, head, seen, scale, loss, d_w_in, d_w_out):
    rows, tokens = x.shape
    vmem = pl.BlockSpec(memory_space=pltpu.VMEM)
    hbm = pl.BlockSpec(memory_space=pltpu.HBM)
    return pl.pallas_call(
        tail_kernel,
        out_shape=(
            jax.ShapeDtypeStruct((rows, tokens), jnp.float32),
            jax.ShapeDtypeStruct((KS * KS, LANES), jnp.float32),
            jax.ShapeDtypeStruct((1, LANES), jnp.float32),
            jax.ShapeDtypeStruct((classes, LANES), jnp.float32),
            jax.ShapeDtypeStruct((1, 1), jnp.float32),
            jax.ShapeDtypeStruct(d_w_in.shape, jnp.float32),
            jax.ShapeDtypeStruct(d_w_out.shape, jnp.float32),
        ),
        in_specs=[vmem] * 10,
        out_specs=(vmem,) * 5 + (hbm,) * 2,
        scratch_shapes=[
            pltpu.VMEM((WIN_H + KS - 1, PAD_W, LANES), jnp.float32),
            pltpu.VMEM((WIN_H + KS - 1, PAD_W, LANES), jnp.float32),
            pltpu.VMEM((WIN_H, WIN_W, LANES), jnp.float32),
            pltpu.VMEM((LANES, tokens), jnp.float32),
            pltpu.VMEM((KS * KS, SUB, LANES), jnp.float32),
            pltpu.VMEM((KS * KS, SUB, LANES), jnp.float32),
            pltpu.SemaphoreType.DMA((2, MOVES)),
        ],
        compiler_params=pltpu.CompilerParams(vmem_limit_bytes=32 * 1024 * 1024),
    )(x, grad, taps, lg, head, seen, scale, loss, d_w_in, d_w_out)


PARTS = 2
SQRT_HALF = 0.7071067811865476
NORMAL = 0.3989422804014327


def lanes_of(j, size=LANES):
    return pl.ds(pl.multiple_of(j * size, size), size)


def rows_of(j, size):
    return pl.ds(pl.multiple_of(j * size, size), size)


def nt_dot(lhs, rhs):
    return lax.dot_general(lhs, rhs, (((1,), (1,)), ((), ())), preferred_element_type=jnp.float32)


def nn_dot(lhs, rhs):
    return jnp.dot(lhs, rhs, preferred_element_type=jnp.float32)


def three_parts(value):
    high = value.astype(jnp.bfloat16)
    rest = value - high.astype(jnp.float32)
    middle = rest.astype(jnp.bfloat16)
    low = (rest - middle.astype(jnp.float32)).astype(jnp.bfloat16)
    return high, middle, low


def stack_rows(parts, height, width):
    row = lax.broadcasted_iota(jnp.int32, (height, width), 0)
    out = jnp.zeros((height, width), jnp.float32)
    for i, part in enumerate(parts):
        out = jnp.where(row == i, part.astype(jnp.float32), out)
    return out.astype(jnp.bfloat16)


def block_kernel(
    n, class_count,
    x_hbm, taps_hbm, gain_hbm, scale_hbm, labels_hbm, head_hbm, w_in_hbm, w_out_hbm,
    land_ref, seen_ref, lg_ref, loss_ref, own_head_ref, own_scale_ref, dwi_ref, dwo_ref,
    x_ref, taps_ref, gain_ref, scale_ref, labels_ref, head_ref, w_in_ref, w_out_ref, load_sem,
    x_grid, wide, taps, turned,
    conv_all, wg, wg_turned, acc, gains, stats, token_rows,
    sh_high, sh_low, mix_both, mix,
    hidden, slope, narrow, back_rows, seen_narrow,
    tw_keep, tw_out, tw_in, rs_out, slots, packs,
    msg, t_in, y_out, y_in, u_in, d_in, z_out, sums,
    send_sem, recv_sem, tw_sem, rs_sem, lg_sem, f_sem,
    t_sem, y_sem, u_sem, d_sem, zs_sem, m_in, m_sem,
):
    a, m = n // 4, n // 2
    rows, tokens = x_ref.shape
    units, channels = w_in_ref.shape
    strips = tokens // LANES
    classes = lg_ref.shape[0]
    pack = classes // 2
    z, y, c = place(n)
    me = index_of(z, y, c)
    chip = z * 2 + y
    twin, across = index_of(z, y, 1 - c), index_of(z, 1 - y, c)
    f32 = jnp.float32

    loads = [
        pltpu.make_async_copy(src, dst, load_sem.at[i])
        for i, (src, dst) in enumerate(
            (
                (x_hbm, x_ref), (taps_hbm, taps_ref), (w_in_hbm, w_in_ref), (gain_hbm, gain_ref),
                (head_hbm, head_ref), (w_out_hbm, w_out_ref), (scale_hbm, scale_ref),
                (labels_hbm, labels_ref),
            )
        )
    ]
    for load in loads:
        load.start()
    barrier = pltpu.get_barrier_semaphore()
    pl.semaphore_signal(barrier, inc=1, device_id={"ch": twin})
    for d in range(1, m):
        pl.semaphore_signal(barrier, inc=1, device_id={"ch": lax.rem(chip + d, m) * 2 + c})

    span = tokens // PARTS
    half = KS // 2
    per = LANES // WIN_W
    if rows < LANES:
        wide[...] = jnp.zeros_like(wide)
    clear_pads(x_grid)
    loads[0].wait()
    loads[1].wait()
    wide[0:rows, :] = x_ref[...].astype(f32)
    spread_taps(taps_ref, taps)
    for s in range(strips):
        put_strip(x_grid, s, wide[:, s * LANES : (s + 1) * LANES])

    def convolve(h):
        blocks = WIN_H // ROWS_AT_ONCE // PARTS

        @pl.loop(h * blocks, (h + 1) * blocks)
        def _(block):
            first = block * ROWS_AT_ONCE
            for col in range(0, WIN_W, SUB):
                outs = conv_piece(x_grid, taps, first, col)
                for r in range(ROWS_AT_ONCE):
                    turned[first + r, col : col + SUB, :] = outs[r]

        for s in range(h * strips // PARTS, (h + 1) * strips // PARTS):
            back = jnp.concatenate([turned[s * per + r] for r in range(per)], axis=0).T
            conv_all[rows_of(me, rows), s * LANES : (s + 1) * LANES] = back[0:rows].astype(
                jnp.bfloat16
            )

    def copy(kind, b, device, h):
        piece = conv_all.at[rows_of(b, rows), pl.ds(h * span, span)]
        return pltpu.make_async_remote_copy(
            src_ref=piece,
            dst_ref=piece,
            send_sem=send_sem.at[kind, b * PARTS + h],
            recv_sem=recv_sem.at[b * PARTS + h],
            device_id={"ch": device},
        )

    balance = a == 4
    odd = lax.rem(z, 2) == 1
    mate = jnp.where(odd, z - 1, z + 1)
    end = (z == 0) | (z == a - 1)

    def to_mate(h):
        return copy(4, across, index_of(mate, y, c), h)

    def when_by_line(own_end, h, then):
        if 2 * h >= PARTS:
            then()
        else:
            pl.when(jnp.logical_not(own_end))(then)

    def send_across(b, below, s, h):
        def go():
            copy(2, b, across, h).start()

        if not balance or s > 1:
            go()
            return
        is_mate = odd if below else jnp.logical_not(odd)
        if 2 * h >= PARTS:
            pl.when(jnp.logical_not(is_mate))(go)
        else:
            pl.when(jnp.logical_not(is_mate) | end)(go)

    for h in range(PARTS):
        convolve(h)
        if h == 0:
            pl.semaphore_wait(barrier, m)

        @pl.when(z < a - 1)
        def _():
            copy(0, me, me + 4, h).start()

        @pl.when(z > 0)
        def _():
            copy(1, me, me - 4, h).start()

        copy(2, me, across, h).start()
        copy(3, me, twin, h).start()

    loads[2].wait()
    loads[3].wait()
    pair = 2 * rows
    gains[...] = jnp.zeros_like(gains)
    ones = jnp.ones((pair, LANES), jnp.bfloat16)
    for p in range(m):
        own = slice(p * pair, (p + 1) * pair)
        gained = w_in_ref[:, own].astype(f32) * gain_ref[:, own]
        gained_narrow = gained.astype(jnp.bfloat16)
        wg[p] = gained_narrow
        wg_turned[p] = gained.T.astype(jnp.bfloat16)
        gains[...] += nn_dot(gained_narrow, ones)

    def scale_head():
        for load in loads[4:]:
            load.wait()
        scaled = head_ref[...].astype(f32) * scale_ref[...]
        high = scaled.astype(jnp.bfloat16)
        sh_high[...] = jnp.zeros_like(sh_high)
        sh_low[...] = jnp.zeros_like(sh_low)
        sh_high[0:class_count, :] = high
        sh_low[0:class_count, :] = (scaled - high.astype(f32)).astype(jnp.bfloat16)

    def mix_head():
        mixed = nt_dot(sh_high[...], w_out_ref[...]) + nt_dot(sh_low[...], w_out_ref[...])
        high = mixed.astype(jnp.bfloat16)
        mix_both[0:classes, :] = high
        mix_both[classes : 2 * classes, :] = (mixed - high.astype(f32)).astype(jnp.bfloat16)

    def mix_back():
        mix[...] = nt_dot(w_out_ref[...], sh_high[...]).astype(jnp.bfloat16)
        channel = lax.broadcasted_iota(jnp.int32, (channels, LANES), 0) - me * rows
        at = lax.broadcasted_iota(jnp.int32, (channels, LANES), 1)
        chosen = ((channel == at) & (at < rows)).astype(f32).astype(jnp.bfloat16)
        own_head_ref[...] = jnp.zeros_like(own_head_ref)
        own_head_ref[0:class_count, :] = nn_dot(head_ref[...], chosen).astype(jnp.bfloat16)
        scale_rows = stack_rows(three_parts(scale_ref[...]), 16, channels)
        own_scale_ref[...] = jnp.sum(nn_dot(scale_rows, chosen), axis=0, keepdims=True)

    def absorb(p, first=False):
        for h in range(PARTS):
            copy(3, p * 2 + 1 - c, twin, h).wait_recv()

        @pl.loop(0, tokens // (2 * LANES))
        def _(g):
            own = lanes_of(g, 2 * LANES)
            block = conv_all[rows_of(p, pair), own]
            product = nn_dot(wg[p], block)
            if first:
                acc[:, own] = product
            else:
                acc[:, own] += product
            block_wide = block.astype(f32)
            whole = jnp.sum(block_wide, axis=0, keepdims=True)
            off = block_wide - whole * (1.0 / pair)
            stats[p, 0:1, own] = whole
            stats[p, 1:2, own] = jnp.sum(off * off, axis=0, keepdims=True)

    def from_line(s, h):
        below, above = me - 4 * s, me + 4 * s

        @pl.when(z >= s)
        def _():
            copy(0, below, me, h).wait_recv()

            @pl.when(z < a - 1)
            def _():
                copy(0, below, me + 4, h).start()

            send_across(below, True, s, h)
            copy(3, below, twin, h).start()

        @pl.when(z + s < a)
        def _():
            copy(1, above, me, h).wait_recv()

            @pl.when(z > 0)
            def _():
                copy(1, above, me - 4, h).start()

            send_across(above, False, s, h)
            copy(3, above, twin, h).start()

    def from_across(s, h):
        def take(b):
            copy(2, b, across, h).wait_recv()
            copy(3, b, twin, h).start()

        if s == 0:
            take(across)
            if balance:
                pl.when(end)(lambda: to_mate(h).start())
            return

        if balance and s == 1 and 2 * h >= PARTS:
            @pl.when(jnp.logical_not(end))
            def _():
                take(across - 4)
                take(across + 4)

            return

        @pl.when(z >= s)
        def _():
            take(across - 4 * s)

        @pl.when(z + s < a)
        def _():
            take(across + 4 * s)

    def absorb_at(s, side):
        if s == 0:
            absorb(z * 2 + side, first=side is y)
            return

        @pl.when(z >= s)
        def _():
            absorb((z - s) * 2 + side)

        @pl.when(z + s < a)
        def _():
            absorb((z + s) * 2 + side)

    def absorb_beside(inner):
        @pl.when(jnp.logical_not(end) if inner else end)
        def _():
            absorb(mate * 2 + 1 - y)
            if inner:
                absorb((2 * z - mate) * 2 + 1 - y)

    work = {
        (1, 0): [scale_head],
        (1, 1): [mix_head],
        (2, 0): [mix_back],
        (2, 1): [lambda: absorb_at(0, y), lambda: absorb_at(0, 1 - y)],
        (3, 0): [lambda: absorb_at(1, y)],
        (3, 1): [lambda: absorb_at(2, y), lambda: absorb_beside(True)],
    }
    for s in range(1, a):
        for h in range(PARTS):
            from_line(s, h)
            from_across(s - 1, h)
            if balance and s == a - 2 and 2 * h >= PARTS:
                pl.when(jnp.logical_not(end))(lambda: to_mate(h).start())
            for item in work.get((s, h), []) if balance else []:
                item()
    for h in range(PARTS):
        from_across(a - 1, h)
    if balance:

        @pl.when(end)
        def _():
            for h in range(PARTS // 2, PARTS):
                block_there = index_of(mate, 1 - y, c)
                copy(2, block_there, across, h).wait_recv()
                copy(3, block_there, twin, h).start()

        absorb_at(2, 1 - y)
        absorb_at(3, y)
        absorb_at(3, 1 - y)
        absorb_beside(False)
    else:
        scale_head()
        mix_head()
        mix_back()
        acc[...] = jnp.zeros_like(acc)

        @pl.loop(0, m)
        def _(p):
            absorb(p)

    total = stats[0, 0:1, :]
    for p in range(1, m):
        total = total + stats[p, 0:1, :]
    tok_mean = total * (1.0 / channels)
    square = jnp.zeros_like(total)
    for p in range(m):
        off = stats[p, 0:1, :] * (1.0 / pair) - tok_mean
        square = square + stats[p, 1:2, :] + (pair * off) * off
    inv_std = 1.0 / jnp.sqrt(square * (1.0 / channels) + norm_eps)
    token_rows[0:1, :] = tok_mean
    token_rows[1:2, :] = inv_std

    step = m // strips
    base = lax.div(chip, step) if step > 1 else chip
    lane = lax.broadcasted_iota(jnp.int32, (pack, LANES), 1)
    left = lane < LANES // 2
    chunk = min(units, 64)

    def to_twin_strip(d):
        return pltpu.make_async_remote_copy(
            src_ref=tw_out.at[d], dst_ref=tw_in.at[d],
            send_sem=tw_sem.at[0, d], recv_sem=tw_sem.at[1, d], device_id={"ch": twin},
        )

    def to_owner(d, owner, source):
        return pltpu.make_async_remote_copy(
            src_ref=rs_out.at[d], dst_ref=slots.at[source],
            send_sem=rs_sem.at[0, d], recv_sem=rs_sem.at[1, source],
            device_id={"ch": owner * 2 + c},
        )

    def strip_at(d):
        both = lax.rem(lax.div(base, 2) + d // 2 + 1, strips // 2)
        side = lax.rem(base, 2)
        return 2 * both + (side if d % 2 else 1 - side)

    def activate(e):
        j = lax.rem(lax.div(base, 2) + e + 1, strips // 2)
        own = lanes_of(j, 2 * LANES)
        mean_here, inv_here = token_rows[0:1, own], token_rows[1:2, own]

        @pl.loop(0, units // chunk)
        def _(g):
            piece = rows_of(g, chunk)
            offset = jnp.concatenate([gains[piece, :]] * 2, axis=1)
            pre = (acc[piece, own] - offset * mean_here) * inv_here
            cum_prob = 0.5 * (1.0 + lax.erf(pre * SQRT_HALF))
            density = jnp.exp(-0.5 * pre * pre) * NORMAL
            acc[piece, own] = pre
            hidden[piece, own] = (pre * cum_prob).astype(jnp.bfloat16)
            slope[piece, own] = (cum_prob + pre * density) * inv_here

        scores = nn_dot(mix_both[...], hidden[:, own])
        scores = scores[0:classes] + scores[classes : 2 * classes] + nn_dot(own_scores[...], x_strip(own))
        for side in range(2):
            here = slice(side * LANES, (side + 1) * LANES)
            upper, lower = scores[0:pack, here], scores[pack : 2 * pack, here]
            first = jnp.where(left, upper, pltpu.roll(lower, LANES // 2, 1))
            second = jnp.where(left, pltpu.roll(upper, LANES // 2, 1), lower)
            d = 2 * e + jnp.where(lax.rem(base, 2) == side, 1, 0)
            tw_keep[d] = jnp.where(c == 0, first, second)
            tw_out[d] = jnp.where(c == 0, second, first)
        for d in (2 * e, 2 * e + 1):
            to_twin_strip(d).start()

    def pass_on(d):
        owner = strip_at(d) * step
        to_twin_strip(d).wait_recv()
        rs_out[d] = tw_keep[d] + tw_in[d]
        if d < strips - 1:
            to_owner(d, owner, chip).start()
        elif step > 1:

            @pl.when(owner != chip)
            def _():
                to_owner(d, owner, chip).start()

    own_scores = own_head_ref

    def x_strip(own):
        return x_ref[:, own] if rows == LANES else wide[:, own].astype(jnp.bfloat16)

    for e in range(strips // 2):
        activate(e)
        if e > 0:
            pass_on(2 * e - 2)
            pass_on(2 * e - 1)
    pass_on(strips - 2)
    pass_on(strips - 1)

    def to_all(r):
        return pltpu.make_async_remote_copy(
            src_ref=packs.at[base, c], dst_ref=packs.at[base, c],
            send_sem=lg_sem.at[0, r], recv_sem=lg_sem.at[1, base],
            device_id={"ch": lax.rem(chip + r, m) * 2 + c},
        )

    def from_owner(j):
        return pltpu.make_async_remote_copy(
            src_ref=packs.at[j, c], dst_ref=packs.at[j, c],
            send_sem=lg_sem.at[0, 0], recv_sem=lg_sem.at[1, j],
            device_id={"ch": twin},
        )

    def forward(j, core):
        return pltpu.make_async_remote_copy(
            src_ref=packs.at[j, core], dst_ref=packs.at[j, core],
            send_sem=f_sem.at[0, j], recv_sem=f_sem.at[1, j],
            device_id={"ch": twin},
        )

    def own_strip():
        whole = rs_out[strips - 1]
        for r in range(1, m):
            source = lax.rem(chip + r, m)
            to_owner(0, 0, source).wait_recv()
            whole = whole + slots[source]
        row = lax.broadcasted_iota(jnp.int32, (pack, LANES), 0)
        kind = row + jnp.where(left, 0, pack)
        scores = jnp.where(kind < class_count, whole, -jnp.inf)
        label = jnp.broadcast_to(labels_ref[pl.ds(base, 1), :], (SUB, LANES))
        moved = pltpu.roll(label, LANES // 2, 1)
        label = jnp.where(left[0:SUB] == (c == 0), label, moved)[0:1]

        def both(value, join):
            value = jnp.broadcast_to(value, (SUB, LANES))
            return join(value, pltpu.roll(value, LANES // 2, 1))[0:1]

        row_max = both(jnp.max(scores, axis=0, keepdims=True), jnp.maximum)
        terms = jnp.exp(scores - row_max)
        exp_total = both(jnp.sum(terms, axis=0, keepdims=True), jnp.add)
        hit = kind == label
        picked = both(
            jnp.sum(jnp.where(hit, whole, 0.0), axis=0, keepdims=True), jnp.add
        )
        loss = jnp.log(exp_total) + row_max - picked
        grads = terms / exp_total - hit.astype(f32)
        packs[base, c, 0:pack] = grads.astype(jnp.bfloat16)
        packs[base, c, pack : pack + 16] = stack_rows(three_parts(loss), 16, LANES)
        for r in range(1, m):
            to_all(r).start()
        forward(base, c).start()

    if step > 1:
        pl.when(base * step == chip)(own_strip)
    else:
        own_strip()

    loss_ref[...] = jnp.zeros_like(loss_ref)

    def receive(d):
        j = strip_at(d)
        if d < strips - 1:
            from_owner(j).wait_recv()
            forward(j, c).start()
        elif step > 1:

            @pl.when(base * step != chip)
            def _():
                from_owner(j).wait_recv()
                forward(j, c).start()

    def go_back(d):
        j = strip_at(d)
        own = lanes_of(j)
        forward(j, 1 - c).wait_recv()
        first, second = packs[j, 0].astype(f32), packs[j, 1].astype(f32)
        loss = jnp.where(left[0:SUB], first[pack : pack + SUB], second[pack : pack + SUB])
        loss_ref[...] += jnp.sum(loss[0:3], axis=0, keepdims=True)
        first, second = first[0:pack], second[0:pack]
        upper = jnp.where(left, first, pltpu.roll(second, LANES // 2, 1))
        lower = jnp.where(left, pltpu.roll(first, LANES // 2, 1), second)
        grads = jnp.concatenate([upper, lower], axis=0).astype(jnp.bfloat16)
        lg_ref[:, own] = grads
        sum_gain, sum_both = jnp.zeros((1, LANES), f32), jnp.zeros((1, LANES), f32)
        for g in range(units // chunk):
            piece = slice(g * chunk, (g + 1) * chunk)
            value = nn_dot(mix[piece, :], grads) * slope[piece, own]
            narrow[piece, own] = value.astype(jnp.bfloat16)
            sum_gain = sum_gain + jnp.sum(gains[piece, :] * value, axis=0, keepdims=True)
            sum_both = sum_both + jnp.sum(acc[piece, own] * value, axis=0, keepdims=True)
        share = sum_both * (1.0 / channels) * token_rows[1:2, own]
        back_rows[0:1, own] = sum_gain * (1.0 / channels) - token_rows[0:1, own] * share
        back_rows[1:2, own] = share

    order_here = [strips - 1] + list(range(strips - 1))
    for i, d in enumerate(order_here):
        receive(d)
        if i > 0:
            go_back(order_here[i - 1])
    go_back(order_here[-1])

    body = strips * rows
    cuts = ((0, body // 2), (body // 2, body + classes))

    def dest(k):
        if k == a - 1:
            return z
        low = jnp.where(k < a - 1 - z, a - 1 - k, k - (a - 1 - z))
        high = jnp.where(k < z, k, a - 1 - (k - z))
        return jnp.where(2 * z < a, low, high)

    def cut(ref, h):
        return ref.at[pl.ds(cuts[h][0], cuts[h][1] - cuts[h][0])]

    def to_twin(zz, side, core, h):
        return pltpu.make_async_remote_copy(
            src_ref=cut(msg.at[index_of(zz, side, core)], h),
            dst_ref=cut(t_in.at[zz * 2 + side], h),
            send_sem=t_sem.at[0, zz * 2 + side, h],
            recv_sem=t_sem.at[1, zz * 2 + side, h],
            device_id={"ch": twin},
        )

    def to_across(k, zz, h):
        return pltpu.make_async_remote_copy(
            src_ref=cut(y_out.at[k], h),
            dst_ref=cut(y_in.at[zz], h),
            send_sem=y_sem.at[0, zz, h],
            recv_sem=y_sem.at[1, zz, h],
            device_id={"ch": across},
        )

    def along(k, zz, landing, sem, device, h):
        return pltpu.make_async_remote_copy(
            src_ref=cut(z_out.at[k], h),
            dst_ref=cut(landing.at[zz], h),
            send_sem=zs_sem.at[k, h],
            recv_sem=sem.at[zz, h],
            device_id={"ch": device},
        )

    def fill(zz, side, core, h):
        p = zz * 2 + side
        b = p * 2 + core
        count = strips // 2
        own = slice(h * count * LANES, (h + 1) * count * LANES)
        grad = nn_dot(wg_turned[p, rows_of(core, rows), :], narrow[:, own])
        term = grad - back_rows[0:1, own] - conv_all[rows_of(b, rows), own].astype(f32) * back_rows[1:2, own]
        term = term.astype(jnp.bfloat16)
        for s in range(count):
            first = (h * count + s) * rows
            msg[b, first : first + rows, :] = term[:, s * LANES : (s + 1) * LANES]

    def see():
        back = nt_dot(lg_ref[...], hidden[...]).astype(jnp.bfloat16)
        for p in range(m):
            block = nn_dot(back, w_out_ref[:, p * pair : (p + 1) * pair]).astype(jnp.bfloat16)
            for core in range(2):
                msg[p * 2 + core, body : body + classes, :] = fit(
                    block[:, core * rows : (core + 1) * rows], 1, LANES
                )

    def slabs(h):
        low, high = cuts[h]
        slab = max(k for k in range(16, 129, 16) if (high - low) % k == 0)
        return [low + i * slab for i in range((high - low) // slab)], slab

    def sums_to_mate(h):
        return pltpu.make_async_remote_copy(
            src_ref=cut(y_out.at[a - 2], h),
            dst_ref=cut(m_in, h),
            send_sem=m_sem.at[0, h],
            recv_sem=m_sem.at[1, h],
            device_id={"ch": index_of(mate, y, c)},
        )

    def cross(k, h):
        zz = dest(k)
        to_twin(zz, 1 - y, c, h).wait_recv()
        low, high = cuts[h]

        starts, slab = slabs(h)
        for start in starts:
            own = slice(start, start + slab)
            y_out[k, own] = (
                msg[index_of(zz, 1 - y, c), own].astype(f32)
                + t_in[zz * 2 + 1 - y, own].astype(f32)
            ).astype(jnp.bfloat16)

        if not balance:
            to_across(k, zz, h).start()
            return
        if k == a - 2:
            when_by_line(end, h, lambda: sums_to_mate(h).start())
            if h == 0:
                pl.when(end)(lambda: to_across(k, zz, h).start())
            return
        if k == a - 1:

            def join():
                sums_to_mate(h).wait_recv()

                starts, slab = slabs(h)
                for start in starts:
                    own = slice(start, start + slab)
                    y_out[k, own] = (y_out[k, own].astype(f32) + m_in[own].astype(f32)).astype(
                        jnp.bfloat16
                    )

            when_by_line(jnp.logical_not(end), h, join)
        to_across(k, zz, h).start()

    turns = [(k, h) for k in range(a) for h in range(2)]
    if balance:
        crossings = [(0, 0), (2, 1), (0, 1), (2, 0), (1, 0), (1, 1), (3, 0), (3, 1)]
        late = crossings[-2:]
    else:
        crossings, late = turns, []
    ready = []
    for i, (k, h) in enumerate(crossings):
        fill(dest(k), 1 - y, 1 - c, h)
        if i == 1:
            see()
        to_twin(dest(k), 1 - y, 1 - c, h).start()
        fill(dest(k), 1 - y, c, h)
        if ready:
            cross(*ready.pop())
        if (k, h) not in late:
            ready.append((k, h))
    for i, (k, h) in enumerate(turns):
        fill(dest(k), y, 1 - c, h)
        to_twin(dest(k), y, 1 - c, h).start()
        fill(dest(k), y, c, h)
        if ready:
            cross(*ready.pop())

    seen_narrow[...] = nt_dot(hidden[...], lg_ref[...]).astype(jnp.bfloat16)
    mean_rows = stack_rows(three_parts(token_rows[0:1, :]), 16, tokens)
    means = jnp.sum(nt_dot(narrow[...], mean_rows), axis=1, keepdims=True)

    swath = 2 * LANES

    def weights_piece(p):
        own = slice(p * swath, (p + 1) * swath)
        dwi_ref[:, own] = (nt_dot(narrow[...], conv_all[own, :]) - means) * gain_ref[:, own]
        dwo_ref[:, own] = nn_dot(seen_narrow[...], sh_high[:, own])

    pieces = list(range(channels // swath))
    share = -(-len(pieces) // (2 * a - 1))

    def sum_up(zz, h, with_across):
        low, high = cuts[h]

        starts, slab = slabs(h)
        for start in starts:
            own = slice(start, start + slab)
            total = msg[index_of(zz, y, c), own].astype(f32) + t_in[zz * 2 + y, own].astype(f32)
            sums[own] = total + y_in[zz, own].astype(f32) if with_across else total

    def add(landing, zz, h):
        low, high = cuts[h]

        starts, slab = slabs(h)
        for start in starts:
            own = slice(start, start + slab)
            sums[own] += landing[zz, own].astype(f32)

    for i, (k, h) in enumerate(turns):
        zz = dest(k)
        for p in pieces[i * share : (i + 1) * share]:
            weights_piece(p)
        to_twin(zz, y, c, h).wait_recv()
        with_across = not (balance and k == a - 2)
        if with_across:
            to_across(k, zz, h).wait_recv()
        sum_up(zz, h, with_across)
        if not with_across and h == 0:

            @pl.when(end)
            def _():
                to_across(k, zz, h).wait_recv()
                add(y_in, zz, h)

        if k < a - 1:

            @pl.when((zz > z) & (z > 0))
            def _():
                along(k, zz, u_in, u_sem, me, h).wait_recv()
                add(u_in, zz, h)

            @pl.when((zz < z) & (z < a - 1))
            def _():
                along(k, zz, d_in, d_sem, me, h).wait_recv()
                add(d_in, zz, h)

            low, high = cuts[h]
            z_out[k, low:high] = sums[low:high].astype(jnp.bfloat16)

            @pl.when(zz > z)
            def _():
                along(k, zz, u_in, u_sem, me + 4, h).start()

            @pl.when(zz < z)
            def _():
                along(k, zz, d_in, d_sem, me - 4, h).start()

        else:

            @pl.when(z > 0)
            def _():
                along(0, z, u_in, u_sem, me, h).wait_recv()
                add(u_in, z, h)

            @pl.when(z < a - 1)
            def _():
                along(0, z, d_in, d_sem, me, h).wait_recv()
                add(d_in, z, h)

            for s in range(h * strips // 2, (h + 1) * strips // 2):
                land_ref[:, s * LANES : (s + 1) * LANES] = sums[s * rows : (s + 1) * rows, :]
        if i == 1:
            for crossing in late:
                cross(*crossing)
    seen_ref[...] = sums[body : body + classes, :]

    for h in range(PARTS):
        for q in range(m):
            copy(3, q * 2 + c, twin, h).wait_send()
        if balance:
            when_by_line(jnp.logical_not(end), h, lambda: to_mate(h).wait_send())
        for zz in range(a):
            if balance:
                crossed = (zz != mate) if 2 * h >= PARTS else ((zz != mate) | end)

                @pl.when(crossed)
                def _():
                    copy(2, index_of(zz, y, c), across, h).wait_send()

            else:
                copy(2, index_of(zz, y, c), across, h).wait_send()

            @pl.when((z < a - 1) & (zz <= z))
            def _():
                copy(0, index_of(zz, y, c), me + 4, h).wait_send()

            @pl.when((z > 0) & (zz >= z))
            def _():
                copy(1, index_of(zz, y, c), me - 4, h).wait_send()

    for d in range(strips):
        to_twin_strip(d).wait_send()
        if d < strips - 1:
            to_owner(d, 0, 0).wait_send()
        elif step > 1:

            @pl.when(base * step != chip)
            def _():
                to_owner(d, 0, 0).wait_send()

        forward(d, c).wait_send()

    def all_left():
        for r in range(1, m):
            to_all(r).wait_send()

    if step > 1:
        pl.when(base * step == chip)(all_left)
    else:
        all_left()
    for k, h in turns:
        zz = dest(k)
        to_twin(zz, 1 - y, 1 - c, h).wait_send()
        to_twin(zz, y, 1 - c, h).wait_send()
        if balance and k == a - 2:
            when_by_line(end, h, lambda: sums_to_mate(h).wait_send())
            if h == 0:
                pl.when(end)(lambda: to_across(k, zz, h).wait_send())
        else:
            to_across(k, zz, h).wait_send()
        if k < a - 1:
            along(k, zz, u_in, u_sem, me, h).wait_send()


def block(n, class_count, x, taps, gain, scale, labels, head, w_in, w_out):
    a, m = n // 4, n // 2
    rows, tokens = x.shape
    units, channels = w_in.shape
    strips = tokens // LANES
    classes = -(-class_count // 32) * 32
    pack = classes // 2
    length = strips * rows + classes
    pair = 2 * rows
    bf16, f32 = jnp.bfloat16, jnp.float32
    vmem = pl.BlockSpec(memory_space=pltpu.VMEM)
    hbm = pl.BlockSpec(memory_space=pltpu.HBM)
    dma = pltpu.SemaphoreType.DMA
    scratch = [
        pltpu.VMEM(x.shape, x.dtype),
        pltpu.VMEM(taps.shape, taps.dtype),
        pltpu.VMEM(gain.shape, gain.dtype),
        pltpu.VMEM(scale.shape, scale.dtype),
        pltpu.VMEM(labels.shape, labels.dtype),
        pltpu.VMEM(head.shape, head.dtype),
        pltpu.VMEM(w_in.shape, w_in.dtype),
        pltpu.VMEM(w_out.shape, w_out.dtype),
        dma((8,)),
        pltpu.VMEM((WIN_H + KS - 1, PAD_W, LANES), f32),
        pltpu.VMEM((LANES, tokens), f32),
        pltpu.VMEM((KS * KS, SUB, LANES), f32),
        pltpu.VMEM((WIN_H, WIN_W, LANES), f32),
        pltpu.VMEM((n * rows, tokens), bf16),
        pltpu.VMEM((m, units, pair), bf16),
        pltpu.VMEM((m, pair, units), bf16),
        pltpu.VMEM((units, tokens), f32),
        pltpu.VMEM((units, LANES), f32),
        pltpu.VMEM((m, SUB, tokens), f32),
        pltpu.VMEM((SUB, tokens), f32),
        pltpu.VMEM((classes, channels), bf16),
        pltpu.VMEM((classes, channels), bf16),
        pltpu.VMEM((2 * classes, units), bf16),
        pltpu.VMEM((units, classes), bf16),
        pltpu.VMEM((units, tokens), bf16),
        pltpu.VMEM((units, tokens), f32),
        pltpu.VMEM((units, tokens), bf16),
        pltpu.VMEM((SUB, tokens), f32),
        pltpu.VMEM((units, classes), bf16),
        pltpu.VMEM((strips, pack, LANES), f32),
        pltpu.VMEM((strips, pack, LANES), f32),
        pltpu.VMEM((strips, pack, LANES), f32),
        pltpu.VMEM((strips, pack, LANES), f32),
        pltpu.VMEM((m, pack, LANES), f32),
        pltpu.VMEM((strips, 2, pack + 16, LANES), bf16),
        pltpu.VMEM((n, length, LANES), bf16),
        pltpu.VMEM((m, length, LANES), bf16),
        pltpu.VMEM((a, length, LANES), bf16),
        pltpu.VMEM((a, length, LANES), bf16),
        pltpu.VMEM((a, length, LANES), bf16),
        pltpu.VMEM((a, length, LANES), bf16),
        pltpu.VMEM((a, length, LANES), bf16),
        pltpu.VMEM((length, LANES), f32),
        dma((5, n * PARTS)),
        dma((n * PARTS,)),
        dma((2, strips)),
        dma((2, m)),
        dma((2, m)),
        dma((2, strips)),
        dma((2, m, 2)),
        dma((2, a, 2)),
        dma((a, 2)),
        dma((a, 2)),
        dma((a, 2)),
        pltpu.VMEM((length, LANES), bf16),
        dma((2, 2)),
    ]
    return pl.pallas_call(
        functools.partial(block_kernel, n, class_count),
        out_shape=(
            pltpu.VMEM((rows, tokens), f32),
            pltpu.VMEM((classes, LANES), f32),
            pltpu.VMEM((classes, tokens), bf16),
            pltpu.VMEM((1, LANES), f32),
            pltpu.VMEM((classes, LANES), bf16),
            pltpu.VMEM((1, LANES), f32),
            pltpu.VMEM((units, channels), f32),
            pltpu.VMEM((units, channels), f32),
        ),
        in_specs=[hbm] * 8,
        out_specs=(vmem,) * 8,
        scratch_shapes=scratch,
        compiler_params=pltpu.CompilerParams(
            collective_id=0, has_side_effects=True,
            vmem_limit_bytes=BLOCK_LIMIT,
        ),
    )(x, taps, gain, scale, labels, head, w_in, w_out)


def per_device(n, features, dw_weight, norm_gain, layer_scale, w_in, w_out, w_head, labels):
    my_rows, tok_count = features.shape
    class_count = w_head.shape[1]
    head = w_head.T
    taps = fit(dw_weight.T, 1, LANES)
    conv_grad, seen, lg, loss, own_head, my_scale, d_w_in, d_w_out = block(
        n, class_count, features, taps, norm_gain[None, :], layer_scale[None, :],
        labels.reshape(-1, LANES), head, w_in, w_out,
    )
    d_features, d_dw, d_scale, d_head, mean_loss, d_w_in, d_w_out = tail(
        class_count, features, fit(conv_grad, 0, LANES), taps, lg, own_head, seen, my_scale, loss, d_w_in, d_w_out
    )
    return (
        d_features, d_dw.T[:my_rows], d_scale[0, :my_rows], d_w_in, d_w_out, d_head.T[:my_rows],
        mean_loss[0],
    )


def solution(mesh):
    placed = (P("ch", "grp"), P("ch", None), P(), P(), P("ch", None), P("ch", None), P(), P("grp"))
    return jax.shard_map(
        functools.partial(per_device, mesh.shape["ch"]),
        mesh=mesh,
        in_specs=placed,
        out_specs=(
            P("ch", "grp"),
            P("ch", "grp"),
            P(("grp", "ch")),
            P(("grp", "ch"), None),
            P(("grp", "ch"), None),
            P("ch", "grp"),
            P("grp"),
        ),
        check_vma=False,
    )
```

```python
import functools
import jax
import jax.numpy as jnp
from jax import lax
from jax.experimental import pallas as pl
from jax.experimental.pallas import tpu as pltpu
from jax.sharding import PartitionSpec as P

KS = 7
WIN_H = 32
WIN_W = 32

norm_eps = 1e-06
BLOCK_LIMIT = 53 * 1024 * 1024


def place(n):
    me = lax.axis_index("ch")
    return lax.div(me, 4), lax.rem(lax.div(me, 2), 2), lax.rem(me, 2)


def index_of(z, y, c):
    return (z * 2 + y) * 2 + c


LANES = 128
MOVES = WIN_H // 8
SUB = 8
PAD_W = WIN_W + 16


def fit(value, axis, length):
    short = length - value.shape[axis]
    if short == 0:
        return value
    pads = [(0, 0)] * value.ndim
    pads[axis] = (0, short)
    return jnp.pad(value, pads)


def clear_pads(grid_ref):
    half = KS // 2
    blank = jnp.zeros((half, PAD_W, LANES), jnp.float32)
    grid_ref[0:half] = blank
    grid_ref[half + WIN_H : 2 * half + WIN_H] = blank

    @pl.loop(0, WIN_H)
    def _(h):
        edge = jnp.zeros((SUB, LANES), jnp.float32)
        grid_ref[half + h, 0:SUB, :] = edge
        grid_ref[half + h, SUB + WIN_W : PAD_W, :] = edge


def put_strip(grid_ref, strip, block):
    half = KS // 2
    turned = block.T
    for r in range(LANES // WIN_W):
        grid_ref[half + strip * (LANES // WIN_W) + r, SUB : SUB + WIN_W, :] = turned[
            r * WIN_W : (r + 1) * WIN_W
        ]


def spread_taps(taps_ref, wide_ref):
    for k in range(KS * KS):
        wide_ref[k] = jnp.broadcast_to(taps_ref[k : k + 1, :], (SUB, LANES))


ROWS_AT_ONCE = 8


def conv_piece(grid_ref, taps_ref, first, col, flip=False):
    outs = [None] * ROWS_AT_ONCE
    for j in range(KS):
        start = SUB + col + j - KS // 2
        seen = [
            grid_ref[first + r, start : start + SUB, :] for r in range(ROWS_AT_ONCE + KS - 1)
        ]
        for i in range(KS):
            k = i * KS + j
            tap = taps_ref[KS * KS - 1 - k if flip else k]
            for r in range(ROWS_AT_ONCE):
                term = tap * seen[r + i]
                outs[r] = term if outs[r] is None else outs[r] + term
    return outs


def tail_kernel(
    x_ref, grad_ref, taps_ref, lg_ref, head_ref, seen_ref, scale_ref, loss_ref, dwi_ref, dwo_ref,
    dx_ref, dtaps_ref, dscale_ref, dhead_ref, mean_ref, dwi_out, dwo_out,
    x_grid, g_grid, turned, wide, taps, sums, move_sem
):
    rows, tokens = x_ref.shape
    tall = dwi_ref.shape[0] // MOVES
    puts = [
        pltpu.make_async_copy(
            src.at[pl.ds(k * tall, tall)], dst.at[pl.ds(k * tall, tall)], move_sem.at[i, k]
        )
        for k in range(MOVES)
        for i, (src, dst) in enumerate(((dwi_ref, dwi_out), (dwo_ref, dwo_out)))
    ]
    for put in puts:
        put.start()
    mean_ref[...] = jnp.sum(loss_ref[...], axis=1, keepdims=True) * (1.0 / tokens)
    strips = tokens // LANES
    wide[...] = jnp.zeros_like(wide)
    wide[0:rows, :] = x_ref[...].astype(jnp.float32)
    spread_taps(taps_ref, taps)
    clear_pads(x_grid)
    clear_pads(g_grid)
    for s in range(strips):
        put_strip(x_grid, s, wide[:, s * LANES : (s + 1) * LANES])
        put_strip(g_grid, s, grad_ref[:, s * LANES : (s + 1) * LANES])
    sums[...] = jnp.zeros_like(sums)
    half = KS // 2

    @pl.loop(0, WIN_H // ROWS_AT_ONCE)
    def _(block):
        first = block * ROWS_AT_ONCE
        for col in range(0, WIN_W, SUB):
            outs = conv_piece(g_grid, taps, first, col, flip=True)
            for r in range(ROWS_AT_ONCE):
                turned[first + r, col : col + SUB, :] = outs[r]
            grads = [
                g_grid[first + half + r, SUB + col : SUB + col + SUB, :]
                for r in range(ROWS_AT_ONCE)
            ]
            for j in range(KS):
                start = SUB + col + j - half
                seen = [
                    x_grid[first + r, start : start + SUB, :]
                    for r in range(ROWS_AT_ONCE + KS - 1)
                ]
                for i in range(KS):
                    total = sums[i * KS + j]
                    for r in range(ROWS_AT_ONCE):
                        total = total + grads[r] * seen[r + i]
                    sums[i * KS + j] = total

    for k in range(KS * KS):
        dtaps_ref[k : k + 1, :] = jnp.sum(sums[k], axis=0, keepdims=True)

    head = head_ref[...].astype(jnp.float32).T.astype(jnp.bfloat16)
    per = LANES // WIN_W
    for s in range(strips):
        own = slice(s * LANES, (s + 1) * LANES)
        back = jnp.concatenate([turned[s * per + r] for r in range(per)], axis=0).T
        out_grad = jnp.dot(head, lg_ref[:, own], preferred_element_type=jnp.float32)
        dx_ref[:, own] = (back + out_grad)[0:rows]
    direct = lax.dot_general(
        lg_ref[...], wide[...].astype(jnp.bfloat16), (((1,), (1,)), ((), ())),
        preferred_element_type=jnp.float32,
    )
    seen = seen_ref[...]
    classes = dhead_ref.shape[0]
    dhead_ref[...] = (direct + scale_ref[...] * seen)[0:classes]
    dscale_ref[...] = jnp.sum(head_ref[...].astype(jnp.float32) * seen, axis=0, keepdims=True)
    for put in puts:
        put.wait()


def tail(classes, x, grad, taps, lg, head, seen, scale, loss, d_w_in, d_w_out):
    rows, tokens = x.shape
    vmem = pl.BlockSpec(memory_space=pltpu.VMEM)
    hbm = pl.BlockSpec(memory_space=pltpu.HBM)
    return pl.pallas_call(
        tail_kernel,
        out_shape=(
            jax.ShapeDtypeStruct((rows, tokens), jnp.float32),
            jax.ShapeDtypeStruct((KS * KS, LANES), jnp.float32),
            jax.ShapeDtypeStruct((1, LANES), jnp.float32),
            jax.ShapeDtypeStruct((classes, LANES), jnp.float32),
            jax.ShapeDtypeStruct((1, 1), jnp.float32),
            jax.ShapeDtypeStruct(d_w_in.shape, jnp.float32),
            jax.ShapeDtypeStruct(d_w_out.shape, jnp.float32),
        ),
        in_specs=[vmem] * 10,
        out_specs=(vmem,) * 5 + (hbm,) * 2,
        scratch_shapes=[
            pltpu.VMEM((WIN_H + KS - 1, PAD_W, LANES), jnp.float32),
            pltpu.VMEM((WIN_H + KS - 1, PAD_W, LANES), jnp.float32),
            pltpu.VMEM((WIN_H, WIN_W, LANES), jnp.float32),
            pltpu.VMEM((LANES, tokens), jnp.float32),
            pltpu.VMEM((KS * KS, SUB, LANES), jnp.float32),
            pltpu.VMEM((KS * KS, SUB, LANES), jnp.float32),
            pltpu.SemaphoreType.DMA((2, MOVES)),
        ],
        compiler_params=pltpu.CompilerParams(vmem_limit_bytes=32 * 1024 * 1024),
    )(x, grad, taps, lg, head, seen, scale, loss, d_w_in, d_w_out)


PARTS = 2
SQRT_HALF = 0.7071067811865476
NORMAL = 0.3989422804014327


def lanes_of(j, size=LANES):
    return pl.ds(pl.multiple_of(j * size, size), size)


def rows_of(j, size):
    return pl.ds(pl.multiple_of(j * size, size), size)


def nt_dot(lhs, rhs):
    return lax.dot_general(lhs, rhs, (((1,), (1,)), ((), ())), preferred_element_type=jnp.float32)


def nn_dot(lhs, rhs):
    return jnp.dot(lhs, rhs, preferred_element_type=jnp.float32)


def three_parts(value):
    high = value.astype(jnp.bfloat16)
    rest = value - high.astype(jnp.float32)
    middle = rest.astype(jnp.bfloat16)
    low = (rest - middle.astype(jnp.float32)).astype(jnp.bfloat16)
    return high, middle, low


def stack_rows(parts, height, width):
    row = lax.broadcasted_iota(jnp.int32, (height, width), 0)
    out = jnp.zeros((height, width), jnp.float32)
    for i, part in enumerate(parts):
        out = jnp.where(row == i, part.astype(jnp.float32), out)
    return out.astype(jnp.bfloat16)


def block_kernel(
    n, class_count,
    x_hbm, taps_hbm, gain_hbm, scale_hbm, labels_hbm, head_hbm, w_in_hbm, w_out_hbm,
    land_ref, seen_ref, lg_ref, loss_ref, own_head_ref, own_scale_ref, dwi_ref, dwo_ref,
    x_ref, taps_ref, gain_ref, scale_ref, labels_ref, head_ref, w_in_ref, w_out_ref, load_sem,
    x_grid, wide, taps, turned,
    conv_all, wg, wg_turned, acc, gains, stats, token_rows,
    sh_high, sh_low, mix_both, mix,
    hidden, slope, narrow, back_rows, seen_narrow,
    tw_keep, tw_out, tw_in, rs_out, slots, packs,
    msg, t_in, y_out, y_in, u_in, d_in, z_out, sums,
    send_sem, recv_sem, tw_sem, rs_sem, lg_sem, f_sem,
    t_sem, y_sem, u_sem, d_sem, zs_sem, m_in, m_sem,
):
    a, m = n // 4, n // 2
    rows, tokens = x_ref.shape
    units, channels = w_in_ref.shape
    strips = tokens // LANES
    classes = lg_ref.shape[0]
    pack = classes // 2
    z, y, c = place(n)
    me = index_of(z, y, c)
    chip = z * 2 + y
    twin, across = index_of(z, y, 1 - c), index_of(z, 1 - y, c)
    f32 = jnp.float32

    loads = [
        pltpu.make_async_copy(src, dst, load_sem.at[i])
        for i, (src, dst) in enumerate(
            (
                (x_hbm, x_ref), (taps_hbm, taps_ref), (w_in_hbm, w_in_ref), (gain_hbm, gain_ref),
                (head_hbm, head_ref), (w_out_hbm, w_out_ref), (scale_hbm, scale_ref),
                (labels_hbm, labels_ref),
            )
        )
    ]
    for load in loads:
        load.start()
    barrier = pltpu.get_barrier_semaphore()
    pl.semaphore_signal(barrier, inc=1, device_id={"ch": twin})
    for d in range(1, m):
        pl.semaphore_signal(barrier, inc=1, device_id={"ch": lax.rem(chip + d, m) * 2 + c})

    span = tokens // PARTS
    half = KS // 2
    per = LANES // WIN_W
    if rows < LANES:
        wide[...] = jnp.zeros_like(wide)
    clear_pads(x_grid)
    loads[0].wait()
    loads[1].wait()
    wide[0:rows, :] = x_ref[...].astype(f32)
    spread_taps(taps_ref, taps)
    for s in range(strips):
        put_strip(x_grid, s, wide[:, s * LANES : (s + 1) * LANES])

    def convolve(h):
        blocks = WIN_H // ROWS_AT_ONCE // PARTS

        @pl.loop(h * blocks, (h + 1) * blocks)
        def _(block):
            first = block * ROWS_AT_ONCE
            for col in range(0, WIN_W, SUB):
                outs = conv_piece(x_grid, taps, first, col)
                for r in range(ROWS_AT_ONCE):
                    turned[first + r, col : col + SUB, :] = outs[r]

        for s in range(h * strips // PARTS, (h + 1) * strips // PARTS):
            back = jnp.concatenate([turned[s * per + r] for r in range(per)], axis=0).T
            conv_all[rows_of(me, rows), s * LANES : (s + 1) * LANES] = back[0:rows].astype(
                jnp.bfloat16
            )

    def copy(kind, b, device, h):
        piece = conv_all.at[rows_of(b, rows), pl.ds(h * span, span)]
        return pltpu.make_async_remote_copy(
            src_ref=piece,
            dst_ref=piece,
            send_sem=send_sem.at[kind, b * PARTS + h],
            recv_sem=recv_sem.at[b * PARTS + h],
            device_id={"ch": device},
        )

    balance = a == 4
    odd = lax.rem(z, 2) == 1
    mate = jnp.where(odd, z - 1, z + 1)
    end = (z == 0) | (z == a - 1)

    def to_mate(h):
        return copy(4, across, index_of(mate, y, c), h)

    def when_by_line(own_end, h, then):
        if 2 * h >= PARTS:
            then()
        else:
            pl.when(jnp.logical_not(own_end))(then)

    def send_across(b, below, s, h):
        def go():
            copy(2, b, across, h).start()

        if not balance or s > 1:
            go()
            return
        is_mate = odd if below else jnp.logical_not(odd)
        if 2 * h >= PARTS:
            pl.when(jnp.logical_not(is_mate))(go)
        else:
            pl.when(jnp.logical_not(is_mate) | end)(go)

    for h in range(PARTS):
        convolve(h)
        if h == 0:
            pl.semaphore_wait(barrier, m)

        @pl.when(z < a - 1)
        def _():
            copy(0, me, me + 4, h).start()

        @pl.when(z > 0)
        def _():
            copy(1, me, me - 4, h).start()

        copy(2, me, across, h).start()
        copy(3, me, twin, h).start()

    loads[2].wait()
    loads[3].wait()
    pair = 2 * rows
    gains[...] = jnp.zeros_like(gains)
    ones = jnp.ones((pair, LANES), jnp.bfloat16)

    def weigh(p):
        own = slice(p * pair, (p + 1) * pair)
        gained = w_in_ref[:, own].astype(f32) * gain_ref[:, own]
        gained_narrow = gained.astype(jnp.bfloat16)
        wg[p] = gained_narrow
        wg_turned[p] = gained.T.astype(jnp.bfloat16)
        gains[...] += nn_dot(gained_narrow, ones)

    soon = m // 2 if balance else m
    for p in range(soon):
        weigh(p)

    def weigh_rest():
        for p in range(soon, m):
            weigh(p)

    def scale_head():
        for load in loads[4:]:
            load.wait()
        scaled = head_ref[...].astype(f32) * scale_ref[...]
        high = scaled.astype(jnp.bfloat16)
        sh_high[...] = jnp.zeros_like(sh_high)
        sh_low[...] = jnp.zeros_like(sh_low)
        sh_high[0:class_count, :] = high
        sh_low[0:class_count, :] = (scaled - high.astype(f32)).astype(jnp.bfloat16)

    def mix_head():
        mixed = nt_dot(sh_high[...], w_out_ref[...]) + nt_dot(sh_low[...], w_out_ref[...])
        high = mixed.astype(jnp.bfloat16)
        mix_both[0:classes, :] = high
        mix_both[classes : 2 * classes, :] = (mixed - high.astype(f32)).astype(jnp.bfloat16)

    def mix_back():
        mix[...] = nt_dot(w_out_ref[...], sh_high[...]).astype(jnp.bfloat16)
        channel = lax.broadcasted_iota(jnp.int32, (channels, LANES), 0) - me * rows
        at = lax.broadcasted_iota(jnp.int32, (channels, LANES), 1)
        chosen = ((channel == at) & (at < rows)).astype(f32).astype(jnp.bfloat16)
        own_head_ref[...] = jnp.zeros_like(own_head_ref)
        own_head_ref[0:class_count, :] = nn_dot(head_ref[...], chosen).astype(jnp.bfloat16)
        scale_rows = stack_rows(three_parts(scale_ref[...]), 16, channels)
        own_scale_ref[...] = jnp.sum(nn_dot(scale_rows, chosen), axis=0, keepdims=True)

    def absorb(p, first=False):
        for h in range(PARTS):
            copy(3, p * 2 + 1 - c, twin, h).wait_recv()

        @pl.loop(0, tokens // (2 * LANES))
        def _(g):
            own = lanes_of(g, 2 * LANES)
            block = conv_all[rows_of(p, pair), own]
            product = nn_dot(wg[p], block)
            if first:
                acc[:, own] = product
            else:
                acc[:, own] += product
            block_wide = block.astype(f32)
            whole = jnp.sum(block_wide, axis=0, keepdims=True)
            off = block_wide - whole * (1.0 / pair)
            stats[p, 0:1, own] = whole
            stats[p, 1:2, own] = jnp.sum(off * off, axis=0, keepdims=True)

    def from_line(s, h):
        below, above = me - 4 * s, me + 4 * s

        @pl.when(z >= s)
        def _():
            copy(0, below, me, h).wait_recv()

            @pl.when(z < a - 1)
            def _():
                copy(0, below, me + 4, h).start()

            send_across(below, True, s, h)
            copy(3, below, twin, h).start()

        @pl.when(z + s < a)
        def _():
            copy(1, above, me, h).wait_recv()

            @pl.when(z > 0)
            def _():
                copy(1, above, me - 4, h).start()

            send_across(above, False, s, h)
            copy(3, above, twin, h).start()

    def from_across(s, h):
        def take(b):
            copy(2, b, across, h).wait_recv()
            copy(3, b, twin, h).start()

        if s == 0:
            take(across)
            if balance:
                pl.when(end)(lambda: to_mate(h).start())
            return

        if balance and s == 1 and 2 * h >= PARTS:
            @pl.when(jnp.logical_not(end))
            def _():
                take(across - 4)
                take(across + 4)

            return

        @pl.when(z >= s)
        def _():
            take(across - 4 * s)

        @pl.when(z + s < a)
        def _():
            take(across + 4 * s)

    def absorb_at(s, side):
        if s == 0:
            absorb(z * 2 + side, first=side is y)
            return

        @pl.when(z >= s)
        def _():
            absorb((z - s) * 2 + side)

        @pl.when(z + s < a)
        def _():
            absorb((z + s) * 2 + side)

    def absorb_beside(inner):
        @pl.when(jnp.logical_not(end) if inner else end)
        def _():
            absorb(mate * 2 + 1 - y)
            if inner:
                absorb((2 * z - mate) * 2 + 1 - y)

    work = {
        (1, 0): [weigh_rest],
        (1, 1): [scale_head],
        (2, 0): [mix_head, mix_back],
        (2, 1): [lambda: absorb_at(0, y), lambda: absorb_at(0, 1 - y)],
        (3, 0): [lambda: absorb_at(1, y)],
        (3, 1): [lambda: absorb_at(2, y), lambda: absorb_beside(True)],
    }
    for s in range(1, a):
        for h in range(PARTS):
            from_line(s, h)
            from_across(s - 1, h)
            if balance and s == a - 2 and 2 * h >= PARTS:
                pl.when(jnp.logical_not(end))(lambda: to_mate(h).start())
            for item in work.get((s, h), []) if balance else []:
                item()
    for h in range(PARTS):
        from_across(a - 1, h)
    if balance:

        @pl.when(end)
        def _():
            for h in range(PARTS // 2, PARTS):
                block_there = index_of(mate, 1 - y, c)
                copy(2, block_there, across, h).wait_recv()
                copy(3, block_there, twin, h).start()

        absorb_at(2, 1 - y)
        absorb_at(3, y)
        absorb_at(3, 1 - y)
        absorb_beside(False)
    else:
        scale_head()
        mix_head()
        mix_back()
        acc[...] = jnp.zeros_like(acc)

        @pl.loop(0, m)
        def _(p):
            absorb(p)

    total = stats[0, 0:1, :]
    for p in range(1, m):
        total = total + stats[p, 0:1, :]
    tok_mean = total * (1.0 / channels)
    square = jnp.zeros_like(total)
    for p in range(m):
        off = stats[p, 0:1, :] * (1.0 / pair) - tok_mean
        square = square + stats[p, 1:2, :] + (pair * off) * off
    inv_std = 1.0 / jnp.sqrt(square * (1.0 / channels) + norm_eps)
    token_rows[0:1, :] = tok_mean
    token_rows[1:2, :] = inv_std

    step = m // strips
    base = lax.div(chip, step) if step > 1 else chip
    lane = lax.broadcasted_iota(jnp.int32, (pack, LANES), 1)
    left = lane < LANES // 2
    chunk = min(units, 64)

    def to_twin_strip(d):
        return pltpu.make_async_remote_copy(
            src_ref=tw_out.at[d], dst_ref=tw_in.at[d],
            send_sem=tw_sem.at[0, d], recv_sem=tw_sem.at[1, d], device_id={"ch": twin},
        )

    def to_owner(d, owner, source):
        return pltpu.make_async_remote_copy(
            src_ref=rs_out.at[d], dst_ref=slots.at[source],
            send_sem=rs_sem.at[0, d], recv_sem=rs_sem.at[1, source],
            device_id={"ch": owner * 2 + c},
        )

    def strip_at(d):
        both = lax.rem(lax.div(base, 2) + d // 2 + 1, strips // 2)
        side = lax.rem(base, 2)
        return 2 * both + (side if d % 2 else 1 - side)

    def activate(e):
        j = lax.rem(lax.div(base, 2) + e + 1, strips // 2)
        own = lanes_of(j, 2 * LANES)
        mean_here, inv_here = token_rows[0:1, own], token_rows[1:2, own]

        @pl.loop(0, units // chunk)
        def _(g):
            piece = rows_of(g, chunk)
            offset = jnp.concatenate([gains[piece, :]] * 2, axis=1)
            pre = (acc[piece, own] - offset * mean_here) * inv_here
            cum_prob = 0.5 * (1.0 + lax.erf(pre * SQRT_HALF))
            density = jnp.exp(-0.5 * pre * pre) * NORMAL
            acc[piece, own] = pre
            hidden[piece, own] = (pre * cum_prob).astype(jnp.bfloat16)
            slope[piece, own] = (cum_prob + pre * density) * inv_here

        scores = nn_dot(mix_both[...], hidden[:, own])
        scores = scores[0:classes] + scores[classes : 2 * classes] + nn_dot(own_scores[...], x_strip(own))
        for side in range(2):
            here = slice(side * LANES, (side + 1) * LANES)
            upper, lower = scores[0:pack, here], scores[pack : 2 * pack, here]
            first = jnp.where(left, upper, pltpu.roll(lower, LANES // 2, 1))
            second = jnp.where(left, pltpu.roll(upper, LANES // 2, 1), lower)
            d = 2 * e + jnp.where(lax.rem(base, 2) == side, 1, 0)
            tw_keep[d] = jnp.where(c == 0, first, second)
            tw_out[d] = jnp.where(c == 0, second, first)
        for d in (2 * e, 2 * e + 1):
            to_twin_strip(d).start()

    def pass_on(d):
        owner = strip_at(d) * step
        to_twin_strip(d).wait_recv()
        rs_out[d] = tw_keep[d] + tw_in[d]
        if d < strips - 1:
            to_owner(d, owner, chip).start()
        elif step > 1:

            @pl.when(owner != chip)
            def _():
                to_owner(d, owner, chip).start()

    own_scores = own_head_ref

    def x_strip(own):
        return x_ref[:, own] if rows == LANES else wide[:, own].astype(jnp.bfloat16)

    for e in range(strips // 2):
        activate(e)
        if e > 0:
            pass_on(2 * e - 2)
            pass_on(2 * e - 1)
    pass_on(strips - 2)
    pass_on(strips - 1)

    def to_all(r):
        return pltpu.make_async_remote_copy(
            src_ref=packs.at[base, c], dst_ref=packs.at[base, c],
            send_sem=lg_sem.at[0, r], recv_sem=lg_sem.at[1, base],
            device_id={"ch": lax.rem(chip + r, m) * 2 + c},
        )

    def from_owner(j):
        return pltpu.make_async_remote_copy(
            src_ref=packs.at[j, c], dst_ref=packs.at[j, c],
            send_sem=lg_sem.at[0, 0], recv_sem=lg_sem.at[1, j],
            device_id={"ch": twin},
        )

    def forward(j, core):
        return pltpu.make_async_remote_copy(
            src_ref=packs.at[j, core], dst_ref=packs.at[j, core],
            send_sem=f_sem.at[0, j], recv_sem=f_sem.at[1, j],
            device_id={"ch": twin},
        )

    def own_strip():
        whole = rs_out[strips - 1]
        for r in range(1, m):
            source = lax.rem(chip + r, m)
            to_owner(0, 0, source).wait_recv()
            whole = whole + slots[source]
        row = lax.broadcasted_iota(jnp.int32, (pack, LANES), 0)
        kind = row + jnp.where(left, 0, pack)
        scores = jnp.where(kind < class_count, whole, -jnp.inf)
        label = jnp.broadcast_to(labels_ref[pl.ds(base, 1), :], (SUB, LANES))
        moved = pltpu.roll(label, LANES // 2, 1)
        label = jnp.where(left[0:SUB] == (c == 0), label, moved)[0:1]

        def both(value, join):
            value = jnp.broadcast_to(value, (SUB, LANES))
            return join(value, pltpu.roll(value, LANES // 2, 1))[0:1]

        row_max = both(jnp.max(scores, axis=0, keepdims=True), jnp.maximum)
        terms = jnp.exp(scores - row_max)
        exp_total = both(jnp.sum(terms, axis=0, keepdims=True), jnp.add)
        hit = kind == label
        picked = both(
            jnp.sum(jnp.where(hit, whole, 0.0), axis=0, keepdims=True), jnp.add
        )
        loss = jnp.log(exp_total) + row_max - picked
        grads = terms / exp_total - hit.astype(f32)
        packs[base, c, 0:pack] = grads.astype(jnp.bfloat16)
        packs[base, c, pack : pack + 16] = stack_rows(three_parts(loss), 16, LANES)
        for r in range(1, m):
            to_all(r).start()
        forward(base, c).start()

    if step > 1:
        pl.when(base * step == chip)(own_strip)
    else:
        own_strip()

    loss_ref[...] = jnp.zeros_like(loss_ref)

    def receive(d):
        j = strip_at(d)
        if d < strips - 1:
            from_owner(j).wait_recv()
            forward(j, c).start()
        elif step > 1:

            @pl.when(base * step != chip)
            def _():
                from_owner(j).wait_recv()
                forward(j, c).start()

    def go_back(d):
        j = strip_at(d)
        own = lanes_of(j)
        forward(j, 1 - c).wait_recv()
        first, second = packs[j, 0].astype(f32), packs[j, 1].astype(f32)
        loss = jnp.where(left[0:SUB], first[pack : pack + SUB], second[pack : pack + SUB])
        loss_ref[...] += jnp.sum(loss[0:3], axis=0, keepdims=True)
        first, second = first[0:pack], second[0:pack]
        upper = jnp.where(left, first, pltpu.roll(second, LANES // 2, 1))
        lower = jnp.where(left, pltpu.roll(first, LANES // 2, 1), second)
        grads = jnp.concatenate([upper, lower], axis=0).astype(jnp.bfloat16)
        lg_ref[:, own] = grads
        sum_gain, sum_both = jnp.zeros((1, LANES), f32), jnp.zeros((1, LANES), f32)
        for g in range(units // chunk):
            piece = slice(g * chunk, (g + 1) * chunk)
            value = nn_dot(mix[piece, :], grads) * slope[piece, own]
            narrow[piece, own] = value.astype(jnp.bfloat16)
            sum_gain = sum_gain + jnp.sum(gains[piece, :] * value, axis=0, keepdims=True)
            sum_both = sum_both + jnp.sum(acc[piece, own] * value, axis=0, keepdims=True)
        share = sum_both * (1.0 / channels) * token_rows[1:2, own]
        back_rows[0:1, own] = sum_gain * (1.0 / channels) - token_rows[0:1, own] * share
        back_rows[1:2, own] = share

    order_here = [strips - 1] + list(range(strips - 1))
    for i, d in enumerate(order_here):
        receive(d)
        if i > 0:
            go_back(order_here[i - 1])
    go_back(order_here[-1])

    body = strips * rows
    cuts = ((0, body // 2), (body // 2, body + classes))

    def dest(k):
        if k == a - 1:
            return z
        low = jnp.where(k < a - 1 - z, a - 1 - k, k - (a - 1 - z))
        high = jnp.where(k < z, k, a - 1 - (k - z))
        return jnp.where(2 * z < a, low, high)

    def cut(ref, h):
        return ref.at[pl.ds(cuts[h][0], cuts[h][1] - cuts[h][0])]

    def to_twin(zz, side, core, h):
        return pltpu.make_async_remote_copy(
            src_ref=cut(msg.at[index_of(zz, side, core)], h),
            dst_ref=cut(t_in.at[zz * 2 + side], h),
            send_sem=t_sem.at[0, zz * 2 + side, h],
            recv_sem=t_sem.at[1, zz * 2 + side, h],
            device_id={"ch": twin},
        )

    def to_across(k, zz, h):
        return pltpu.make_async_remote_copy(
            src_ref=cut(y_out.at[k], h),
            dst_ref=cut(y_in.at[zz], h),
            send_sem=y_sem.at[0, zz, h],
            recv_sem=y_sem.at[1, zz, h],
            device_id={"ch": across},
        )

    def along(k, zz, landing, sem, device, h):
        return pltpu.make_async_remote_copy(
            src_ref=cut(z_out.at[k], h),
            dst_ref=cut(landing.at[zz], h),
            send_sem=zs_sem.at[k, h],
            recv_sem=sem.at[zz, h],
            device_id={"ch": device},
        )

    def fill(zz, side, core, h):
        p = zz * 2 + side
        b = p * 2 + core
        count = strips // 2
        own = slice(h * count * LANES, (h + 1) * count * LANES)
        grad = nn_dot(wg_turned[p, rows_of(core, rows), :], narrow[:, own])
        term = grad - back_rows[0:1, own] - conv_all[rows_of(b, rows), own].astype(f32) * back_rows[1:2, own]
        term = term.astype(jnp.bfloat16)
        for s in range(count):
            first = (h * count + s) * rows
            msg[b, first : first + rows, :] = term[:, s * LANES : (s + 1) * LANES]

    def see():
        back = nt_dot(lg_ref[...], hidden[...]).astype(jnp.bfloat16)
        for p in range(m):
            block = nn_dot(back, w_out_ref[:, p * pair : (p + 1) * pair]).astype(jnp.bfloat16)
            for core in range(2):
                msg[p * 2 + core, body : body + classes, :] = fit(
                    block[:, core * rows : (core + 1) * rows], 1, LANES
                )

    def slabs(h):
        low, high = cuts[h]
        slab = max(k for k in range(16, 129, 16) if (high - low) % k == 0)
        return [low + i * slab for i in range((high - low) // slab)], slab

    def sums_to_mate(h):
        return pltpu.make_async_remote_copy(
            src_ref=cut(y_out.at[a - 2], h),
            dst_ref=cut(m_in, h),
            send_sem=m_sem.at[0, h],
            recv_sem=m_sem.at[1, h],
            device_id={"ch": index_of(mate, y, c)},
        )

    def cross(k, h):
        zz = dest(k)
        to_twin(zz, 1 - y, c, h).wait_recv()
        low, high = cuts[h]

        starts, slab = slabs(h)
        for start in starts:
            own = slice(start, start + slab)
            y_out[k, own] = (
                msg[index_of(zz, 1 - y, c), own].astype(f32)
                + t_in[zz * 2 + 1 - y, own].astype(f32)
            ).astype(jnp.bfloat16)

        if not balance:
            to_across(k, zz, h).start()
            return
        if k == a - 2:
            when_by_line(end, h, lambda: sums_to_mate(h).start())
            if h == 0:
                pl.when(end)(lambda: to_across(k, zz, h).start())
            return
        if k == a - 1:

            def join():
                sums_to_mate(h).wait_recv()

                starts, slab = slabs(h)
                for start in starts:
                    own = slice(start, start + slab)
                    y_out[k, own] = (y_out[k, own].astype(f32) + m_in[own].astype(f32)).astype(
                        jnp.bfloat16
                    )

            when_by_line(jnp.logical_not(end), h, join)
        to_across(k, zz, h).start()

    turns = [(k, h) for k in range(a) for h in range(2)]
    if balance:
        crossings = [(0, 0), (2, 1), (0, 1), (2, 0), (1, 0), (1, 1), (3, 0), (3, 1)]
        late = crossings[-2:]
    else:
        crossings, late = turns, []
    ready = []
    for i, (k, h) in enumerate(crossings):
        fill(dest(k), 1 - y, 1 - c, h)
        if i == 1:
            see()
        to_twin(dest(k), 1 - y, 1 - c, h).start()
        fill(dest(k), 1 - y, c, h)
        if ready:
            cross(*ready.pop())
        if (k, h) not in late:
            ready.append((k, h))
    for i, (k, h) in enumerate(turns):
        fill(dest(k), y, 1 - c, h)
        to_twin(dest(k), y, 1 - c, h).start()
        fill(dest(k), y, c, h)
        if ready:
            cross(*ready.pop())

    seen_narrow[...] = nt_dot(hidden[...], lg_ref[...]).astype(jnp.bfloat16)
    mean_rows = stack_rows(three_parts(token_rows[0:1, :]), 16, tokens)
    means = jnp.sum(nt_dot(narrow[...], mean_rows), axis=1, keepdims=True)

    swath = 2 * LANES

    def weights_piece(p):
        own = slice(p * swath, (p + 1) * swath)
        dwi_ref[:, own] = (nt_dot(narrow[...], conv_all[own, :]) - means) * gain_ref[:, own]
        dwo_ref[:, own] = nn_dot(seen_narrow[...], sh_high[:, own])

    pieces = list(range(channels // swath))
    share = -(-len(pieces) // (2 * a - 1))

    def sum_up(zz, h, with_across):
        low, high = cuts[h]

        starts, slab = slabs(h)
        for start in starts:
            own = slice(start, start + slab)
            total = msg[index_of(zz, y, c), own].astype(f32) + t_in[zz * 2 + y, own].astype(f32)
            sums[own] = total + y_in[zz, own].astype(f32) if with_across else total

    def add(landing, zz, h):
        low, high = cuts[h]

        starts, slab = slabs(h)
        for start in starts:
            own = slice(start, start + slab)
            sums[own] += landing[zz, own].astype(f32)

    for i, (k, h) in enumerate(turns):
        zz = dest(k)
        for p in pieces[i * share : (i + 1) * share]:
            weights_piece(p)
        to_twin(zz, y, c, h).wait_recv()
        with_across = not (balance and k == a - 2)
        if with_across:
            to_across(k, zz, h).wait_recv()
        sum_up(zz, h, with_across)
        if not with_across and h == 0:

            @pl.when(end)
            def _():
                to_across(k, zz, h).wait_recv()
                add(y_in, zz, h)

        if k < a - 1:

            @pl.when((zz > z) & (z > 0))
            def _():
                along(k, zz, u_in, u_sem, me, h).wait_recv()
                add(u_in, zz, h)

            @pl.when((zz < z) & (z < a - 1))
            def _():
                along(k, zz, d_in, d_sem, me, h).wait_recv()
                add(d_in, zz, h)

            low, high = cuts[h]
            z_out[k, low:high] = sums[low:high].astype(jnp.bfloat16)

            @pl.when(zz > z)
            def _():
                along(k, zz, u_in, u_sem, me + 4, h).start()

            @pl.when(zz < z)
            def _():
                along(k, zz, d_in, d_sem, me - 4, h).start()

        else:

            @pl.when(z > 0)
            def _():
                along(0, z, u_in, u_sem, me, h).wait_recv()
                add(u_in, z, h)

            @pl.when(z < a - 1)
            def _():
                along(0, z, d_in, d_sem, me, h).wait_recv()
                add(d_in, z, h)

            for s in range(h * strips // 2, (h + 1) * strips // 2):
                land_ref[:, s * LANES : (s + 1) * LANES] = sums[s * rows : (s + 1) * rows, :]
        if i == 1:
            for crossing in late:
                cross(*crossing)
    seen_ref[...] = sums[body : body + classes, :]

    for h in range(PARTS):
        for q in range(m):
            copy(3, q * 2 + c, twin, h).wait_send()
        if balance:
            when_by_line(jnp.logical_not(end), h, lambda: to_mate(h).wait_send())
        for zz in range(a):
            if balance:
                crossed = (zz != mate) if 2 * h >= PARTS else ((zz != mate) | end)

                @pl.when(crossed)
                def _():
                    copy(2, index_of(zz, y, c), across, h).wait_send()

            else:
                copy(2, index_of(zz, y, c), across, h).wait_send()

            @pl.when((z < a - 1) & (zz <= z))
            def _():
                copy(0, index_of(zz, y, c), me + 4, h).wait_send()

            @pl.when((z > 0) & (zz >= z))
            def _():
                copy(1, index_of(zz, y, c), me - 4, h).wait_send()

    for d in range(strips):
        to_twin_strip(d).wait_send()
        if d < strips - 1:
            to_owner(d, 0, 0).wait_send()
        elif step > 1:

            @pl.when(base * step != chip)
            def _():
                to_owner(d, 0, 0).wait_send()

        forward(d, c).wait_send()

    def all_left():
        for r in range(1, m):
            to_all(r).wait_send()

    if step > 1:
        pl.when(base * step == chip)(all_left)
    else:
        all_left()
    for k, h in turns:
        zz = dest(k)
        to_twin(zz, 1 - y, 1 - c, h).wait_send()
        to_twin(zz, y, 1 - c, h).wait_send()
        if balance and k == a - 2:
            when_by_line(end, h, lambda: sums_to_mate(h).wait_send())
            if h == 0:
                pl.when(end)(lambda: to_across(k, zz, h).wait_send())
        else:
            to_across(k, zz, h).wait_send()
        if k < a - 1:
            along(k, zz, u_in, u_sem, me, h).wait_send()


def block(n, class_count, x, taps, gain, scale, labels, head, w_in, w_out):
    a, m = n // 4, n // 2
    rows, tokens = x.shape
    units, channels = w_in.shape
    strips = tokens // LANES
    classes = -(-class_count // 32) * 32
    pack = classes // 2
    length = strips * rows + classes
    pair = 2 * rows
    bf16, f32 = jnp.bfloat16, jnp.float32
    vmem = pl.BlockSpec(memory_space=pltpu.VMEM)
    hbm = pl.BlockSpec(memory_space=pltpu.HBM)
    dma = pltpu.SemaphoreType.DMA
    scratch = [
        pltpu.VMEM(x.shape, x.dtype),
        pltpu.VMEM(taps.shape, taps.dtype),
        pltpu.VMEM(gain.shape, gain.dtype),
        pltpu.VMEM(scale.shape, scale.dtype),
        pltpu.VMEM(labels.shape, labels.dtype),
        pltpu.VMEM(head.shape, head.dtype),
        pltpu.VMEM(w_in.shape, w_in.dtype),
        pltpu.VMEM(w_out.shape, w_out.dtype),
        dma((8,)),
        pltpu.VMEM((WIN_H + KS - 1, PAD_W, LANES), f32),
        pltpu.VMEM((LANES, tokens), f32),
        pltpu.VMEM((KS * KS, SUB, LANES), f32),
        pltpu.VMEM((WIN_H, WIN_W, LANES), f32),
        pltpu.VMEM((n * rows, tokens), bf16),
        pltpu.VMEM((m, units, pair), bf16),
        pltpu.VMEM((m, pair, units), bf16),
        pltpu.VMEM((units, tokens), f32),
        pltpu.VMEM((units, LANES), f32),
        pltpu.VMEM((m, SUB, tokens), f32),
        pltpu.VMEM((SUB, tokens), f32),
        pltpu.VMEM((classes, channels), bf16),
        pltpu.VMEM((classes, channels), bf16),
        pltpu.VMEM((2 * classes, units), bf16),
        pltpu.VMEM((units, classes), bf16),
        pltpu.VMEM((units, tokens), bf16),
        pltpu.VMEM((units, tokens), f32),
        pltpu.VMEM((units, tokens), bf16),
        pltpu.VMEM((SUB, tokens), f32),
        pltpu.VMEM((units, classes), bf16),
        pltpu.VMEM((strips, pack, LANES), f32),
        pltpu.VMEM((strips, pack, LANES), f32),
        pltpu.VMEM((strips, pack, LANES), f32),
        pltpu.VMEM((strips, pack, LANES), f32),
        pltpu.VMEM((m, pack, LANES), f32),
        pltpu.VMEM((strips, 2, pack + 16, LANES), bf16),
        pltpu.VMEM((n, length, LANES), bf16),
        pltpu.VMEM((m, length, LANES), bf16),
        pltpu.VMEM((a, length, LANES), bf16),
        pltpu.VMEM((a, length, LANES), bf16),
        pltpu.VMEM((a, length, LANES), bf16),
        pltpu.VMEM((a, length, LANES), bf16),
        pltpu.VMEM((a, length, LANES), bf16),
        pltpu.VMEM((length, LANES), f32),
        dma((5, n * PARTS)),
        dma((n * PARTS,)),
        dma((2, strips)),
        dma((2, m)),
        dma((2, m)),
        dma((2, strips)),
        dma((2, m, 2)),
        dma((2, a, 2)),
        dma((a, 2)),
        dma((a, 2)),
        dma((a, 2)),
        pltpu.VMEM((length, LANES), bf16),
        dma((2, 2)),
    ]
    return pl.pallas_call(
        functools.partial(block_kernel, n, class_count),
        out_shape=(
            pltpu.VMEM((rows, tokens), f32),
            pltpu.VMEM((classes, LANES), f32),
            pltpu.VMEM((classes, tokens), bf16),
            pltpu.VMEM((1, LANES), f32),
            pltpu.VMEM((classes, LANES), bf16),
            pltpu.VMEM((1, LANES), f32),
            pltpu.VMEM((units, channels), f32),
            pltpu.VMEM((units, channels), f32),
        ),
        in_specs=[hbm] * 8,
        out_specs=(vmem,) * 8,
        scratch_shapes=scratch,
        compiler_params=pltpu.CompilerParams(
            collective_id=0, has_side_effects=True,
            vmem_limit_bytes=BLOCK_LIMIT,
        ),
    )(x, taps, gain, scale, labels, head, w_in, w_out)


def per_device(n, features, dw_weight, norm_gain, layer_scale, w_in, w_out, w_head, labels):
    my_rows, tok_count = features.shape
    class_count = w_head.shape[1]
    head = w_head.T
    taps = fit(dw_weight.T, 1, LANES)
    conv_grad, seen, lg, loss, own_head, my_scale, d_w_in, d_w_out = block(
        n, class_count, features, taps, norm_gain[None, :], layer_scale[None, :],
        labels.reshape(-1, LANES), head, w_in, w_out,
    )
    d_features, d_dw, d_scale, d_head, mean_loss, d_w_in, d_w_out = tail(
        class_count, features, fit(conv_grad, 0, LANES), taps, lg, own_head, seen, my_scale, loss, d_w_in, d_w_out
    )
    return (
        d_features, d_dw.T[:my_rows], d_scale[0, :my_rows], d_w_in, d_w_out, d_head.T[:my_rows],
        mean_loss[0],
    )


def solution(mesh):
    placed = (P("ch", "grp"), P("ch", None), P(), P(), P("ch", None), P("ch", None), P(), P("grp"))
    return jax.shard_map(
        functools.partial(per_device, mesh.shape["ch"]),
        mesh=mesh,
        in_specs=placed,
        out_specs=(
            P("ch", "grp"),
            P("ch", "grp"),
            P(("grp", "ch")),
            P(("grp", "ch"), None),
            P(("grp", "ch"), None),
            P("ch", "grp"),
            P("grp"),
        ),
        check_vma=False,
    )
```
